32 devices in a mesh: tile: 8 (over z, x), wp: 4 (over y, core).
Axes of the slice: x: 2, y: 2, z: 4, core: 2. Of those that a mesh axis runs over, the one named last changes fastest.
Arguments:
- visibilities: float32 [8192, 2, 128], P(('tile', 'wp')), may hold values from -6 to 6
- vis_weight: float32 [8192, 128], P(('tile', 'wp')), may hold values from 0.2 to 5
- cell_index: int32 [8192, 128], P(('tile', 'wp')), may hold values from 0 to 4095
- tap_offsets: int32 [8192, 128], P(('tile', 'wp')), may hold values from 0 to 255
- routes: int32 [8192, 1], P(('tile', 'wp')), may hold values from 0 to 31; in each aligned block of 256 rows (0 to 255, 256 to 511, ...) at most 16 rows name the same one
- patch_index: int32 [8192], P(('tile', 'wp')), may hold values from 0 to 255
- kernel: float32 [16, 8], replicated, may hold values from 0.1 to 1
Outputs:
- uv_grid: float32 [4, 8, 2, 1024, 1024], P('wp', 'tile')
The draws below stay inside these ranges and needn't reach their ends.
Inputs may be any that keep to these rules, and one draw needn't show every extreme that they name: `routes`: the 256 blocks of one device name no value more than 16 times, a bound that some block reaches.
All inputs are finite; a program needn't handle non-finite values.
Results may differ from the reference program's by a relative error of at most 0.0003.
Values sent between devices are 32-bit elements; how exact they have to be, the bound alone decides.
No kernel may reach another device: no remote copies, remote signals or barrier semaphores. Data moves between devices by JAX's collectives and lax.ppermute only.
A program may use at most 192 MiB of HBM per device.

```python
import math
import jax
import jax.numpy as jnp
import numpy as np
from jax import lax

GRID = 8192
TCOLS = 8
SUB = 64
KW = 8
OVER = 16
ROWS = 128
BLK_DEV = 256
TILE = 1024
TILES = 8
NU = 1024
NW = 4
BLOCKS = 8192
CAP = 16
SIDE = 16


def touch_ends(values, key, least, top_value):
    spot = [jax.random.randint(jax.random.fold_in(key, axis), (), 0, length) for axis, length in enumerate(values.shape)]
    widest = values.shape.index(max(values.shape))
    beside = spot[:widest] + [(spot[widest] + 1) % values.shape[widest]] + spot[widest + 1:]
    return values.at[tuple(spot)].set(least).at[tuple(beside)].set(top_value)


def shard_levels(key, shape, shards, smallest, top_value):
    factor_of = 1.0
    for dim, shards_of in shards:
        steps = jax.random.uniform(jax.random.fold_in(jax.random.fold_in(key, 6), dim), (shards_of,), jnp.float32, smallest / len(shards), top_value / len(shards))
        factor_of = factor_of * jnp.repeat(jnp.exp(steps), shape[dim] // shards_of).reshape((-1,) + (1,) * (len(shape) - 1 - dim))
    return factor_of


def shared_out(stream_key, own, number, rows, number_of, top, reach, lean):
    sequence = jax.random.permutation(stream_key, number_of)
    crowded, ordinary = portions_of(number_of, rows * top, reach, lean, True), portions_of(number_of, rows * top, reach, lean, False)
    places = jnp.arange(number_of)

    def named(tallies, turn):
        used = int((tallies > 0).sum())
        fixed = max(1, used // 4)
        shifted = fixed + (places - fixed + turn * (used - fixed)) % max(1, number_of - fixed)
        return jnp.zeros((number_of,), jnp.int32).at[sequence[jnp.where(places < fixed, places, shifted)]].set(jnp.asarray(tallies, jnp.int32))

    tallies = jnp.where(number % 4 == 0, named(crowded, number // 4), named(ordinary, number - number // 4 - 1))
    mixed = jax.random.permutation(jax.random.fold_in(own, 3), number_of)
    giver, receiver = mixed[0:number_of // 2 * 2:2], mixed[1:number_of // 2 * 2:2]
    room = jnp.minimum(tallies[giver] - 1, reach - tallies[receiver]) // 2
    room = jnp.where((giver == sequence[0]) | (receiver == sequence[0]) | (tallies[receiver] == 0), 0, jnp.maximum(room, 0))
    shifted = jax.random.randint(jax.random.fold_in(own, 4), (number_of // 2,), 0, 1 << 20) % (room + 1)
    tallies = tallies.at[giver].add(-shifted).at[receiver].add(shifted)
    members = jnp.searchsorted(jnp.cumsum(tallies), jnp.arange(rows * top), side="right").astype(jnp.int32)
    table = members.reshape(top, rows).T
    table = table[jax.random.permutation(jax.random.fold_in(own, 1), rows)]
    turn = jax.random.randint(jax.random.fold_in(own, 2), (rows, 1), 0, top)
    return jnp.take_along_axis(table, (jnp.arange(top)[None, :] + turn) % top, axis=1)


def portions_of(number_of, total, most, slope, full):
    weights = [(1 << 20) // math.isqrt(standing ** slope) + 1 for standing in range(1, number_of + 1)]
    largest = most if full else min(most, max(-(-total // number_of), total * weights[0] // sum(weights)))
    least = 1 if total - largest >= number_of - 1 else 0
    counts, surplus = [largest] + [least] * (number_of - 1), total - largest - least * (number_of - 1)
    while surplus > 0:
        free = [i for i in range(1, number_of) if counts[i] < largest] or [i for i in range(1, number_of) if counts[i] < most]
        whole, left = sum([weights[i] for i in free]), surplus
        for i in free:
            extra = min(most - counts[i], max(1, left * weights[i] // whole), surplus)
            counts[i] = counts[i] + extra
            surplus = surplus - extra
    return np.array(counts)


def gaussian(rng, extent, scale, bound, split=(), held_as=jnp.bfloat16):
    entries = scale * jax.random.normal(rng, extent, jnp.float32)
    if split:
        entries = entries * shard_levels(rng, extent, split, -0.22, 0.18)
    return jnp.clip(entries, -bound, bound).astype(held_as)


def setup_inputs(seed: int = 0) -> dict:
    streams_of = jax.random.split(jax.random.key(seed), 8)
    visibilities = gaussian(streams_of[0], (BLOCKS, 2, ROWS), 1.0, 6.0, ((0, 32),), jnp.float32)
    vis_weight = jnp.clip(jnp.exp(math.log(5.0) - 3.218876 * jax.random.uniform(streams_of[1], (BLOCKS, ROWS), jnp.float32) ** shard_levels(streams_of[1], (BLOCKS, ROWS), ((0, 32),), -0.2, 0.2)), 0.2, 5.0)
    cell_index = touch_ends(jax.random.randint(streams_of[2], (BLOCKS, ROWS), 0, SUB * SUB), jax.random.fold_in(streams_of[2], 1), 0, (SUB * SUB) - 1).astype(jnp.int32)
    tap_offsets = touch_ends(jax.random.randint(streams_of[3], (BLOCKS, ROWS), 0, OVER * OVER), jax.random.fold_in(streams_of[3], 1), 0, (OVER * OVER) - 1).astype(jnp.int32)
    routes_keys = jax.random.split(jax.random.fold_in(streams_of[4], 1), BLOCKS // BLK_DEV)
    routes_turns = jax.random.permutation(jax.random.fold_in(streams_of[4], 3), BLOCKS // BLK_DEV)
    routes = jax.vmap(lambda own, number: shared_out(jax.random.fold_in(streams_of[4], 2), own, number, BLK_DEV, NW * TILES, 1, CAP, 2))(routes_keys, routes_turns).reshape((BLOCKS, 1))
    patch_index = touch_ends(jax.random.randint(streams_of[5], (BLOCKS,), 0, SIDE * SIDE), jax.random.fold_in(streams_of[5], 1), 0, (SIDE * SIDE) - 1).astype(jnp.int32)
    kernel = jnp.clip(jnp.exp(jax.random.uniform(streams_of[6], (OVER, KW), jnp.float32, math.log(0.1), math.log(1.0))), 0.1, 1.0)
    return dict(visibilities=visibilities, vis_weight=vis_weight, cell_index=cell_index, tap_offsets=tap_offsets, routes=routes, patch_index=patch_index, kernel=kernel)


def reference(visibilities, vis_weight, cell_index, tap_offsets, routes, patch_index, kernel):
    rows_u = NU + KW
    cols_v = GRID + KW
    target = routes[:, 0]
    w_plane = target % NW
    owner_tile = target // NW
    base_row = (owner_tile // TCOLS) * TILE + (patch_index // SIDE) * SUB
    base_col = (owner_tile % TCOLS) * TILE + (patch_index % SIDE) * SUB
    groups = BLOCKS // BLK_DEV
    tap_steps = jnp.arange(KW, dtype=jnp.int32)
    components = jnp.arange(2, dtype=jnp.int32)

    def regroup(values):
        return values.reshape((groups, BLK_DEV) + values.shape[1:])

    def add_group(flat_grid, group):
        group_vis, group_weight, group_cell, group_offset, group_row, group_col, group_plane = group
        kern_u = kernel[group_offset // OVER]
        kern_v = kernel[group_offset % OVER]
        scaled = group_vis * group_weight[:, None, :]
        contribution = scaled[:, :, :, None, None] * kern_u[:, None, :, :, None] * kern_v[:, None, :, None, :]
        pos_u = group_row[:, None] + group_cell // SUB
        pos_v = group_col[:, None] + group_cell % SUB
        flat_index = (group_plane[:, None, None, None, None] * 2 + components[None, :, None, None, None]) * rows_u
        flat_index = (flat_index + pos_u[:, None, :, None, None] + tap_steps[None, None, None, :, None]) * cols_v
        flat_index = flat_index + pos_v[:, None, :, None, None] + tap_steps[None, None, None, None, :]
        return flat_grid.at[flat_index.reshape(-1)].add(contribution.reshape(-1)), None

    flat_grid = jnp.zeros((NW * 2 * rows_u * cols_v,), jnp.float32)
    inputs = (regroup(visibilities), regroup(vis_weight), regroup(cell_index), regroup(tap_offsets),
              regroup(base_row), regroup(base_col), regroup(w_plane))
    flat_grid, _ = lax.scan(add_group, flat_grid, inputs)
    uv_grid = flat_grid.reshape(NW, 2, rows_u, cols_v)[:, :, :NU, :GRID]
    uv_grid = uv_grid.reshape(NW, 2, NU // TILE, TILE, TCOLS, TILE)
    uv_grid = jnp.transpose(uv_grid, (0, 2, 4, 1, 3, 5))
    return uv_grid.reshape(NW, TILES, 2, TILE, TILE)
```

```python
import functools

import jax
import jax.numpy as jnp
from jax import lax
from jax.experimental import pallas as pl
from jax.experimental.pallas import tpu as pltpu
from jax.sharding import PartitionSpec as P

TCOLS = 8
SUB = 64
KW = 8
OVER = 16
TILE = 1024
ROWS = 128
SIDE = TILE // SUB
PATCHES = SIDE * SIDE
ROW_BLOCK = 2 * (SUB + KW)
FIRST = SIDE
DUMMY = FIRST + PATCHES
UNROLL = 4

f32 = jnp.float32
bf16 = jnp.bfloat16


def lanes(shape):
    return lax.broadcasted_iota(jnp.int32, shape, len(shape) - 1)


def pack_kernel(peers, cap, routes, patch, vis, weight, cell, tap, out, count):
    blocks = vis.shape[0]
    lane = lanes((1, ROWS))

    def clear(d, carry):
        count[d] = 0
        out[d, 3 * cap] = jnp.zeros((1, ROWS), f32)
        return carry

    lax.fori_loop(0, peers, clear, 0)

    def place(b, carry):
        d = routes[b]
        k = count[d]
        count[d] = k + 1
        w = weight[pl.ds(b, 1), :]
        both = vis[b] * w
        c = cell[pl.ds(b, 1), :]
        t = tap[pl.ds(b, 1), :]
        at_u = ((t >> 4) << 3) | ((c >> 6) & 7)
        at_v = ((t & 15) << 3) | (c & 7)
        code = ((c >> 9) << 17) | (((c >> 3) & 7) << 14) | (at_u << 7) | at_v
        out[d, 3 * k] = both[0:1, :]
        out[d, 3 * k + 1] = both[1:2, :]
        out[d, 3 * k + 2] = code.astype(f32)
        row = out[d, 3 * cap]
        row = jnp.where(lane == k, patch[b].astype(f32), row)
        row = jnp.where(lane == cap, (k + 1).astype(f32), row)
        out[d, 3 * cap] = row
        return carry

    lax.fori_loop(0, blocks, place, 0, unroll=4)


def split(x):
    hi = x.astype(bf16)
    return hi, (x - hi.astype(f32)).astype(bf16)


def twice(x):
    return jnp.concatenate([x, x], axis=0)


def spread(groups, values):
    zero = jnp.zeros((16, ROWS), bf16)
    picks = [groups == 2.0 * g for g in range(SUB // 16)]
    return [[jnp.where(pick, value, zero) for pick in picks] for value in values]


def patch_product(re, im, code, table):
    sub = lax.broadcasted_iota(jnp.int32, (8, ROWS), 0)
    at_v = code & 127
    at_u = (code >> 7) & 127
    first_v = (code >> 14) & 7
    first_u = (code >> 17) & 7
    ku = jnp.take_along_axis(table, at_u, axis=1)
    kv = jnp.take_along_axis(table, at_v, axis=1)
    group_u = (first_u + jnp.where(sub < (at_u & 7), 1, 0)).astype(f32)
    group_v = (first_v + jnp.where(sub < (at_v & 7), 1, 0)).astype(f32)
    step_u = jnp.concatenate([group_u, group_u - 1.0], axis=0).astype(bf16)
    step_v = jnp.concatenate([group_v, group_v - 1.0], axis=0).astype(bf16)
    u_re, u_im = re * ku, im * ku
    zero = jnp.zeros((16, ROWS), bf16)

    re_hi, re_lo = split(twice(u_re))
    im_hi, im_lo = split(twice(u_im))
    last_hi, last_lo = split(jnp.concatenate([u_re, u_im], axis=0))
    re_hi, re_lo, im_hi, im_lo = spread(step_u, [re_hi, re_lo, im_hi, im_lo])
    past = twice(group_u).astype(bf16) == 8.0
    last_hi = jnp.where(past, last_hi, zero)
    last_lo = jnp.where(past, last_lo, zero)
    left_hi = jnp.concatenate(re_hi + im_hi + [last_hi], axis=0)
    left_lo = jnp.concatenate(re_lo + im_lo + [last_lo], axis=0)
    left = jnp.concatenate([left_hi, left_lo], axis=1)

    v_hi, v_lo = split(twice(kv))
    end = step_v == 8.0
    (hi_rows, lo_rows) = spread(step_v, [v_hi, v_lo])
    hi_rows.append(jnp.where(end, v_hi, zero))
    lo_rows.append(jnp.where(end, v_lo, zero))
    fill = [zero] * (8 - len(hi_rows))
    right = jnp.concatenate(hi_rows + fill + lo_rows + fill, axis=0)
    right = jnp.concatenate([right, right], axis=1)
    product = lax.dot_general(left, right, (((1,), (1,)), ((), ())), preferred_element_type=f32)
    return product[:, :ROWS] + product[:, ROWS:]


def tap_table(kernel):
    sub = lax.broadcasted_iota(jnp.int32, (8, ROWS), 0)
    lane = lanes((8, ROWS))
    which_tap = (sub - lane) & 7
    which_level = lane >> 3
    table = jnp.zeros((8, ROWS), f32)
    for a in range(KW):
        row = jnp.zeros((8, ROWS), f32)
        for o in range(OVER):
            row = jnp.where(which_level == o, kernel[o, a], row)
        table = jnp.where(which_tap == a, row, table)
    return table


def grid_kernel(peers, cap, with_low, kernel, arrived, out, right, *rest):
    low, rest = (rest[0], rest[1:]) if with_low else (None, rest)
    acc, stage, meta, slots, meta_sem, out_sems = rest
    meta_copy = pltpu.make_async_copy(arrived.at[:, 3 * cap, 0, :], meta, meta_sem)
    meta_copy.start()

    def clear(i, carry):
        acc[i] = jnp.zeros((ROW_BLOCK, ROWS), f32)
        return carry

    lax.fori_loop(0, DUMMY, clear, 0)
    table = tap_table(kernel)
    meta_copy.wait()

    def gather_source(s, total):
        for k in range(cap):
            slots[total + k] = (s * cap + k) * 512 + (meta[s, k].astype(jnp.int32) + FIRST)
        return total + meta[s, cap].astype(jnp.int32)

    total = lax.fori_loop(0, peers, gather_source, 0)
    for k in range(UNROLL):
        slots[total + k] = DUMMY

    def work(step, carry):
        for i in range(UNROLL):
            entry = slots[step * UNROLL + i]
            slot = entry >> 9
            where_to = entry & 511
            source = slot // cap
            k = slot - source * cap
            re = jnp.broadcast_to(arrived[source, 3 * k], (8, ROWS))
            im = jnp.broadcast_to(arrived[source, 3 * k + 1], (8, ROWS))
            code = jnp.broadcast_to(arrived[source, 3 * k + 2], (8, ROWS)).astype(jnp.int32)
            acc[where_to] += patch_product(re, im, code, table)
        return carry

    lax.fori_loop(0, (total + UNROLL - 1) // UNROLL, work, 0)

    lane = lanes((8, ROWS))

    def rows_of(c, h, band, col):
        part = acc[FIRST + band * SIDE + col, pl.ds(c * SUB + 8 * h, 8), :]
        if h == 0:
            part = part + acc[band * SIDE + col, pl.ds(2 * SUB + 8 * c, 8), :]
        return part

    def copy_out(band):
        rows = pl.ds(band * SUB, SUB)
        return pltpu.make_async_copy(stage.at[:, rows, :], out.at[:, rows, :], out_sems.at[band])

    def fold(pair, carry):
        for c in range(2):
            edge = jnp.zeros((8, ROWS), f32)
            for half in range(2):
                band = pair * 2 + half
                for h in range(8):
                    before = jnp.zeros((8, ROWS), f32)
                    for t in range(TILE // ROWS):
                        even = rows_of(c, h, band, 2 * t)
                        odd = rows_of(c, h, band, 2 * t + 1)
                        turned = pltpu.roll(odd, SUB, 1)
                        stage[c, pl.ds(band * SUB + 8 * h, 8), pl.ds(t * ROWS, ROWS)] = even + jnp.where(
                            lane < SUB, before, turned
                        )
                        before = turned
                    k = half * 8 + h
                    moved = pltpu.roll(before, 8 * k, 1) if k else before
                    edge = jnp.where((lane >> 3) == k, moved, edge)
            right[c, pair] = edge
        for half in range(2):
            copy_out(pair * 2 + half).start()
        return carry

    lax.fori_loop(0, SIDE // 2, fold, 0)
    if with_low:
        for c in range(2):
            before = jnp.zeros((8, ROWS), f32)
            for t in range(TILE // ROWS):
                rows = pl.ds(2 * SUB + 8 * c, 8)
                even = acc[FIRST + (SIDE - 1) * SIDE + 2 * t, rows, :]
                turned = pltpu.roll(acc[FIRST + (SIDE - 1) * SIDE + 2 * t + 1, rows, :], SUB, 1)
                low[c, :, pl.ds(t * ROWS, ROWS)] = even + jnp.where(lane < SUB, before, turned)
                before = turned
            low[c, :, pl.ds(TILE, ROWS)] = jnp.where(lane < KW, before, 0.0)

    def finish(band, carry):
        copy_out(band).wait()
        return carry

    lax.fori_loop(0, SIDE, finish, 0)


def edge_kernel(edge, grid_in, grid_out, columns, in_sems, out_sems):
    lane = lanes((8, ROWS))
    pairs = SIDE // 2

    def fetch(pair):
        rows = pl.ds(pair * 2 * SUB, 2 * SUB)
        return pltpu.make_async_copy(
            grid_in.at[:, rows, pl.ds(0, ROWS)], columns.at[:, rows, :], in_sems.at[pair]
        )

    def put(pair):
        rows = pl.ds(pair * 2 * SUB, 2 * SUB)
        return pltpu.make_async_copy(
            columns.at[:, rows, :], grid_out.at[:, rows, pl.ds(0, ROWS)], out_sems.at[pair]
        )

    for pair in range(pairs):
        fetch(pair).start()

    def add(pair, carry):
        fetch(pair).wait()
        for c in range(2):
            packed = edge[c, pair]
            for k in range(16):
                moved = pltpu.roll(packed, ROWS - 8 * k, 1) if k else packed
                rows = pl.ds(pair * 2 * SUB + 8 * k, 8)
                columns[c, rows, :] += jnp.where(lane < KW, moved, 0.0)
        put(pair).start()
        return carry

    lax.fori_loop(0, pairs, add, 0)
    for pair in range(pairs):
        put(pair).wait()


def shifted(block, axis, distance):
    devices = range(lax.axis_size(axis))
    route = [(i - distance, i) for i in devices if i - distance in devices]
    return lax.ppermute(block, axis, route)


def shards(visibilities, vis_weight, cell_index, tap_offsets, routes, patch_index, kernel):
    blocks = visibilities.shape[0]
    tile_count = lax.axis_size("tile")
    plane_count = lax.axis_size("wp")
    peers = tile_count * plane_count
    cap = max(2, 2 * blocks // peers)
    rows = 3 * cap + 1
    vmem = pl.BlockSpec(memory_space=pltpu.VMEM)
    smem = pl.BlockSpec(memory_space=pltpu.SMEM)
    hbm = pl.BlockSpec(memory_space=pl.ANY)

    buckets = pl.pallas_call(
        functools.partial(pack_kernel, peers, cap),
        out_shape=jax.ShapeDtypeStruct((peers, rows, 1, ROWS), f32),
        in_specs=[smem, smem, vmem, vmem, vmem, vmem],
        out_specs=vmem,
        scratch_shapes=[pltpu.SMEM((peers,), jnp.int32)],
        compiler_params=pltpu.CompilerParams(vmem_limit_bytes=16 << 20),
        name="pack",
    )(routes[:, 0], patch_index, visibilities, vis_weight, cell_index, tap_offsets)

    arrived = lax.all_to_all(buckets, ("tile", "wp"), split_axis=0, concat_axis=0, tiled=True)

    with_low = tile_count > TCOLS
    out_shape = [
        jax.ShapeDtypeStruct((2, TILE, TILE), f32),
        jax.ShapeDtypeStruct((2, SIDE // 2, 8, ROWS), f32),
    ]
    out_specs = [hbm, vmem]
    if with_low:
        out_shape.append(jax.ShapeDtypeStruct((2, KW, TILE + ROWS), f32))
        out_specs.append(vmem)
    results = pl.pallas_call(
        functools.partial(grid_kernel, peers, cap, with_low),
        out_shape=out_shape,
        in_specs=[smem, vmem],
        out_specs=out_specs,
        scratch_shapes=[
            pltpu.VMEM((DUMMY + 1, ROW_BLOCK, ROWS), f32),
            pltpu.VMEM((2, TILE, TILE), f32),
            pltpu.SMEM((peers, ROWS), f32),
            pltpu.SMEM((peers * cap + max(cap, UNROLL),), jnp.int32),
            pltpu.SemaphoreType.DMA,
            pltpu.SemaphoreType.DMA((SIDE,)),
        ],
        compiler_params=pltpu.CompilerParams(vmem_limit_bytes=48 << 20),
        name="grid",
    )(kernel, arrived)
    own, right = results[0], results[1]

    place = lax.axis_index("tile")
    from_left = shifted(right, "tile", 1)
    if with_low:
        from_left = jnp.where(place % TCOLS == 0, 0.0, from_left)
    own = pl.pallas_call(
        edge_kernel,
        out_shape=jax.ShapeDtypeStruct((2, TILE, TILE), f32),
        in_specs=[vmem, hbm],
        out_specs=hbm,
        scratch_shapes=[
            pltpu.VMEM((2, TILE, ROWS), f32),
            pltpu.SemaphoreType.DMA((SIDE // 2,)),
            pltpu.SemaphoreType.DMA((SIDE // 2,)),
        ],
        input_output_aliases={1: 0},
        compiler_params=pltpu.CompilerParams(vmem_limit_bytes=16 << 20),
        name="edges",
    )(from_left, own)
    if with_low:
        low = results[2]
        from_above = shifted(low, "tile", TCOLS)
        from_corner = shifted(low[:, :, TILE:], "tile", TCOLS + 1)
        from_corner = jnp.where(place % TCOLS == 0, 0.0, from_corner)
        own = own.at[:, :KW, :].add(from_above[:, :, :TILE])
        own = own.at[:, :KW, :ROWS].add(from_corner)
    return own.reshape(1, 1, 2, TILE, TILE)


def solution(mesh):
    in_specs = (
        P(("tile", "wp"), None, None),
        P(("tile", "wp"), None),
        P(("tile", "wp"), None),
        P(("tile", "wp"), None),
        P(("tile", "wp"), None),
        P(("tile", "wp")),
        P(),
    )
    out_specs = P("wp", "tile", None, None, None)
    return jax.shard_map(shards, mesh=mesh, in_specs=in_specs, out_specs=out_specs, check_vma=False)
```

```python
import functools

import jax
import jax.numpy as jnp
from jax import lax
from jax.experimental import pallas as pl
from jax.experimental.pallas import tpu as pltpu
from jax.sharding import PartitionSpec as P

TCOLS = 8
SUB = 64
KW = 8
OVER = 16
TILE = 1024
ROWS = 128
SIDE = TILE // SUB
PATCHES = SIDE * SIDE
ROW_BLOCK = 2 * (SUB + KW)
FIRST = SIDE
DUMMY = FIRST + PATCHES
UNROLL = 8

f32 = jnp.float32
bf16 = jnp.bfloat16


def lanes(shape):
    return lax.broadcasted_iota(jnp.int32, shape, len(shape) - 1)


def pack_kernel(peers, cap, routes, patch, vis, weight, cell, tap, out, *scratch):
    routes_s, patch_s, vis_v, weight_v, cell_v, tap_v, meta, meta_v, place, sems = scratch
    blocks = vis.shape[0]
    rows = 3 * cap + 1
    sources = (routes, patch, vis, weight, cell, tap)
    targets = (routes_s, patch_s, vis_v, weight_v, cell_v, tap_v)
    copies = [pltpu.make_async_copy(a, b, sems.at[i]) for i, (a, b) in enumerate(zip(sources, targets))]
    for copy in copies:
        copy.start()

    def clear(d, carry):
        meta[d, cap] = 0
        return carry

    lax.fori_loop(0, peers, clear, 0, unroll=8)
    copies[0].wait()
    copies[1].wait()

    def choose(b, carry):
        d = routes_s[b]
        k = meta[d, cap]
        meta[d, cap] = k + 1
        meta[d, k] = patch_s[b]
        place[b] = d * rows + 3 * k
        return carry

    lax.fori_loop(0, blocks, choose, 0, unroll=8)
    meta_copy = pltpu.make_async_copy(meta, meta_v, sems.at[6])
    meta_copy.start()
    for copy in copies[2:]:
        copy.wait()

    def move(step, carry):
        first = pl.multiple_of(step * 8, 8)
        block_rows = pl.ds(first, 8)
        w = weight_v[block_rows, :]
        c = cell_v[block_rows, :]
        t = tap_v[block_rows, :]
        at_u = ((t >> 4) << 3) | ((c >> 6) & 7)
        at_v = ((t & 15) << 3) | (c & 7)
        code = (((c >> 9) << 17) | (((c >> 3) & 7) << 14) | (at_u << 7) | at_v).astype(f32)
        for i in range(8):
            row = place[first + i]
            both = vis_v[first + i] * w[i : i + 1, :]
            out[row] = both[0:1, :]
            out[row + 1] = both[1:2, :]
            out[row + 2] = code[i : i + 1, :]
        return carry

    lax.fori_loop(0, blocks // 8, move, 0)
    meta_copy.wait()

    def put_meta(d, carry):
        out[d * rows + 3 * cap] = meta_v[pl.ds(d, 1), :].astype(f32)
        return carry

    lax.fori_loop(0, peers, put_meta, 0, unroll=8)


def split(x):
    hi = x.astype(bf16)
    return hi, (x - hi.astype(f32)).astype(bf16)


def twice(x):
    return jnp.concatenate([x, x], axis=0)


def spread(groups, count, values):
    zero = jnp.zeros((16, ROWS), bf16)
    picks = [groups == 2.0 * g for g in range(count)]
    return [[jnp.where(pick, value, zero) for pick in picks] for value in values]


def patch_product(re, im, code, parity, table):
    sub = lax.broadcasted_iota(jnp.int32, (8, ROWS), 0)
    at_v = code & 127
    at_u = (code >> 7) & 127
    ku = jnp.take_along_axis(table, at_u, axis=1)
    kv = jnp.take_along_axis(table, at_v, axis=1)
    group_u = ((code >> 17) & 7) + jnp.where(sub < (at_u & 7), 1, 0)
    group_v = ((code >> 14) & 7) + jnp.where(sub < (at_v & 7), 1, 0) + 8 * parity
    step_u = jnp.concatenate([group_u, group_u - 1], axis=0).astype(f32).astype(bf16)
    step_v = jnp.concatenate([group_v & 15, (group_v + 15) & 15], axis=0).astype(f32).astype(bf16)
    u_re, u_im = re * ku, im * ku
    zero = jnp.zeros((16, ROWS), bf16)

    re_hi, re_lo = split(twice(u_re))
    im_hi, im_lo = split(twice(u_im))
    last_hi, last_lo = split(jnp.concatenate([u_re, u_im], axis=0))
    re_hi, re_lo, im_hi, im_lo = spread(step_u, SUB // 16, [re_hi, re_lo, im_hi, im_lo])
    past = twice(group_u).astype(f32).astype(bf16) == 8.0
    last_hi = jnp.where(past, last_hi, zero)
    last_lo = jnp.where(past, last_lo, zero)
    left_hi = jnp.concatenate(re_hi + im_hi + [last_hi], axis=0)
    left_lo = jnp.concatenate(re_lo + im_lo + [last_lo], axis=0)
    left = jnp.concatenate([left_hi, left_lo], axis=1)

    v_hi, v_lo = split(twice(kv))
    hi_rows, lo_rows = spread(step_v, ROWS // 16, [v_hi, v_lo])
    right = jnp.concatenate(hi_rows + lo_rows, axis=0)
    right = jnp.concatenate([right, right], axis=1)
    product = lax.dot_general(left, right, (((1,), (1,)), ((), ())), preferred_element_type=f32)
    return product[:, :ROWS] + product[:, ROWS:]


def tap_table(kernel):
    sub = lax.broadcasted_iota(jnp.int32, (8, ROWS), 0)
    lane = lanes((8, ROWS))
    which_tap = (sub - lane) & 7
    which_level = lane >> 3
    table = jnp.zeros((8, ROWS), f32)
    for a in range(KW):
        row = jnp.zeros((8, ROWS), f32)
        for o in range(OVER):
            row = jnp.where(which_level == o, kernel[a, o], row)
        table = jnp.where(which_tap == a, row, table)
    return table


def grid_kernel(peers, cap, with_low, kernel, arrived, out, right, *rest):
    low, rest = (rest[0], rest[1:]) if with_low else (None, rest)
    acc, stage, meta_v, meta, slots, meta_sem, out_sems = rest
    rows = 3 * cap + 1
    lane_row = lanes((1, ROWS))

    def entries(s, carry):
        row = arrived[s * rows + 3 * cap].astype(jnp.int32)
        entry = (s * rows + 3 * lane_row) * 512 + (row + FIRST)
        meta_v[pl.ds(s, 1), :] = jnp.where(lane_row < cap, entry, row)
        return carry

    lax.fori_loop(0, peers, entries, 0, unroll=8)
    meta_copy = pltpu.make_async_copy(meta_v, meta, meta_sem)
    meta_copy.start()
    table = tap_table(kernel)
    meta_copy.wait()
    share = (DUMMY + peers - 1) // peers

    def prepare(s, total):
        for k in range(cap):
            slots[total + k] = meta[s, k]
        for i in range(share):
            acc[s * share + i] = jnp.zeros((ROW_BLOCK, ROWS), f32)
        return total + meta[s, cap]

    total = lax.fori_loop(0, peers, prepare, 0)
    for k in range(UNROLL):
        slots[total + k] = DUMMY

    def work(step, carry):
        for i in range(UNROLL):
            entry = slots[step * UNROLL + i]
            row = entry >> 9
            where_to = entry & 511
            re = jnp.broadcast_to(arrived[row], (8, ROWS))
            im = jnp.broadcast_to(arrived[row + 1], (8, ROWS))
            code = jnp.broadcast_to(arrived[row + 2], (8, ROWS)).astype(jnp.int32)
            acc[where_to] += patch_product(re, im, code, entry & 1, table)
        return carry

    lax.fori_loop(0, (total + UNROLL - 1) // UNROLL, work, 0)

    lane = lanes((8, ROWS))

    def rows_of(c, h, band, col):
        part = acc[FIRST + band * SIDE + col, pl.ds(c * SUB + 8 * h, 8), :]
        if h == 0:
            part = part + acc[band * SIDE + col, pl.ds(2 * SUB + 8 * c, 8), :]
        return part

    def copy_out(band):
        rows = pl.ds(band * SUB, SUB)
        return pltpu.make_async_copy(stage.at[:, rows, :], out.at[:, rows, :], out_sems.at[band])

    def fold(pair, carry):
        for c in range(2):
            edge = jnp.zeros((8, ROWS), f32)
            for half in range(2):
                band = pair * 2 + half
                for h in range(8):
                    before = jnp.zeros((8, ROWS), f32)
                    for t in range(TILE // ROWS):
                        even = rows_of(c, h, band, 2 * t)
                        odd = rows_of(c, h, band, 2 * t + 1)
                        stage[c, pl.ds(band * SUB + 8 * h, 8), pl.ds(t * ROWS, ROWS)] = even + jnp.where(
                            lane < SUB, before, odd
                        )
                        before = odd
                    k = half * 8 + h
                    moved = pltpu.roll(before, 8 * k, 1) if k else before
                    edge = jnp.where((lane >> 3) == k, moved, edge)
            right[c, pair] = edge
        for half in range(2):
            copy_out(pair * 2 + half).start()
        return carry

    lax.fori_loop(0, SIDE // 2, fold, 0)
    if with_low:
        for c in range(2):
            before = jnp.zeros((8, ROWS), f32)
            for t in range(TILE // ROWS):
                rows = pl.ds(2 * SUB + 8 * c, 8)
                even = acc[FIRST + (SIDE - 1) * SIDE + 2 * t, rows, :]
                odd = acc[FIRST + (SIDE - 1) * SIDE + 2 * t + 1, rows, :]
                low[c, :, pl.ds(t * ROWS, ROWS)] = even + jnp.where(lane < SUB, before, odd)
                before = odd
            low[c, :, pl.ds(TILE, ROWS)] = jnp.where(lane < KW, before, 0.0)

    def finish(band, carry):
        copy_out(band).wait()
        return carry

    lax.fori_loop(0, SIDE, finish, 0)


def edge_kernel(edge, grid_in, grid_out, columns, in_sems, out_sems):
    lane = lanes((8, ROWS))
    pairs = SIDE // 2

    def fetch(pair):
        rows = pl.ds(pair * 2 * SUB, 2 * SUB)
        return pltpu.make_async_copy(
            grid_in.at[:, rows, pl.ds(0, ROWS)], columns.at[:, rows, :], in_sems.at[pair]
        )

    def put(pair):
        rows = pl.ds(pair * 2 * SUB, 2 * SUB)
        return pltpu.make_async_copy(
            columns.at[:, rows, :], grid_out.at[:, rows, pl.ds(0, ROWS)], out_sems.at[pair]
        )

    for pair in range(pairs):
        fetch(pair).start()

    def add(pair, carry):
        fetch(pair).wait()
        for c in range(2):
            packed = edge[c, pair]
            for k in range(16):
                moved = pltpu.roll(packed, ROWS - 8 * k, 1) if k else packed
                rows = pl.ds(pair * 2 * SUB + 8 * k, 8)
                columns[c, rows, :] += jnp.where(lane < KW, moved, 0.0)
        put(pair).start()
        return carry

    lax.fori_loop(0, pairs, add, 0)
    for pair in range(pairs):
        put(pair).wait()


def shifted(block, axis, distance):
    devices = range(lax.axis_size(axis))
    route = [(i - distance, i) for i in devices if i - distance in devices]
    return lax.ppermute(block, axis, route)


def shards(visibilities, vis_weight, cell_index, tap_offsets, routes, patch_index, kernel):
    blocks = visibilities.shape[0]
    tile_count = lax.axis_size("tile")
    plane_count = lax.axis_size("wp")
    peers = tile_count * plane_count
    cap = max(2, 2 * blocks // peers)
    rows = 3 * cap + 1
    vmem = pl.BlockSpec(memory_space=pltpu.VMEM)
    smem = pl.BlockSpec(memory_space=pltpu.SMEM)
    hbm = pl.BlockSpec(memory_space=pl.ANY)

    buckets = pl.pallas_call(
        functools.partial(pack_kernel, peers, cap),
        out_shape=jax.ShapeDtypeStruct((peers * rows, 1, ROWS), f32),
        in_specs=[hbm] * 6,
        out_specs=vmem,
        scratch_shapes=[
            pltpu.SMEM((blocks,), jnp.int32),
            pltpu.SMEM((blocks,), jnp.int32),
            pltpu.VMEM((blocks, 2, ROWS), f32),
            pltpu.VMEM((blocks, ROWS), f32),
            pltpu.VMEM((blocks, ROWS), jnp.int32),
            pltpu.VMEM((blocks, ROWS), jnp.int32),
            pltpu.SMEM((peers, ROWS), jnp.int32),
            pltpu.VMEM((peers, ROWS), jnp.int32),
            pltpu.SMEM((blocks,), jnp.int32),
            pltpu.SemaphoreType.DMA((7,)),
        ],
        compiler_params=pltpu.CompilerParams(vmem_limit_bytes=60 << 20),
        name="pack",
    )(routes[:, 0], patch_index, visibilities, vis_weight, cell_index, tap_offsets)

    arrived = lax.all_to_all(buckets, ("tile", "wp"), split_axis=0, concat_axis=0, tiled=True)

    with_low = tile_count > TCOLS
    out_shape = [
        jax.ShapeDtypeStruct((2, TILE, TILE), f32),
        jax.ShapeDtypeStruct((2, SIDE // 2, 8, ROWS), f32),
    ]
    out_specs = [hbm, vmem]
    if with_low:
        out_shape.append(jax.ShapeDtypeStruct((2, KW, TILE + ROWS), f32))
        out_specs.append(vmem)
    results = pl.pallas_call(
        functools.partial(grid_kernel, peers, cap, with_low),
        out_shape=out_shape,
        in_specs=[smem, vmem],
        out_specs=out_specs,
        scratch_shapes=[
            pltpu.VMEM((-(-DUMMY // peers) * peers + 1, ROW_BLOCK, ROWS), f32),
            pltpu.VMEM((2, TILE, TILE), f32),
            pltpu.VMEM((peers, ROWS), jnp.int32),
            pltpu.SMEM((peers, ROWS), jnp.int32),
            pltpu.SMEM((peers * cap + max(cap, UNROLL),), jnp.int32),
            pltpu.SemaphoreType.DMA,
            pltpu.SemaphoreType.DMA((SIDE,)),
        ],
        compiler_params=pltpu.CompilerParams(vmem_limit_bytes=48 << 20),
        name="grid",
    )(kernel.T, arrived)
    own, right = results[0], results[1]

    place = lax.axis_index("tile")
    from_left = shifted(right, "tile", 1)
    if with_low:
        from_left = jnp.where(place % TCOLS == 0, 0.0, from_left)
    own = pl.pallas_call(
        edge_kernel,
        out_shape=jax.ShapeDtypeStruct((2, TILE, TILE), f32),
        in_specs=[vmem, hbm],
        out_specs=hbm,
        scratch_shapes=[
            pltpu.VMEM((2, TILE, ROWS), f32),
            pltpu.SemaphoreType.DMA((SIDE // 2,)),
            pltpu.SemaphoreType.DMA((SIDE // 2,)),
        ],
        input_output_aliases={1: 0},
        compiler_params=pltpu.CompilerParams(vmem_limit_bytes=16 << 20),
        name="edges",
    )(from_left, own)
    if with_low:
        low = results[2]
        from_above = shifted(low, "tile", TCOLS)
        from_corner = shifted(low[:, :, TILE:], "tile", TCOLS + 1)
        from_corner = jnp.where(place % TCOLS == 0, 0.0, from_corner)
        own = own.at[:, :KW, :].add(from_above[:, :, :TILE])
        own = own.at[:, :KW, :ROWS].add(from_corner)
    return own.reshape(1, 1, 2, TILE, TILE)


def solution(mesh):
    in_specs = (
        P(("tile", "wp"), None, None),
        P(("tile", "wp"), None),
        P(("tile", "wp"), None),
        P(("tile", "wp"), None),
        P(("tile", "wp"), None),
        P(("tile", "wp")),
        P(),
    )
    out_specs = P("wp", "tile", None, None, None)
    return jax.shard_map(shards, mesh=mesh, in_specs=in_specs, out_specs=out_specs, check_vma=False)
```

```python
import functools

import jax
import jax.numpy as jnp
from jax import lax
from jax.experimental import pallas as pl
from jax.experimental.pallas import tpu as pltpu
from jax.sharding import PartitionSpec as P

TCOLS = 8
SUB = 64
KW = 8
OVER = 16
TILE = 1024
ROWS = 128
SIDE = TILE // SUB
PATCHES = SIDE * SIDE
ROW_BLOCK = 2 * (SUB + KW)
FIRST = SIDE
DUMMY = FIRST + PATCHES
UNROLL = 16

f32 = jnp.float32
bf16 = jnp.bfloat16


def lanes(shape):
    return lax.broadcasted_iota(jnp.int32, shape, len(shape) - 1)


def pack_kernel(peers, cap, routes, patch, vis, weight, cell, tap, out, *scratch):
    routes_s, patch_s, vis_v, weight_v, cell_v, tap_v, meta, meta_v, place, sems = scratch
    blocks = vis.shape[0]
    rows = 3 * cap + 1
    sources = (routes, patch, vis, weight, cell, tap)
    targets = (routes_s, patch_s, vis_v, weight_v, cell_v, tap_v)
    copies = [pltpu.make_async_copy(a, b, sems.at[i]) for i, (a, b) in enumerate(zip(sources, targets))]
    for copy in copies:
        copy.start()

    def clear(d, carry):
        meta[d, cap] = 0
        return carry

    lax.fori_loop(0, peers, clear, 0, unroll=8)
    copies[0].wait()
    copies[1].wait()

    def choose(b, carry):
        d = routes_s[b]
        k = meta[d, cap]
        meta[d, cap] = k + 1
        meta[d, k] = patch_s[b]
        place[b] = d * rows + 3 * k
        return carry

    lax.fori_loop(0, blocks, choose, 0, unroll=8)
    meta_copy = pltpu.make_async_copy(meta, meta_v, sems.at[6])
    meta_copy.start()
    for copy in copies[2:]:
        copy.wait()

    def move(step, carry):
        first = pl.multiple_of(step * 8, 8)
        block_rows = pl.ds(first, 8)
        w = weight_v[block_rows, :]
        c = cell_v[block_rows, :]
        t = tap_v[block_rows, :]
        at_u = ((t >> 4) << 3) | ((c >> 6) & 7)
        at_v = ((t & 15) << 3) | (c & 7)
        code = (((c >> 9) << 17) | (((c >> 3) & 7) << 14) | (at_u << 7) | at_v).astype(f32)
        for i in range(8):
            row = place[first + i]
            both = vis_v[first + i] * w[i : i + 1, :]
            out[row] = both[0:1, :]
            out[row + 1] = both[1:2, :]
            out[row + 2] = code[i : i + 1, :]
        return carry

    lax.fori_loop(0, blocks // 8, move, 0)
    meta_copy.wait()

    def put_meta(d, carry):
        out[d * rows + 3 * cap] = meta_v[pl.ds(d, 1), :].astype(f32)
        return carry

    lax.fori_loop(0, peers, put_meta, 0, unroll=8)


def split(x):
    hi = x.astype(bf16)
    return hi, (x - hi.astype(f32)).astype(bf16)


def twice(x):
    return jnp.concatenate([x, x], axis=0)


def spread(groups, count, values):
    zero = jnp.zeros((16, ROWS), bf16)
    picks = [groups == 2.0 * g for g in range(count)]
    return [[jnp.where(pick, value, zero) for pick in picks] for value in values]


def patch_product(re, im, code, parity, table):
    sub = lax.broadcasted_iota(jnp.int32, (8, ROWS), 0)
    at_v = code & 127
    at_u = (code >> 7) & 127
    ku = jnp.take_along_axis(table, at_u, axis=1)
    kv = jnp.take_along_axis(table, at_v, axis=1)
    group_u = ((code >> 17) & 7) + jnp.where(sub < (at_u & 7), 1, 0)
    group_v = ((code >> 14) & 7) + jnp.where(sub < (at_v & 7), 1, 0) + 8 * parity
    step_u = jnp.concatenate([group_u, group_u - 1], axis=0).astype(f32).astype(bf16)
    step_v = jnp.concatenate([group_v & 15, (group_v + 15) & 15], axis=0).astype(f32).astype(bf16)
    u_re, u_im = re * ku, im * ku
    zero = jnp.zeros((16, ROWS), bf16)

    re_hi, re_lo = split(twice(u_re))
    im_hi, im_lo = split(twice(u_im))
    last_hi, last_lo = split(jnp.concatenate([u_re, u_im], axis=0))
    re_hi, re_lo, im_hi, im_lo = spread(step_u, SUB // 16, [re_hi, re_lo, im_hi, im_lo])
    past = twice(group_u).astype(f32).astype(bf16) == 8.0
    last_hi = jnp.where(past, last_hi, zero)
    last_lo = jnp.where(past, last_lo, zero)
    left_hi = jnp.concatenate(re_hi + im_hi + [last_hi], axis=0)
    left_lo = jnp.concatenate(re_lo + im_lo + [last_lo], axis=0)
    left = jnp.concatenate([left_hi, left_lo], axis=1)

    v_hi, v_lo = split(twice(kv))
    hi_rows, lo_rows = spread(step_v, ROWS // 16, [v_hi, v_lo])
    right = jnp.concatenate(hi_rows + lo_rows, axis=0)
    right = jnp.concatenate([right, right], axis=1)
    product = lax.dot_general(left, right, (((1,), (1,)), ((), ())), preferred_element_type=f32)
    return product[:, :ROWS] + product[:, ROWS:]


def tap_table(kernel):
    sub = lax.broadcasted_iota(jnp.int32, (8, ROWS), 0)
    lane = lanes((8, ROWS))
    which_tap = (sub - lane) & 7
    which_level = lane >> 3
    table = jnp.zeros((8, ROWS), f32)
    for a in range(KW):
        row = jnp.zeros((8, ROWS), f32)
        for o in range(OVER):
            row = jnp.where(which_level == o, kernel[a, o], row)
        table = jnp.where(which_tap == a, row, table)
    return table


def grid_kernel(peers, cap, with_low, kernel, arrived, out, right, *rest):
    low, rest = (rest[0], rest[1:]) if with_low else (None, rest)
    acc, stage, meta_v, meta, slots, meta_sem, out_sems = rest
    rows = 3 * cap + 1
    lane_row = lanes((1, ROWS))

    def entries(s, carry):
        row = arrived[s * rows + 3 * cap].astype(jnp.int32)
        entry = (s * rows + 3 * lane_row) * 512 + (row + FIRST)
        meta_v[pl.ds(s, 1), :] = jnp.where(lane_row < cap, entry, row)
        return carry

    lax.fori_loop(0, peers, entries, 0, unroll=8)
    meta_copy = pltpu.make_async_copy(meta_v, meta, meta_sem)
    meta_copy.start()
    table = tap_table(kernel)
    meta_copy.wait()
    share = (DUMMY + peers - 1) // peers

    def prepare(s, total):
        for k in range(cap):
            slots[total + k] = meta[s, k]
        for i in range(share):
            acc[s * share + i] = jnp.zeros((ROW_BLOCK, ROWS), f32)
        return total + meta[s, cap]

    total = lax.fori_loop(0, peers, prepare, 0)
    for k in range(UNROLL):
        slots[total + k] = DUMMY

    def work(step, carry):
        for i in range(UNROLL):
            entry = slots[step * UNROLL + i]
            row = entry >> 9
            where_to = entry & 511
            re = jnp.broadcast_to(arrived[row], (8, ROWS))
            im = jnp.broadcast_to(arrived[row + 1], (8, ROWS))
            code = jnp.broadcast_to(arrived[row + 2], (8, ROWS)).astype(jnp.int32)
            acc[where_to] += patch_product(re, im, code, entry & 1, table)
        return carry

    lax.fori_loop(0, (total + UNROLL - 1) // UNROLL, work, 0)

    lane = lanes((8, ROWS))

    def rows_of(c, h, band, col):
        part = acc[FIRST + band * SIDE + col, pl.ds(c * SUB + 8 * h, 8), :]
        if h == 0:
            part = part + acc[band * SIDE + col, pl.ds(2 * SUB + 8 * c, 8), :]
        return part

    def copy_out(band):
        rows = pl.ds(band * SUB, SUB)
        return pltpu.make_async_copy(stage.at[:, rows, :], out.at[:, rows, :], out_sems.at[band])

    def fold(pair, carry):
        for c in range(2):
            edge = jnp.zeros((8, ROWS), f32)
            for half in range(2):
                band = pair * 2 + half
                for h in range(8):
                    before = jnp.zeros((8, ROWS), f32)
                    for t in range(TILE // ROWS):
                        even = rows_of(c, h, band, 2 * t)
                        odd = rows_of(c, h, band, 2 * t + 1)
                        stage[c, pl.ds(band * SUB + 8 * h, 8), pl.ds(t * ROWS, ROWS)] = even + jnp.where(
                            lane < SUB, before, odd
                        )
                        before = odd
                    k = half * 8 + h
                    moved = pltpu.roll(before, 8 * k, 1) if k else before
                    edge = jnp.where((lane >> 3) == k, moved, edge)
            right[c, pair] = edge
        for half in range(2):
            copy_out(pair * 2 + half).start()
        return carry

    lax.fori_loop(0, SIDE // 2, fold, 0)
    if with_low:
        for c in range(2):
            before = jnp.zeros((8, ROWS), f32)
            for t in range(TILE // ROWS):
                rows = pl.ds(2 * SUB + 8 * c, 8)
                even = acc[FIRST + (SIDE - 1) * SIDE + 2 * t, rows, :]
                odd = acc[FIRST + (SIDE - 1) * SIDE + 2 * t + 1, rows, :]
                low[c, :, pl.ds(t * ROWS, ROWS)] = even + jnp.where(lane < SUB, before, odd)
                before = odd
            low[c, :, pl.ds(TILE, ROWS)] = jnp.where(lane < KW, before, 0.0)

    def finish(band, carry):
        copy_out(band).wait()
        return carry

    lax.fori_loop(0, SIDE, finish, 0)


def edge_kernel(edge, grid_in, grid_out, columns, in_sems, out_sems):
    lane = lanes((8, ROWS))
    pairs = SIDE // 2

    def fetch(pair):
        rows = pl.ds(pair * 2 * SUB, 2 * SUB)
        return pltpu.make_async_copy(
            grid_in.at[:, rows, pl.ds(0, ROWS)], columns.at[:, rows, :], in_sems.at[pair]
        )

    def put(pair):
        rows = pl.ds(pair * 2 * SUB, 2 * SUB)
        return pltpu.make_async_copy(
            columns.at[:, rows, :], grid_out.at[:, rows, pl.ds(0, ROWS)], out_sems.at[pair]
        )

    for pair in range(pairs):
        fetch(pair).start()

    def add(pair, carry):
        fetch(pair).wait()
        for c in range(2):
            packed = edge[c, pair]
            for k in range(16):
                moved = pltpu.roll(packed, ROWS - 8 * k, 1) if k else packed
                rows = pl.ds(pair * 2 * SUB + 8 * k, 8)
                columns[c, rows, :] += jnp.where(lane < KW, moved, 0.0)
        put(pair).start()
        return carry

    lax.fori_loop(0, pairs, add, 0)
    for pair in range(pairs):
        put(pair).wait()


def shifted(block, axis, distance):
    devices = range(lax.axis_size(axis))
    route = [(i - distance, i) for i in devices if i - distance in devices]
    return lax.ppermute(block, axis, route)


def shards(visibilities, vis_weight, cell_index, tap_offsets, routes, patch_index, kernel):
    blocks = visibilities.shape[0]
    tile_count = lax.axis_size("tile")
    plane_count = lax.axis_size("wp")
    peers = tile_count * plane_count
    cap = max(2, 2 * blocks // peers)
    rows = 3 * cap + 1
    vmem = pl.BlockSpec(memory_space=pltpu.VMEM)
    smem = pl.BlockSpec(memory_space=pltpu.SMEM)
    hbm = pl.BlockSpec(memory_space=pl.ANY)

    buckets = pl.pallas_call(
        functools.partial(pack_kernel, peers, cap),
        out_shape=jax.ShapeDtypeStruct((peers * rows, 1, ROWS), f32),
        in_specs=[hbm] * 6,
        out_specs=vmem,
        scratch_shapes=[
            pltpu.SMEM((blocks,), jnp.int32),
            pltpu.SMEM((blocks,), jnp.int32),
            pltpu.VMEM((blocks, 2, ROWS), f32),
            pltpu.VMEM((blocks, ROWS), f32),
            pltpu.VMEM((blocks, ROWS), jnp.int32),
            pltpu.VMEM((blocks, ROWS), jnp.int32),
            pltpu.SMEM((peers, ROWS), jnp.int32),
            pltpu.VMEM((peers, ROWS), jnp.int32),
            pltpu.SMEM((blocks,), jnp.int32),
            pltpu.SemaphoreType.DMA((7,)),
        ],
        compiler_params=pltpu.CompilerParams(vmem_limit_bytes=60 << 20),
        name="pack",
    )(routes[:, 0], patch_index, visibilities, vis_weight, cell_index, tap_offsets)

    arrived = lax.all_to_all(buckets, ("tile", "wp"), split_axis=0, concat_axis=0, tiled=True)

    with_low = tile_count > TCOLS
    out_shape = [
        jax.ShapeDtypeStruct((2, TILE, TILE), f32),
        jax.ShapeDtypeStruct((2, SIDE // 2, 8, ROWS), f32),
    ]
    out_specs = [hbm, vmem]
    if with_low:
        out_shape.append(jax.ShapeDtypeStruct((2, KW, TILE + ROWS), f32))
        out_specs.append(vmem)
    results = pl.pallas_call(
        functools.partial(grid_kernel, peers, cap, with_low),
        out_shape=out_shape,
        in_specs=[smem, vmem],
        out_specs=out_specs,
        scratch_shapes=[
            pltpu.VMEM((-(-DUMMY // peers) * peers + 1, ROW_BLOCK, ROWS), f32),
            pltpu.VMEM((2, TILE, TILE), f32),
            pltpu.VMEM((peers, ROWS), jnp.int32),
            pltpu.SMEM((peers, ROWS), jnp.int32),
            pltpu.SMEM((peers * cap + max(cap, UNROLL),), jnp.int32),
            pltpu.SemaphoreType.DMA,
            pltpu.SemaphoreType.DMA((SIDE,)),
        ],
        compiler_params=pltpu.CompilerParams(vmem_limit_bytes=48 << 20),
        name="grid",
    )(kernel.T, arrived)
    own, right = results[0], results[1]

    place = lax.axis_index("tile")
    from_left = shifted(right, "tile", 1)
    if with_low:
        from_left = jnp.where(place % TCOLS == 0, 0.0, from_left)
    own = pl.pallas_call(
        edge_kernel,
        out_shape=jax.ShapeDtypeStruct((2, TILE, TILE), f32),
        in_specs=[vmem, hbm],
        out_specs=hbm,
        scratch_shapes=[
            pltpu.VMEM((2, TILE, ROWS), f32),
            pltpu.SemaphoreType.DMA((SIDE // 2,)),
            pltpu.SemaphoreType.DMA((SIDE // 2,)),
        ],
        input_output_aliases={1: 0},
        compiler_params=pltpu.CompilerParams(vmem_limit_bytes=16 << 20),
        name="edges",
    )(from_left, own)
    if with_low:
        low = results[2]
        from_above = shifted(low, "tile", TCOLS)
        from_corner = shifted(low[:, :, TILE:], "tile", TCOLS + 1)
        from_corner = jnp.where(place % TCOLS == 0, 0.0, from_corner)
        own = own.at[:, :KW, :].add(from_above[:, :, :TILE])
        own = own.at[:, :KW, :ROWS].add(from_corner)
    return own.reshape(1, 1, 2, TILE, TILE)


def solution(mesh):
    in_specs = (
        P(("tile", "wp"), None, None),
        P(("tile", "wp"), None),
        P(("tile", "wp"), None),
        P(("tile", "wp"), None),
        P(("tile", "wp"), None),
        P(("tile", "wp")),
        P(),
    )
    out_specs = P("wp", "tile", None, None, None)
    return jax.shard_map(shards, mesh=mesh, in_specs=in_specs, out_specs=out_specs, check_vma=False)
```

```python
import functools

import jax
import jax.numpy as jnp
from jax import lax
from jax.experimental import pallas as pl
from jax.experimental.pallas import tpu as pltpu
from jax.sharding import PartitionSpec as P

TCOLS = 8
SUB = 64
KW = 8
OVER = 16
TILE = 1024
ROWS = 128
SIDE = TILE // SUB
PATCHES = SIDE * SIDE
ROW_BLOCK = 2 * (SUB + KW)
FIRST = SIDE
DUMMY = FIRST + PATCHES
UNROLL = 16

f32 = jnp.float32
bf16 = jnp.bfloat16


def lanes(shape):
    return lax.broadcasted_iota(jnp.int32, shape, len(shape) - 1)


def pack_kernel(peers, cap, routes, patch, vis, weight, cell, tap, out, *scratch):
    routes_s, patch_s, vis_v, weight_v, cell_v, tap_v, meta, meta_v, place, sems = scratch
    blocks = vis.shape[0]
    rows = 3 * cap + 1
    sources = (routes, patch, vis, weight, cell, tap)
    targets = (routes_s, patch_s, vis_v, weight_v, cell_v, tap_v)
    copies = [pltpu.make_async_copy(a, b, sems.at[i]) for i, (a, b) in enumerate(zip(sources, targets))]
    for copy in copies:
        copy.start()

    def clear(d, carry):
        meta[d, cap] = 0
        return carry

    lax.fori_loop(0, peers, clear, 0, unroll=8)
    copies[0].wait()
    copies[1].wait()

    def choose(b, carry):
        d = routes_s[b]
        k = meta[d, cap]
        meta[d, cap] = k + 1
        meta[d, k] = patch_s[b]
        place[b] = d * rows + 3 * k
        return carry

    lax.fori_loop(0, blocks, choose, 0, unroll=8)
    meta_copy = pltpu.make_async_copy(meta, meta_v, sems.at[6])
    meta_copy.start()
    for copy in copies[2:]:
        copy.wait()

    def move(step, carry):
        first = pl.multiple_of(step * 8, 8)
        block_rows = pl.ds(first, 8)
        w = weight_v[block_rows, :]
        c = cell_v[block_rows, :]
        t = tap_v[block_rows, :]
        at_u = ((t >> 4) << 3) | ((c >> 6) & 7)
        at_v = ((t & 15) << 3) | (c & 7)
        code = (((c >> 9) << 17) | (((c >> 3) & 7) << 14) | (at_u << 7) | at_v).astype(f32)
        for i in range(8):
            row = place[first + i]
            both = vis_v[first + i] * w[i : i + 1, :]
            out[row] = both[0:1, :]
            out[row + 1] = both[1:2, :]
            out[row + 2] = code[i : i + 1, :]
        return carry

    lax.fori_loop(0, blocks // 8, move, 0)
    meta_copy.wait()

    def put_meta(d, carry):
        out[d * rows + 3 * cap] = meta_v[pl.ds(d, 1), :].astype(f32)
        return carry

    lax.fori_loop(0, peers, put_meta, 0, unroll=8)


def split(x):
    hi = x.astype(bf16)
    return hi, (x - hi.astype(f32)).astype(bf16)


def twice(x):
    return jnp.concatenate([x, x], axis=0)


def spread(groups, count, values):
    zero = jnp.zeros((16, ROWS), bf16)
    picks = [groups == 2.0 * g for g in range(count)]
    return [[jnp.where(pick, value, zero) for pick in picks] for value in values]


def patch_product(re, im, code, parity, table):
    sub = lax.broadcasted_iota(jnp.int32, (8, ROWS), 0)
    at_v = code & 127
    at_u = (code >> 7) & 127
    ku = jnp.take_along_axis(table, at_u, axis=1)
    kv = jnp.take_along_axis(table, at_v, axis=1)
    group_u = ((code >> 17) & 7) + jnp.where(sub < (at_u & 7), 1, 0)
    group_v = ((code >> 14) & 7) + jnp.where(sub < (at_v & 7), 1, 0) + 8 * parity
    step_u = jnp.concatenate([group_u, group_u - 1], axis=0).astype(f32).astype(bf16)
    step_v = jnp.concatenate([group_v & 15, (group_v + 15) & 15], axis=0).astype(f32).astype(bf16)
    u_re, u_im = re * ku, im * ku
    zero = jnp.zeros((16, ROWS), bf16)

    re_hi, re_lo = split(twice(u_re))
    im_hi, im_lo = split(twice(u_im))
    last_hi, last_lo = split(jnp.concatenate([u_re, u_im], axis=0))
    re_hi, re_lo, im_hi, im_lo = spread(step_u, SUB // 16, [re_hi, re_lo, im_hi, im_lo])
    past = twice(group_u).astype(f32).astype(bf16) == 8.0
    last_hi = jnp.where(past, last_hi, zero)
    last_lo = jnp.where(past, last_lo, zero)
    left_hi = jnp.concatenate(re_hi + im_hi + [last_hi], axis=0)
    left_lo = jnp.concatenate(re_lo + im_lo + [last_lo], axis=0)
    left = jnp.concatenate([left_hi, left_lo, left_hi], axis=1)

    v_hi, v_lo = split(twice(kv))
    hi_rows, lo_rows = spread(step_v, ROWS // 16, [v_hi, v_lo])
    right_hi = jnp.concatenate(hi_rows, axis=0)
    right = jnp.concatenate([right_hi, right_hi, jnp.concatenate(lo_rows, axis=0)], axis=1)
    return lax.dot_general(left, right, (((1,), (1,)), ((), ())), preferred_element_type=f32)


def tap_table(kernel):
    sub = lax.broadcasted_iota(jnp.int32, (8, ROWS), 0)
    lane = lanes((8, ROWS))
    which_tap = (sub - lane) & 7
    which_level = lane >> 3
    table = jnp.zeros((8, ROWS), f32)
    for a in range(KW):
        row = jnp.zeros((8, ROWS), f32)
        for o in range(OVER):
            row = jnp.where(which_level == o, kernel[a, o], row)
        table = jnp.where(which_tap == a, row, table)
    return table


def grid_kernel(peers, cap, with_low, kernel, arrived, out, right, *rest):
    low, rest = (rest[0], rest[1:]) if with_low else (None, rest)
    acc, stage, meta_v, meta, slots, meta_sem, out_sems = rest
    rows = 3 * cap + 1
    lane_row = lanes((1, ROWS))

    def entries(s, carry):
        row = arrived[s * rows + 3 * cap].astype(jnp.int32)
        entry = (s * rows + 3 * lane_row) * 512 + (row + FIRST)
        meta_v[pl.ds(s, 1), :] = jnp.where(lane_row < cap, entry, row)
        return carry

    lax.fori_loop(0, peers, entries, 0, unroll=8)
    meta_copy = pltpu.make_async_copy(meta_v, meta, meta_sem)
    meta_copy.start()
    table = tap_table(kernel)
    meta_copy.wait()
    share = (DUMMY + peers - 1) // peers

    def prepare(s, total):
        for k in range(cap):
            slots[total + k] = meta[s, k]
        for i in range(share):
            acc[s * share + i] = jnp.zeros((ROW_BLOCK, ROWS), f32)
        return total + meta[s, cap]

    total = lax.fori_loop(0, peers, prepare, 0)
    for k in range(UNROLL):
        slots[total + k] = DUMMY

    def work(step, carry):
        for i in range(UNROLL):
            entry = slots[step * UNROLL + i]
            row = entry >> 9
            where_to = entry & 511
            re = jnp.broadcast_to(arrived[row], (8, ROWS))
            im = jnp.broadcast_to(arrived[row + 1], (8, ROWS))
            code = jnp.broadcast_to(arrived[row + 2], (8, ROWS)).astype(jnp.int32)
            acc[where_to] += patch_product(re, im, code, entry & 1, table)
        return carry

    lax.fori_loop(0, (total + UNROLL - 1) // UNROLL, work, 0)

    lane = lanes((8, ROWS))

    def rows_of(c, h, band, col):
        part = acc[FIRST + band * SIDE + col, pl.ds(c * SUB + 8 * h, 8), :]
        if h == 0:
            part = part + acc[band * SIDE + col, pl.ds(2 * SUB + 8 * c, 8), :]
        return part

    def copy_out(band):
        rows = pl.ds(band * SUB, SUB)
        return pltpu.make_async_copy(stage.at[:, rows, :], out.at[:, rows, :], out_sems.at[band])

    def fold(pair, carry):
        for c in range(2):
            edge = jnp.zeros((8, ROWS), f32)
            for half in range(2):
                band = pair * 2 + half
                for h in range(8):
                    before = jnp.zeros((8, ROWS), f32)
                    for t in range(TILE // ROWS):
                        even = rows_of(c, h, band, 2 * t)
                        odd = rows_of(c, h, band, 2 * t + 1)
                        stage[c, pl.ds(band * SUB + 8 * h, 8), pl.ds(t * ROWS, ROWS)] = even + jnp.where(
                            lane < SUB, before, odd
                        )
                        before = odd
                    k = half * 8 + h
                    moved = pltpu.roll(before, 8 * k, 1) if k else before
                    edge = jnp.where((lane >> 3) == k, moved, edge)
            right[c, pair] = edge
        for half in range(2):
            copy_out(pair * 2 + half).start()
        return carry

    lax.fori_loop(0, SIDE // 2, fold, 0)
    if with_low:
        for c in range(2):
            before = jnp.zeros((8, ROWS), f32)
            for t in range(TILE // ROWS):
                rows = pl.ds(2 * SUB + 8 * c, 8)
                even = acc[FIRST + (SIDE - 1) * SIDE + 2 * t, rows, :]
                odd = acc[FIRST + (SIDE - 1) * SIDE + 2 * t + 1, rows, :]
                low[c, :, pl.ds(t * ROWS, ROWS)] = even + jnp.where(lane < SUB, before, odd)
                before = odd
            low[c, :, pl.ds(TILE, ROWS)] = jnp.where(lane < KW, before, 0.0)

    def finish(band, carry):
        copy_out(band).wait()
        return carry

    lax.fori_loop(0, SIDE, finish, 0)


def edge_kernel(edge, grid_in, grid_out, columns, in_sems, out_sems):
    lane = lanes((8, ROWS))
    pairs = SIDE // 2

    def fetch(pair):
        rows = pl.ds(pair * 2 * SUB, 2 * SUB)
        return pltpu.make_async_copy(
            grid_in.at[:, rows, pl.ds(0, ROWS)], columns.at[:, rows, :], in_sems.at[pair]
        )

    def put(pair):
        rows = pl.ds(pair * 2 * SUB, 2 * SUB)
        return pltpu.make_async_copy(
            columns.at[:, rows, :], grid_out.at[:, rows, pl.ds(0, ROWS)], out_sems.at[pair]
        )

    for pair in range(pairs):
        fetch(pair).start()

    def add(pair, carry):
        fetch(pair).wait()
        for c in range(2):
            packed = edge[c, pair]
            for k in range(16):
                moved = pltpu.roll(packed, ROWS - 8 * k, 1) if k else packed
                rows = pl.ds(pair * 2 * SUB + 8 * k, 8)
                columns[c, rows, :] += jnp.where(lane < KW, moved, 0.0)
        put(pair).start()
        return carry

    lax.fori_loop(0, pairs, add, 0)
    for pair in range(pairs):
        put(pair).wait()


def shifted(block, axis, distance):
    devices = range(lax.axis_size(axis))
    route = [(i - distance, i) for i in devices if i - distance in devices]
    return lax.ppermute(block, axis, route)


def shards(visibilities, vis_weight, cell_index, tap_offsets, routes, patch_index, kernel):
    blocks = visibilities.shape[0]
    tile_count = lax.axis_size("tile")
    plane_count = lax.axis_size("wp")
    peers = tile_count * plane_count
    cap = max(2, 2 * blocks // peers)
    rows = 3 * cap + 1
    vmem = pl.BlockSpec(memory_space=pltpu.VMEM)
    smem = pl.BlockSpec(memory_space=pltpu.SMEM)
    hbm = pl.BlockSpec(memory_space=pl.ANY)

    buckets = pl.pallas_call(
        functools.partial(pack_kernel, peers, cap),
        out_shape=jax.ShapeDtypeStruct((peers * rows, 1, ROWS), f32),
        in_specs=[hbm] * 6,
        out_specs=vmem,
        scratch_shapes=[
            pltpu.SMEM((blocks,), jnp.int32),
            pltpu.SMEM((blocks,), jnp.int32),
            pltpu.VMEM((blocks, 2, ROWS), f32),
            pltpu.VMEM((blocks, ROWS), f32),
            pltpu.VMEM((blocks, ROWS), jnp.int32),
            pltpu.VMEM((blocks, ROWS), jnp.int32),
            pltpu.SMEM((peers, ROWS), jnp.int32),
            pltpu.VMEM((peers, ROWS), jnp.int32),
            pltpu.SMEM((blocks,), jnp.int32),
            pltpu.SemaphoreType.DMA((7,)),
        ],
        compiler_params=pltpu.CompilerParams(vmem_limit_bytes=60 << 20),
        name="pack",
    )(routes[:, 0], patch_index, visibilities, vis_weight, cell_index, tap_offsets)

    arrived = lax.all_to_all(buckets, ("tile", "wp"), split_axis=0, concat_axis=0, tiled=True)

    with_low = tile_count > TCOLS
    out_shape = [
        jax.ShapeDtypeStruct((2, TILE, TILE), f32),
        jax.ShapeDtypeStruct((2, SIDE // 2, 8, ROWS), f32),
    ]
    out_specs = [hbm, vmem]
    if with_low:
        out_shape.append(jax.ShapeDtypeStruct((2, KW, TILE + ROWS), f32))
        out_specs.append(vmem)
    results = pl.pallas_call(
        functools.partial(grid_kernel, peers, cap, with_low),
        out_shape=out_shape,
        in_specs=[smem, vmem],
        out_specs=out_specs,
        scratch_shapes=[
            pltpu.VMEM((-(-DUMMY // peers) * peers + 1, ROW_BLOCK, ROWS), f32),
            pltpu.VMEM((2, TILE, TILE), f32),
            pltpu.VMEM((peers, ROWS), jnp.int32),
            pltpu.SMEM((peers, ROWS), jnp.int32),
            pltpu.SMEM((peers * cap + max(cap, UNROLL),), jnp.int32),
            pltpu.SemaphoreType.DMA,
            pltpu.SemaphoreType.DMA((SIDE,)),
        ],
        compiler_params=pltpu.CompilerParams(vmem_limit_bytes=48 << 20),
        name="grid",
    )(kernel.T, arrived)
    own, right = results[0], results[1]

    place = lax.axis_index("tile")
    from_left = shifted(right, "tile", 1)
    if with_low:
        from_left = jnp.where(place % TCOLS == 0, 0.0, from_left)
    own = pl.pallas_call(
        edge_kernel,
        out_shape=jax.ShapeDtypeStruct((2, TILE, TILE), f32),
        in_specs=[vmem, hbm],
        out_specs=hbm,
        scratch_shapes=[
            pltpu.VMEM((2, TILE, ROWS), f32),
            pltpu.SemaphoreType.DMA((SIDE // 2,)),
            pltpu.SemaphoreType.DMA((SIDE // 2,)),
        ],
        input_output_aliases={1: 0},
        compiler_params=pltpu.CompilerParams(vmem_limit_bytes=16 << 20),
        name="edges",
    )(from_left, own)
    if with_low:
        low = results[2]
        from_above = shifted(low, "tile", TCOLS)
        from_corner = shifted(low[:, :, TILE:], "tile", TCOLS + 1)
        from_corner = jnp.where(place % TCOLS == 0, 0.0, from_corner)
        own = own.at[:, :KW, :].add(from_above[:, :, :TILE])
        own = own.at[:, :KW, :ROWS].add(from_corner)
    return own.reshape(1, 1, 2, TILE, TILE)


def solution(mesh):
    in_specs = (
        P(("tile", "wp"), None, None),
        P(("tile", "wp"), None),
        P(("tile", "wp"), None),
        P(("tile", "wp"), None),
        P(("tile", "wp"), None),
        P(("tile", "wp")),
        P(),
    )
    out_specs = P("wp", "tile", None, None, None)
    return jax.shard_map(shards, mesh=mesh, in_specs=in_specs, out_specs=out_specs, check_vma=False)
```

```python
import functools

import jax
import jax.numpy as jnp
from jax import lax
from jax.experimental import pallas as pl
from jax.experimental.pallas import tpu as pltpu
from jax.sharding import PartitionSpec as P

TCOLS = 8
SUB = 64
KW = 8
OVER = 16
TILE = 1024
ROWS = 128
SIDE = TILE // SUB
PATCHES = SIDE * SIDE
ROW_BLOCK = 2 * (SUB + KW)
FIRST = SIDE
DUMMY = FIRST + PATCHES
UNROLL = 16

f32 = jnp.float32
bf16 = jnp.bfloat16


def lanes(shape):
    return lax.broadcasted_iota(jnp.int32, shape, len(shape) - 1)


def pack_kernel(peers, cap, routes, patch, vis, weight, cell, tap, out, *scratch):
    routes_s, patch_s, vis_v, weight_v, cell_v, tap_v, meta, meta_v, place, sems = scratch
    blocks = vis.shape[0]
    rows = 3 * cap + 1
    sources = (routes, patch, vis, weight, cell, tap)
    targets = (routes_s, patch_s, vis_v, weight_v, cell_v, tap_v)
    copies = [pltpu.make_async_copy(a, b, sems.at[i]) for i, (a, b) in enumerate(zip(sources, targets))]
    for copy in copies:
        copy.start()

    def clear(d, carry):
        meta[d, cap] = 0
        return carry

    lax.fori_loop(0, peers, clear, 0, unroll=8)
    copies[0].wait()
    copies[1].wait()

    def choose(b, carry):
        d = routes_s[b]
        k = meta[d, cap]
        meta[d, cap] = k + 1
        meta[d, k] = patch_s[b]
        place[b] = d * rows + 3 * k
        return carry

    lax.fori_loop(0, blocks, choose, 0, unroll=8)
    meta_copy = pltpu.make_async_copy(meta, meta_v, sems.at[6])
    meta_copy.start()
    for copy in copies[2:]:
        copy.wait()

    def move(step, carry):
        first = pl.multiple_of(step * 8, 8)
        block_rows = pl.ds(first, 8)
        w = weight_v[block_rows, :]
        c = cell_v[block_rows, :]
        t = tap_v[block_rows, :]
        at_u = ((t >> 4) << 3) | ((c >> 6) & 7)
        at_v = ((t & 15) << 3) | (c & 7)
        code = (((c >> 9) << 17) | (((c >> 3) & 7) << 14) | (at_u << 7) | at_v).astype(f32)
        for i in range(8):
            row = place[first + i]
            both = vis_v[first + i] * w[i : i + 1, :]
            out[row] = both[0:1, :]
            out[row + 1] = both[1:2, :]
            out[row + 2] = code[i : i + 1, :]
        return carry

    lax.fori_loop(0, blocks // 8, move, 0)
    meta_copy.wait()

    def put_meta(d, carry):
        out[d * rows + 3 * cap] = meta_v[pl.ds(d, 1), :].astype(f32)
        return carry

    lax.fori_loop(0, peers, put_meta, 0, unroll=8)


def split(x):
    hi = x.astype(bf16)
    return hi, (x - hi.astype(f32)).astype(bf16)


def twice(x):
    return jnp.concatenate([x, x], axis=0)


def look_up(table, index):
    numbers = lax.GatherDimensionNumbers(
        offset_dims=(),
        collapsed_slice_dims=(1,),
        start_index_map=(1,),
        operand_batching_dims=(0,),
        start_indices_batching_dims=(0,),
    )
    return lax.gather(
        table, index[..., None], numbers, (1, 1), mode=lax.GatherScatterMode.PROMISE_IN_BOUNDS
    )


def spread(groups, count, values):
    zero = jnp.zeros((16, ROWS), bf16)
    picks = [groups == 2.0 * g for g in range(count)]
    return [[jnp.where(pick, value, zero) for pick in picks] for value in values]


def patch_product(re, im, code, parity, table):
    sub = lax.broadcasted_iota(jnp.int32, (8, ROWS), 0)
    at_v = code & 127
    at_u = (code >> 7) & 127
    ku = look_up(table, at_u)
    kv = look_up(table, at_v)
    group_u = ((code >> 17) & 7) + jnp.where(sub < (at_u & 7), 1, 0)
    group_v = ((code >> 14) & 7) + jnp.where(sub < (at_v & 7), 1, 0) + 8 * parity
    step_u = jnp.concatenate([group_u, group_u - 1], axis=0).astype(f32).astype(bf16)
    step_v = jnp.concatenate([group_v & 15, (group_v + 15) & 15], axis=0).astype(f32).astype(bf16)
    u_re, u_im = re * ku, im * ku
    zero = jnp.zeros((16, ROWS), bf16)

    re_hi, re_lo = split(twice(u_re))
    im_hi, im_lo = split(twice(u_im))
    last_hi, last_lo = split(jnp.concatenate([u_re, u_im], axis=0))
    re_hi, re_lo, im_hi, im_lo = spread(step_u, SUB // 16, [re_hi, re_lo, im_hi, im_lo])
    past = twice(group_u).astype(f32).astype(bf16) == 8.0
    last_hi = jnp.where(past, last_hi, zero)
    last_lo = jnp.where(past, last_lo, zero)
    left_hi = jnp.concatenate(re_hi + im_hi + [last_hi], axis=0)
    left_lo = jnp.concatenate(re_lo + im_lo + [last_lo], axis=0)
    left = jnp.concatenate([left_hi, left_lo], axis=0)
    left = jnp.concatenate([left, left], axis=1)

    v_hi, v_lo = split(twice(kv))
    hi_rows, lo_rows = spread(step_v, ROWS // 16, [v_hi, v_lo])
    right = jnp.concatenate([jnp.concatenate(hi_rows, axis=0), jnp.concatenate(lo_rows, axis=0)], axis=1)
    product = lax.dot_general(left, right, (((1,), (1,)), ((), ())), preferred_element_type=f32)
    return product[:ROW_BLOCK] + product[ROW_BLOCK:]


def tap_table(kernel):
    sub = lax.broadcasted_iota(jnp.int32, (8, ROWS), 0)
    lane = lanes((8, ROWS))
    which_tap = (sub - lane) & 7
    which_level = lane >> 3
    table = jnp.zeros((8, ROWS), f32)
    for a in range(KW):
        row = jnp.zeros((8, ROWS), f32)
        for o in range(OVER):
            row = jnp.where(which_level == o, kernel[a, o], row)
        table = jnp.where(which_tap == a, row, table)
    return table


def grid_kernel(peers, cap, with_low, kernel, arrived, out, right, *rest):
    low, rest = (rest[0], rest[1:]) if with_low else (None, rest)
    acc, stage, meta_v, meta, slots, meta_sem, out_sems = rest
    rows = 3 * cap + 1
    lane_row = lanes((1, ROWS))

    def entries(s, carry):
        row = arrived[s * rows + 3 * cap].astype(jnp.int32)
        entry = (s * rows + 3 * lane_row) * 512 + (row + FIRST)
        meta_v[pl.ds(s, 1), :] = jnp.where(lane_row < cap, entry, row)
        return carry

    lax.fori_loop(0, peers, entries, 0, unroll=8)
    meta_copy = pltpu.make_async_copy(meta_v, meta, meta_sem)
    meta_copy.start()
    table = tap_table(kernel)
    meta_copy.wait()
    share = (DUMMY + peers - 1) // peers

    def prepare(s, total):
        for k in range(cap):
            slots[total + k] = meta[s, k]
        for i in range(share):
            acc[s * share + i] = jnp.zeros((ROW_BLOCK, ROWS), f32)
        return total + meta[s, cap]

    total = lax.fori_loop(0, peers, prepare, 0)
    for k in range(UNROLL):
        slots[total + k] = DUMMY

    def work(step, carry):
        for i in range(UNROLL):
            entry = slots[step * UNROLL + i]
            row = entry >> 9
            where_to = entry & 511
            re = jnp.broadcast_to(arrived[row], (8, ROWS))
            im = jnp.broadcast_to(arrived[row + 1], (8, ROWS))
            code = jnp.broadcast_to(arrived[row + 2], (8, ROWS)).astype(jnp.int32)
            acc[where_to] += patch_product(re, im, code, entry & 1, table)
        return carry

    lax.fori_loop(0, (total + UNROLL - 1) // UNROLL, work, 0)

    lane = lanes((8, ROWS))

    def rows_of(c, h, band, col):
        part = acc[FIRST + band * SIDE + col, pl.ds(c * SUB + 8 * h, 8), :]
        if h == 0:
            part = part + acc[band * SIDE + col, pl.ds(2 * SUB + 8 * c, 8), :]
        return part

    def copy_out(band):
        rows = pl.ds(band * SUB, SUB)
        return pltpu.make_async_copy(stage.at[:, rows, :], out.at[:, rows, :], out_sems.at[band])

    def fold(pair, carry):
        for c in range(2):
            edge = jnp.zeros((8, ROWS), f32)
            for half in range(2):
                band = pair * 2 + half
                for h in range(8):
                    before = jnp.zeros((8, ROWS), f32)
                    for t in range(TILE // ROWS):
                        even = rows_of(c, h, band, 2 * t)
                        odd = rows_of(c, h, band, 2 * t + 1)
                        stage[c, pl.ds(band * SUB + 8 * h, 8), pl.ds(t * ROWS, ROWS)] = even + jnp.where(
                            lane < SUB, before, odd
                        )
                        before = odd
                    k = half * 8 + h
                    moved = pltpu.roll(before, 8 * k, 1) if k else before
                    edge = jnp.where((lane >> 3) == k, moved, edge)
            right[c, pair] = edge
        for half in range(2):
            copy_out(pair * 2 + half).start()
        return carry

    lax.fori_loop(0, SIDE // 2, fold, 0)
    if with_low:
        for c in range(2):
            before = jnp.zeros((8, ROWS), f32)
            for t in range(TILE // ROWS):
                rows = pl.ds(2 * SUB + 8 * c, 8)
                even = acc[FIRST + (SIDE - 1) * SIDE + 2 * t, rows, :]
                odd = acc[FIRST + (SIDE - 1) * SIDE + 2 * t + 1, rows, :]
                low[c, :, pl.ds(t * ROWS, ROWS)] = even + jnp.where(lane < SUB, before, odd)
                before = odd
            low[c, :, pl.ds(TILE, ROWS)] = jnp.where(lane < KW, before, 0.0)

    def finish(band, carry):
        copy_out(band).wait()
        return carry

    lax.fori_loop(0, SIDE, finish, 0)


def edge_kernel(edge, grid_in, grid_out, columns, in_sems, out_sems):
    lane = lanes((8, ROWS))
    pairs = SIDE // 2

    def fetch(pair):
        rows = pl.ds(pair * 2 * SUB, 2 * SUB)
        return pltpu.make_async_copy(
            grid_in.at[:, rows, pl.ds(0, ROWS)], columns.at[:, rows, :], in_sems.at[pair]
        )

    def put(pair):
        rows = pl.ds(pair * 2 * SUB, 2 * SUB)
        return pltpu.make_async_copy(
            columns.at[:, rows, :], grid_out.at[:, rows, pl.ds(0, ROWS)], out_sems.at[pair]
        )

    for pair in range(pairs):
        fetch(pair).start()

    def add(pair, carry):
        fetch(pair).wait()
        for c in range(2):
            packed = edge[c, pair]
            for k in range(16):
                moved = pltpu.roll(packed, ROWS - 8 * k, 1) if k else packed
                rows = pl.ds(pair * 2 * SUB + 8 * k, 8)
                columns[c, rows, :] += jnp.where(lane < KW, moved, 0.0)
        put(pair).start()
        return carry

    lax.fori_loop(0, pairs, add, 0)
    for pair in range(pairs):
        put(pair).wait()


def shifted(block, axis, distance):
    devices = range(lax.axis_size(axis))
    route = [(i - distance, i) for i in devices if i - distance in devices]
    return lax.ppermute(block, axis, route)


def shards(visibilities, vis_weight, cell_index, tap_offsets, routes, patch_index, kernel):
    blocks = visibilities.shape[0]
    tile_count = lax.axis_size("tile")
    plane_count = lax.axis_size("wp")
    peers = tile_count * plane_count
    cap = max(2, 2 * blocks // peers)
    rows = 3 * cap + 1
    vmem = pl.BlockSpec(memory_space=pltpu.VMEM)
    smem = pl.BlockSpec(memory_space=pltpu.SMEM)
    hbm = pl.BlockSpec(memory_space=pl.ANY)

    buckets = pl.pallas_call(
        functools.partial(pack_kernel, peers, cap),
        out_shape=jax.ShapeDtypeStruct((peers * rows, 1, ROWS), f32),
        in_specs=[hbm] * 6,
        out_specs=vmem,
        scratch_shapes=[
            pltpu.SMEM((blocks,), jnp.int32),
            pltpu.SMEM((blocks,), jnp.int32),
            pltpu.VMEM((blocks, 2, ROWS), f32),
            pltpu.VMEM((blocks, ROWS), f32),
            pltpu.VMEM((blocks, ROWS), jnp.int32),
            pltpu.VMEM((blocks, ROWS), jnp.int32),
            pltpu.SMEM((peers, ROWS), jnp.int32),
            pltpu.VMEM((peers, ROWS), jnp.int32),
            pltpu.SMEM((blocks,), jnp.int32),
            pltpu.SemaphoreType.DMA((7,)),
        ],
        compiler_params=pltpu.CompilerParams(vmem_limit_bytes=60 << 20),
        name="pack",
    )(routes[:, 0], patch_index, visibilities, vis_weight, cell_index, tap_offsets)

    arrived = lax.all_to_all(buckets, ("tile", "wp"), split_axis=0, concat_axis=0, tiled=True)

    with_low = tile_count > TCOLS
    out_shape = [
        jax.ShapeDtypeStruct((2, TILE, TILE), f32),
        jax.ShapeDtypeStruct((2, SIDE // 2, 8, ROWS), f32),
    ]
    out_specs = [hbm, vmem]
    if with_low:
        out_shape.append(jax.ShapeDtypeStruct((2, KW, TILE + ROWS), f32))
        out_specs.append(vmem)
    results = pl.pallas_call(
        functools.partial(grid_kernel, peers, cap, with_low),
        out_shape=out_shape,
        in_specs=[smem, vmem],
        out_specs=out_specs,
        scratch_shapes=[
            pltpu.VMEM((-(-DUMMY // peers) * peers + 1, ROW_BLOCK, ROWS), f32),
            pltpu.VMEM((2, TILE, TILE), f32),
            pltpu.VMEM((peers, ROWS), jnp.int32),
            pltpu.SMEM((peers, ROWS), jnp.int32),
            pltpu.SMEM((peers * cap + max(cap, UNROLL),), jnp.int32),
            pltpu.SemaphoreType.DMA,
            pltpu.SemaphoreType.DMA((SIDE,)),
        ],
        compiler_params=pltpu.CompilerParams(vmem_limit_bytes=48 << 20),
        name="grid",
    )(kernel.T, arrived)
    own, right = results[0], results[1]

    place = lax.axis_index("tile")
    from_left = shifted(right, "tile", 1)
    if with_low:
        from_left = jnp.where(place % TCOLS == 0, 0.0, from_left)
    own = pl.pallas_call(
        edge_kernel,
        out_shape=jax.ShapeDtypeStruct((2, TILE, TILE), f32),
        in_specs=[vmem, hbm],
        out_specs=hbm,
        scratch_shapes=[
            pltpu.VMEM((2, TILE, ROWS), f32),
            pltpu.SemaphoreType.DMA((SIDE // 2,)),
            pltpu.SemaphoreType.DMA((SIDE // 2,)),
        ],
        input_output_aliases={1: 0},
        compiler_params=pltpu.CompilerParams(vmem_limit_bytes=16 << 20),
        name="edges",
    )(from_left, own)
    if with_low:
        low = results[2]
        from_above = shifted(low, "tile", TCOLS)
        from_corner = shifted(low[:, :, TILE:], "tile", TCOLS + 1)
        from_corner = jnp.where(place % TCOLS == 0, 0.0, from_corner)
        own = own.at[:, :KW, :].add(from_above[:, :, :TILE])
        own = own.at[:, :KW, :ROWS].add(from_corner)
    return own.reshape(1, 1, 2, TILE, TILE)


def solution(mesh):
    in_specs = (
        P(("tile", "wp"), None, None),
        P(("tile", "wp"), None),
        P(("tile", "wp"), None),
        P(("tile", "wp"), None),
        P(("tile", "wp"), None),
        P(("tile", "wp")),
        P(),
    )
    out_specs = P("wp", "tile", None, None, None)
    return jax.shard_map(shards, mesh=mesh, in_specs=in_specs, out_specs=out_specs, check_vma=False)
```

```python
import functools

import jax
import jax.numpy as jnp
from jax import lax
from jax.experimental import pallas as pl
from jax.experimental.pallas import tpu as pltpu
from jax.sharding import PartitionSpec as P

TCOLS = 8
SUB = 64
KW = 8
OVER = 16
TILE = 1024
ROWS = 128
SIDE = TILE // SUB
PATCHES = SIDE * SIDE
ROW_BLOCK = 2 * (SUB + KW)
FIRST = SIDE
DUMMY = FIRST + PATCHES
UNROLL = 32

f32 = jnp.float32
bf16 = jnp.bfloat16


def lanes(shape):
    return lax.broadcasted_iota(jnp.int32, shape, len(shape) - 1)


def pack_kernel(peers, cap, routes, patch, vis, weight, cell, tap, out, *scratch):
    routes_s, patch_s, vis_v, weight_v, cell_v, tap_v, meta, meta_v, place, sems = scratch
    blocks = vis.shape[0]
    rows = 3 * cap + 1
    sources = (routes, patch, vis, weight, cell, tap)
    targets = (routes_s, patch_s, vis_v, weight_v, cell_v, tap_v)
    copies = [pltpu.make_async_copy(a, b, sems.at[i]) for i, (a, b) in enumerate(zip(sources, targets))]
    for copy in copies:
        copy.start()

    def clear(d, carry):
        meta[d, cap] = 0
        return carry

    lax.fori_loop(0, peers, clear, 0, unroll=8)
    copies[0].wait()
    copies[1].wait()

    def choose(b, carry):
        d = routes_s[b]
        k = meta[d, cap]
        meta[d, cap] = k + 1
        meta[d, k] = patch_s[b]
        place[b] = d * rows + 3 * k
        return carry

    lax.fori_loop(0, blocks, choose, 0, unroll=8)
    meta_copy = pltpu.make_async_copy(meta, meta_v, sems.at[6])
    meta_copy.start()
    for copy in copies[2:]:
        copy.wait()

    def move(step, carry):
        first = pl.multiple_of(step * 8, 8)
        block_rows = pl.ds(first, 8)
        w = weight_v[block_rows, :]
        c = cell_v[block_rows, :]
        t = tap_v[block_rows, :]
        at_u = ((t >> 4) << 3) | ((c >> 6) & 7)
        at_v = ((t & 15) << 3) | (c & 7)
        code = (((c >> 9) << 17) | (((c >> 3) & 7) << 14) | (at_u << 7) | at_v).astype(f32)
        for i in range(8):
            row = place[first + i]
            both = vis_v[first + i] * w[i : i + 1, :]
            out[row] = both[0:1, :]
            out[row + 1] = both[1:2, :]
            out[row + 2] = code[i : i + 1, :]
        return carry

    lax.fori_loop(0, blocks // 8, move, 0)
    meta_copy.wait()

    def put_meta(d, carry):
        out[d * rows + 3 * cap] = meta_v[pl.ds(d, 1), :].astype(f32)
        return carry

    lax.fori_loop(0, peers, put_meta, 0, unroll=8)


def split(x):
    hi = x.astype(bf16)
    return hi, (x - hi.astype(f32)).astype(bf16)


def twice(x):
    return jnp.concatenate([x, x], axis=0)


def look_up(table, index):
    numbers = lax.GatherDimensionNumbers(
        offset_dims=(),
        collapsed_slice_dims=(1,),
        start_index_map=(1,),
        operand_batching_dims=(0,),
        start_indices_batching_dims=(0,),
    )
    return lax.gather(
        table, index[..., None], numbers, (1, 1), mode=lax.GatherScatterMode.PROMISE_IN_BOUNDS
    )


def spread(picks, values):
    zero = jnp.zeros((16, ROWS), bf16)
    return [[jnp.where(pick, value, zero) for pick in picks] for value in values]


def patch_product(re, im, code, parity, table):
    sub = lax.broadcasted_iota(jnp.int32, (8, ROWS), 0)
    at_v = code & 127
    at_u = (code >> 7) & 127
    ku = look_up(table, at_u)
    kv = look_up(table, at_v)
    group_u = ((code >> 17) & 7) + jnp.where(sub < (at_u & 7), 1, 0)
    group_v = ((code >> 14) & 7) + jnp.where(sub < (at_v & 7), 1, 0) + 8 * parity
    step_u = twice(group_u.astype(f32)).astype(bf16)
    step_v = jnp.concatenate([group_v & 15, (group_v + 15) & 15], axis=0).astype(f32).astype(bf16)

    u_hi, u_lo = split(jnp.concatenate([re * ku, im * ku], axis=0))
    hi_rows, lo_rows = spread([step_u == float(g) for g in range(SUB // 8 + 1)], [u_hi, u_lo])
    left_hi, left_lo = jnp.concatenate(hi_rows, axis=0), jnp.concatenate(lo_rows, axis=0)
    left = jnp.concatenate([left_hi, left_lo, left_hi], axis=1)

    v_hi, v_lo = split(twice(kv))
    hi_rows, lo_rows = spread([step_v == 2.0 * g for g in range(ROWS // 16)], [v_hi, v_lo])
    right_hi, right_lo = jnp.concatenate(hi_rows, axis=0), jnp.concatenate(lo_rows, axis=0)
    right = jnp.concatenate([right_hi, right_hi, right_lo], axis=1)
    return lax.dot_general(left, right, (((1,), (1,)), ((), ())), preferred_element_type=f32)


def tap_table(kernel):
    sub = lax.broadcasted_iota(jnp.int32, (8, ROWS), 0)
    lane = lanes((8, ROWS))
    which_tap = (sub - lane) & 7
    which_level = lane >> 3
    table = jnp.zeros((8, ROWS), f32)
    for a in range(KW):
        row = jnp.zeros((8, ROWS), f32)
        for o in range(OVER):
            row = jnp.where(which_level == o, kernel[a, o], row)
        table = jnp.where(which_tap == a, row, table)
    return table


def grid_kernel(peers, cap, with_low, kernel, arrived, out, right, first, *rest):
    low, rest = (rest[0], rest[1:]) if with_low else (None, rest)
    acc, stage, meta_v, meta, slots, meta_sem, out_sems = rest
    rows = 3 * cap + 1
    lane_row = lanes((1, ROWS))

    def entries(s, carry):
        row = arrived[s * rows + 3 * cap].astype(jnp.int32)
        entry = (s * rows + 3 * lane_row) * 512 + (row + FIRST)
        meta_v[pl.ds(s, 1), :] = jnp.where(lane_row < cap, entry, row)
        return carry

    lax.fori_loop(0, peers, entries, 0, unroll=8)
    meta_copy = pltpu.make_async_copy(meta_v, meta, meta_sem)
    meta_copy.start()
    table = tap_table(kernel)
    meta_copy.wait()
    share = (DUMMY + peers - 1) // peers

    def prepare(s, total):
        for k in range(cap):
            slots[total + k] = meta[s, k]
        for i in range(share):
            acc[s * share + i] = jnp.zeros((ROW_BLOCK, ROWS), f32)
        return total + meta[s, cap]

    total = lax.fori_loop(0, peers, prepare, 0)
    for k in range(UNROLL):
        slots[total + k] = DUMMY

    def work(step, carry):
        for i in range(UNROLL):
            entry = slots[step * UNROLL + i]
            row = entry >> 9
            where_to = entry & 511
            re = jnp.broadcast_to(arrived[row], (8, ROWS))
            im = jnp.broadcast_to(arrived[row + 1], (8, ROWS))
            code = jnp.broadcast_to(arrived[row + 2], (8, ROWS)).astype(jnp.int32)
            acc[where_to] += patch_product(re, im, code, entry & 1, table)
        return carry

    lax.fori_loop(0, (total + UNROLL - 1) // UNROLL, work, 0)

    lane = lanes((8, ROWS))

    def rows_of(c, h, band, col):
        part = acc[FIRST + band * SIDE + col, pl.ds(16 * h + 8 * c, 8), :]
        if h == 0:
            part = part + acc[band * SIDE + col, pl.ds(2 * SUB + 8 * c, 8), :]
        return part

    def copy_out(band):
        rows = pl.ds(band * SUB, SUB)
        return pltpu.make_async_copy(
            stage.at[:, rows, :], out.at[:, rows, pl.ds(ROWS, TILE - ROWS)], out_sems.at[band]
        )

    def fold(pair, carry):
        for c in range(2):
            edge = jnp.zeros((8, ROWS), f32)
            for half in range(2):
                band = pair * 2 + half
                for h in range(8):
                    before = jnp.zeros((8, ROWS), f32)
                    for t in range(TILE // ROWS):
                        even = rows_of(c, h, band, 2 * t)
                        odd = rows_of(c, h, band, 2 * t + 1)
                        rows = pl.ds(band * SUB + 8 * h, 8)
                        columns = even + jnp.where(lane < SUB, before, odd)
                        if t == 0:
                            first[c, rows, :] = columns
                        else:
                            stage[c, rows, pl.ds((t - 1) * ROWS, ROWS)] = columns
                        before = odd
                    k = half * 8 + h
                    moved = pltpu.roll(before, 8 * k, 1) if k else before
                    edge = jnp.where((lane >> 3) == k, moved, edge)
            right[c, pair] = edge
        for half in range(2):
            copy_out(pair * 2 + half).start()
        return carry

    lax.fori_loop(0, SIDE // 2, fold, 0)
    if with_low:
        for c in range(2):
            before = jnp.zeros((8, ROWS), f32)
            for t in range(TILE // ROWS):
                rows = pl.ds(2 * SUB + 8 * c, 8)
                even = acc[FIRST + (SIDE - 1) * SIDE + 2 * t, rows, :]
                odd = acc[FIRST + (SIDE - 1) * SIDE + 2 * t + 1, rows, :]
                low[c, :, pl.ds(t * ROWS, ROWS)] = even + jnp.where(lane < SUB, before, odd)
                before = odd
            low[c, :, pl.ds(TILE, ROWS)] = jnp.where(lane < KW, before, 0.0)

    def finish(band, carry):
        copy_out(band).wait()
        return carry

    lax.fori_loop(0, SIDE, finish, 0)


def edge_kernel(edge, first, grid_in, grid_out, columns, out_sems):
    lane = lanes((8, ROWS))
    pairs = SIDE // 2

    def put(pair):
        rows = pl.ds(pair * 2 * SUB, 2 * SUB)
        return pltpu.make_async_copy(
            columns.at[:, rows, :], grid_out.at[:, rows, pl.ds(0, ROWS)], out_sems.at[pair]
        )

    def add(pair, carry):
        for c in range(2):
            packed = edge[c, pair]
            for k in range(16):
                moved = pltpu.roll(packed, ROWS - 8 * k, 1) if k else packed
                rows = pl.ds(pair * 2 * SUB + 8 * k, 8)
                columns[c, rows, :] = first[c, rows, :] + jnp.where(lane < KW, moved, 0.0)
        put(pair).start()
        return carry

    lax.fori_loop(0, pairs, add, 0)
    for pair in range(pairs):
        put(pair).wait()


def shifted(block, axis, distance):
    devices = range(lax.axis_size(axis))
    route = [(i - distance, i) for i in devices if i - distance in devices]
    return lax.ppermute(block, axis, route)


def shards(visibilities, vis_weight, cell_index, tap_offsets, routes, patch_index, kernel):
    blocks = visibilities.shape[0]
    tile_count = lax.axis_size("tile")
    plane_count = lax.axis_size("wp")
    peers = tile_count * plane_count
    cap = max(2, 2 * blocks // peers)
    rows = 3 * cap + 1
    vmem = pl.BlockSpec(memory_space=pltpu.VMEM)
    smem = pl.BlockSpec(memory_space=pltpu.SMEM)
    hbm = pl.BlockSpec(memory_space=pl.ANY)

    buckets = pl.pallas_call(
        functools.partial(pack_kernel, peers, cap),
        out_shape=jax.ShapeDtypeStruct((peers * rows, 1, ROWS), f32),
        in_specs=[hbm] * 6,
        out_specs=vmem,
        scratch_shapes=[
            pltpu.SMEM((blocks,), jnp.int32),
            pltpu.SMEM((blocks,), jnp.int32),
            pltpu.VMEM((blocks, 2, ROWS), f32),
            pltpu.VMEM((blocks, ROWS), f32),
            pltpu.VMEM((blocks, ROWS), jnp.int32),
            pltpu.VMEM((blocks, ROWS), jnp.int32),
            pltpu.SMEM((peers, ROWS), jnp.int32),
            pltpu.VMEM((peers, ROWS), jnp.int32),
            pltpu.SMEM((blocks,), jnp.int32),
            pltpu.SemaphoreType.DMA((7,)),
        ],
        compiler_params=pltpu.CompilerParams(vmem_limit_bytes=60 << 20),
        name="pack",
    )(routes[:, 0], patch_index, visibilities, vis_weight, cell_index, tap_offsets)

    arrived = lax.all_to_all(buckets, ("tile", "wp"), split_axis=0, concat_axis=0, tiled=True)

    with_low = tile_count > TCOLS
    out_shape = [
        jax.ShapeDtypeStruct((2, TILE, TILE), f32),
        jax.ShapeDtypeStruct((2, SIDE // 2, 8, ROWS), f32),
        jax.ShapeDtypeStruct((2, TILE, ROWS), f32),
    ]
    out_specs = [hbm, vmem, vmem]
    if with_low:
        out_shape.append(jax.ShapeDtypeStruct((2, KW, TILE + ROWS), f32))
        out_specs.append(vmem)
    results = pl.pallas_call(
        functools.partial(grid_kernel, peers, cap, with_low),
        out_shape=out_shape,
        in_specs=[smem, vmem],
        out_specs=out_specs,
        scratch_shapes=[
            pltpu.VMEM((-(-DUMMY // peers) * peers + 1, ROW_BLOCK, ROWS), f32),
            pltpu.VMEM((2, TILE, TILE - ROWS), f32),
            pltpu.VMEM((peers, ROWS), jnp.int32),
            pltpu.SMEM((peers, ROWS), jnp.int32),
            pltpu.SMEM((peers * cap + max(cap, UNROLL),), jnp.int32),
            pltpu.SemaphoreType.DMA,
            pltpu.SemaphoreType.DMA((SIDE,)),
        ],
        compiler_params=pltpu.CompilerParams(vmem_limit_bytes=48 << 20),
        name="grid",
    )(kernel.T, arrived)
    own, right, first = results[:3]

    place = lax.axis_index("tile")
    from_left = shifted(right, "tile", 1)
    if with_low:
        from_left = jnp.where(place % TCOLS == 0, 0.0, from_left)
    own = pl.pallas_call(
        edge_kernel,
        out_shape=jax.ShapeDtypeStruct((2, TILE, TILE), f32),
        in_specs=[vmem, vmem, hbm],
        out_specs=hbm,
        scratch_shapes=[
            pltpu.VMEM((2, TILE, ROWS), f32),
            pltpu.SemaphoreType.DMA((SIDE // 2,)),
        ],
        input_output_aliases={2: 0},
        compiler_params=pltpu.CompilerParams(vmem_limit_bytes=16 << 20),
        name="edges",
    )(from_left, first, own)
    if with_low:
        low = results[3]
        from_above = shifted(low, "tile", TCOLS)
        from_corner = shifted(low[:, :, TILE:], "tile", TCOLS + 1)
        from_corner = jnp.where(place % TCOLS == 0, 0.0, from_corner)
        own = own.at[:, :KW, :].add(from_above[:, :, :TILE])
        own = own.at[:, :KW, :ROWS].add(from_corner)
    return own.reshape(1, 1, 2, TILE, TILE)


def solution(mesh):
    in_specs = (
        P(("tile", "wp"), None, None),
        P(("tile", "wp"), None),
        P(("tile", "wp"), None),
        P(("tile", "wp"), None),
        P(("tile", "wp"), None),
        P(("tile", "wp")),
        P(),
    )
    out_specs = P("wp", "tile", None, None, None)
    return jax.shard_map(shards, mesh=mesh, in_specs=in_specs, out_specs=out_specs, check_vma=False)
```

```python
import functools

import jax
import jax.numpy as jnp
from jax import lax
from jax.experimental import pallas as pl
from jax.experimental.pallas import tpu as pltpu
from jax.sharding import PartitionSpec as P

TCOLS = 8
SUB = 64
KW = 8
OVER = 16
TILE = 1024
ROWS = 128
SIDE = TILE // SUB
PATCHES = SIDE * SIDE
ROW_BLOCK = 2 * (SUB + KW)
FIRST = SIDE
DUMMY = FIRST + PATCHES
UNROLL = 32

f32 = jnp.float32
bf16 = jnp.bfloat16


def lanes(shape):
    return lax.broadcasted_iota(jnp.int32, shape, len(shape) - 1)


def pack_kernel(peers, cap, routes, patch, vis, weight, cell, tap, out, *scratch):
    routes_s, patch_s, vis_v, weight_v, cell_v, tap_v, meta, meta_v, place, sems = scratch
    blocks = vis.shape[0]
    rows = 3 * cap + 1
    sources = (routes, patch, vis, weight, cell, tap)
    targets = (routes_s, patch_s, vis_v, weight_v, cell_v, tap_v)
    copies = [pltpu.make_async_copy(a, b, sems.at[i]) for i, (a, b) in enumerate(zip(sources, targets))]
    for copy in copies:
        copy.start()

    def clear(d, carry):
        meta[d, cap] = 0
        return carry

    lax.fori_loop(0, peers, clear, 0, unroll=8)
    copies[0].wait()
    copies[1].wait()

    def choose(b, carry):
        d = routes_s[b]
        k = meta[d, cap]
        meta[d, cap] = k + 1
        meta[d, k] = patch_s[b]
        place[b] = d * rows + 3 * k
        return carry

    lax.fori_loop(0, blocks, choose, 0, unroll=8)
    meta_copy = pltpu.make_async_copy(meta, meta_v, sems.at[6])
    meta_copy.start()
    for copy in copies[2:]:
        copy.wait()

    def move(step, carry):
        first = pl.multiple_of(step * 8, 8)
        block_rows = pl.ds(first, 8)
        w = weight_v[block_rows, :]
        c = cell_v[block_rows, :]
        t = tap_v[block_rows, :]
        at_u = ((t >> 4) << 3) | ((c >> 6) & 7)
        at_v = ((t & 15) << 3) | (c & 7)
        code = (((c >> 9) << 17) | (((c >> 3) & 7) << 14) | (at_u << 7) | at_v).astype(f32)
        for i in range(8):
            row = place[first + i]
            both = vis_v[first + i] * w[i : i + 1, :]
            out[row] = both[0:1, :]
            out[row + 1] = both[1:2, :]
            out[row + 2] = code[i : i + 1, :]
        return carry

    lax.fori_loop(0, blocks // 8, move, 0)
    meta_copy.wait()

    def put_meta(d, carry):
        out[d * rows + 3 * cap] = meta_v[pl.ds(d, 1), :].astype(f32)
        return carry

    lax.fori_loop(0, peers, put_meta, 0, unroll=8)


def split(x):
    hi = x.astype(bf16)
    return hi, (x - hi.astype(f32)).astype(bf16)


def twice(x):
    return jnp.concatenate([x, x], axis=0)


def look_up(table, index):
    numbers = lax.GatherDimensionNumbers(
        offset_dims=(),
        collapsed_slice_dims=(1,),
        start_index_map=(1,),
        operand_batching_dims=(0,),
        start_indices_batching_dims=(0,),
    )
    return lax.gather(
        table, index[..., None], numbers, (1, 1), mode=lax.GatherScatterMode.PROMISE_IN_BOUNDS
    )


def spread(picks, values):
    zero = jnp.zeros((16, ROWS), bf16)
    return [[jnp.where(pick, value, zero) for pick in picks] for value in values]


def patch_product(re, im, code, parity, table):
    sub = lax.broadcasted_iota(jnp.int32, (8, ROWS), 0)
    at_v = code & 127
    at_u = (code >> 7) & 127
    ku = look_up(table, at_u)
    kv = look_up(table, at_v)
    group_u = ((code >> 17) & 7) + jnp.where(sub < (at_u & 7), 1, 0)
    group_v = ((code >> 14) & 7) + jnp.where(sub < (at_v & 7), 1, 0) + 8 * parity
    step_u = twice(group_u.astype(f32)).astype(bf16)
    step_v = jnp.concatenate([group_v & 15, (group_v + 15) & 15], axis=0).astype(f32).astype(bf16)

    u_hi, u_lo = split(jnp.concatenate([re * ku, im * ku], axis=0))
    hi_rows, lo_rows = spread([step_u == float(g) for g in range(SUB // 8 + 1)], [u_hi, u_lo])
    left_hi, left_lo = jnp.concatenate(hi_rows, axis=0), jnp.concatenate(lo_rows, axis=0)
    left = jnp.concatenate([left_hi, left_lo], axis=1)

    v_hi, v_lo = split(twice(kv))
    hi_rows, lo_rows = spread([step_v == 2.0 * g for g in range(ROWS // 16)], [v_hi, v_lo])
    right = jnp.concatenate([jnp.concatenate(hi_rows, axis=0).T, jnp.concatenate(lo_rows, axis=0).T], axis=1)
    product = jnp.dot(left, twice(right), preferred_element_type=f32)
    return product[:, :ROWS] + product[:, ROWS:]


def tap_table(kernel):
    sub = lax.broadcasted_iota(jnp.int32, (8, ROWS), 0)
    lane = lanes((8, ROWS))
    which_tap = (sub - lane) & 7
    which_level = lane >> 3
    table = jnp.zeros((8, ROWS), f32)
    for a in range(KW):
        row = jnp.zeros((8, ROWS), f32)
        for o in range(OVER):
            row = jnp.where(which_level == o, kernel[a, o], row)
        table = jnp.where(which_tap == a, row, table)
    return table


def grid_kernel(peers, cap, with_low, kernel, arrived, out, right, first, *rest):
    low, rest = (rest[0], rest[1:]) if with_low else (None, rest)
    acc, stage, meta_v, meta, slots, meta_sem, out_sems = rest
    rows = 3 * cap + 1
    lane_row = lanes((1, ROWS))

    def entries(s, carry):
        row = arrived[s * rows + 3 * cap].astype(jnp.int32)
        entry = (s * rows + 3 * lane_row) * 512 + (row + FIRST)
        meta_v[pl.ds(s, 1), :] = jnp.where(lane_row < cap, entry, row)
        return carry

    lax.fori_loop(0, peers, entries, 0, unroll=8)
    meta_copy = pltpu.make_async_copy(meta_v, meta, meta_sem)
    meta_copy.start()
    table = tap_table(kernel)
    meta_copy.wait()
    share = (DUMMY + peers - 1) // peers

    def prepare(s, total):
        for k in range(cap):
            slots[total + k] = meta[s, k]
        for i in range(share):
            acc[s * share + i] = jnp.zeros((ROW_BLOCK, ROWS), f32)
        return total + meta[s, cap]

    total = lax.fori_loop(0, peers, prepare, 0)
    for k in range(UNROLL):
        slots[total + k] = DUMMY

    def work(step, carry):
        for i in range(UNROLL):
            entry = slots[step * UNROLL + i]
            row = entry >> 9
            where_to = entry & 511
            re = jnp.broadcast_to(arrived[row], (8, ROWS))
            im = jnp.broadcast_to(arrived[row + 1], (8, ROWS))
            code = jnp.broadcast_to(arrived[row + 2], (8, ROWS)).astype(jnp.int32)
            acc[where_to] += patch_product(re, im, code, entry & 1, table)
        return carry

    lax.fori_loop(0, (total + UNROLL - 1) // UNROLL, work, 0)

    lane = lanes((8, ROWS))

    def rows_of(c, h, band, col):
        part = acc[FIRST + band * SIDE + col, pl.ds(16 * h + 8 * c, 8), :]
        if h == 0:
            part = part + acc[band * SIDE + col, pl.ds(2 * SUB + 8 * c, 8), :]
        return part

    def copy_out(band):
        rows = pl.ds(band * SUB, SUB)
        return pltpu.make_async_copy(
            stage.at[:, rows, :], out.at[:, rows, pl.ds(ROWS, TILE - ROWS)], out_sems.at[band]
        )

    def fold(pair, carry):
        for c in range(2):
            edge = jnp.zeros((8, ROWS), f32)
            for half in range(2):
                band = pair * 2 + half
                for h in range(8):
                    before = jnp.zeros((8, ROWS), f32)
                    for t in range(TILE // ROWS):
                        even = rows_of(c, h, band, 2 * t)
                        odd = rows_of(c, h, band, 2 * t + 1)
                        rows = pl.ds(band * SUB + 8 * h, 8)
                        columns = even + jnp.where(lane < SUB, before, odd)
                        if t == 0:
                            first[c, rows, :] = columns
                        else:
                            stage[c, rows, pl.ds((t - 1) * ROWS, ROWS)] = columns
                        before = odd
                    k = half * 8 + h
                    moved = pltpu.roll(before, 8 * k, 1) if k else before
                    edge = jnp.where((lane >> 3) == k, moved, edge)
            right[c, pair] = edge
        for half in range(2):
            copy_out(pair * 2 + half).start()
        return carry

    lax.fori_loop(0, SIDE // 2, fold, 0)
    if with_low:
        for c in range(2):
            before = jnp.zeros((8, ROWS), f32)
            for t in range(TILE // ROWS):
                rows = pl.ds(2 * SUB + 8 * c, 8)
                even = acc[FIRST + (SIDE - 1) * SIDE + 2 * t, rows, :]
                odd = acc[FIRST + (SIDE - 1) * SIDE + 2 * t + 1, rows, :]
                low[c, :, pl.ds(t * ROWS, ROWS)] = even + jnp.where(lane < SUB, before, odd)
                before = odd
            low[c, :, pl.ds(TILE, ROWS)] = jnp.where(lane < KW, before, 0.0)

    def finish(band, carry):
        copy_out(band).wait()
        return carry

    lax.fori_loop(0, SIDE, finish, 0)


def edge_kernel(edge, first, grid_in, grid_out, columns, out_sems):
    lane = lanes((8, ROWS))
    pairs = SIDE // 2

    def put(pair):
        rows = pl.ds(pair * 2 * SUB, 2 * SUB)
        return pltpu.make_async_copy(
            columns.at[:, rows, :], grid_out.at[:, rows, pl.ds(0, ROWS)], out_sems.at[pair]
        )

    def add(pair, carry):
        for c in range(2):
            packed = edge[c, pair]
            for k in range(16):
                moved = pltpu.roll(packed, ROWS - 8 * k, 1) if k else packed
                rows = pl.ds(pair * 2 * SUB + 8 * k, 8)
                columns[c, rows, :] = first[c, rows, :] + jnp.where(lane < KW, moved, 0.0)
        put(pair).start()
        return carry

    lax.fori_loop(0, pairs, add, 0)
    for pair in range(pairs):
        put(pair).wait()


def shifted(block, axis, distance):
    devices = range(lax.axis_size(axis))
    route = [(i - distance, i) for i in devices if i - distance in devices]
    return lax.ppermute(block, axis, route)


def shards(visibilities, vis_weight, cell_index, tap_offsets, routes, patch_index, kernel):
    blocks = visibilities.shape[0]
    tile_count = lax.axis_size("tile")
    plane_count = lax.axis_size("wp")
    peers = tile_count * plane_count
    cap = max(2, 2 * blocks // peers)
    rows = 3 * cap + 1
    vmem = pl.BlockSpec(memory_space=pltpu.VMEM)
    smem = pl.BlockSpec(memory_space=pltpu.SMEM)
    hbm = pl.BlockSpec(memory_space=pl.ANY)

    buckets = pl.pallas_call(
        functools.partial(pack_kernel, peers, cap),
        out_shape=jax.ShapeDtypeStruct((peers * rows, 1, ROWS), f32),
        in_specs=[hbm] * 6,
        out_specs=vmem,
        scratch_shapes=[
            pltpu.SMEM((blocks,), jnp.int32),
            pltpu.SMEM((blocks,), jnp.int32),
            pltpu.VMEM((blocks, 2, ROWS), f32),
            pltpu.VMEM((blocks, ROWS), f32),
            pltpu.VMEM((blocks, ROWS), jnp.int32),
            pltpu.VMEM((blocks, ROWS), jnp.int32),
            pltpu.SMEM((peers, ROWS), jnp.int32),
            pltpu.VMEM((peers, ROWS), jnp.int32),
            pltpu.SMEM((blocks,), jnp.int32),
            pltpu.SemaphoreType.DMA((7,)),
        ],
        compiler_params=pltpu.CompilerParams(vmem_limit_bytes=60 << 20),
        name="pack",
    )(routes[:, 0], patch_index, visibilities, vis_weight, cell_index, tap_offsets)

    arrived = lax.all_to_all(buckets, ("tile", "wp"), split_axis=0, concat_axis=0, tiled=True)

    with_low = tile_count > TCOLS
    out_shape = [
        jax.ShapeDtypeStruct((2, TILE, TILE), f32),
        jax.ShapeDtypeStruct((2, SIDE // 2, 8, ROWS), f32),
        jax.ShapeDtypeStruct((2, TILE, ROWS), f32),
    ]
    out_specs = [hbm, vmem, vmem]
    if with_low:
        out_shape.append(jax.ShapeDtypeStruct((2, KW, TILE + ROWS), f32))
        out_specs.append(vmem)
    results = pl.pallas_call(
        functools.partial(grid_kernel, peers, cap, with_low),
        out_shape=out_shape,
        in_specs=[smem, vmem],
        out_specs=out_specs,
        scratch_shapes=[
            pltpu.VMEM((-(-DUMMY // peers) * peers + 1, ROW_BLOCK, ROWS), f32),
            pltpu.VMEM((2, TILE, TILE - ROWS), f32),
            pltpu.VMEM((peers, ROWS), jnp.int32),
            pltpu.SMEM((peers, ROWS), jnp.int32),
            pltpu.SMEM((peers * cap + max(cap, UNROLL),), jnp.int32),
            pltpu.SemaphoreType.DMA,
            pltpu.SemaphoreType.DMA((SIDE,)),
        ],
        compiler_params=pltpu.CompilerParams(vmem_limit_bytes=48 << 20),
        name="grid",
    )(kernel.T, arrived)
    own, right, first = results[:3]

    place = lax.axis_index("tile")
    from_left = shifted(right, "tile", 1)
    if with_low:
        from_left = jnp.where(place % TCOLS == 0, 0.0, from_left)
    own = pl.pallas_call(
        edge_kernel,
        out_shape=jax.ShapeDtypeStruct((2, TILE, TILE), f32),
        in_specs=[vmem, vmem, hbm],
        out_specs=hbm,
        scratch_shapes=[
            pltpu.VMEM((2, TILE, ROWS), f32),
            pltpu.SemaphoreType.DMA((SIDE // 2,)),
        ],
        input_output_aliases={2: 0},
        compiler_params=pltpu.CompilerParams(vmem_limit_bytes=16 << 20),
        name="edges",
    )(from_left, first, own)
    if with_low:
        low = results[3]
        from_above = shifted(low, "tile", TCOLS)
        from_corner = shifted(low[:, :, TILE:], "tile", TCOLS + 1)
        from_corner = jnp.where(place % TCOLS == 0, 0.0, from_corner)
        own = own.at[:, :KW, :].add(from_above[:, :, :TILE])
        own = own.at[:, :KW, :ROWS].add(from_corner)
    return own.reshape(1, 1, 2, TILE, TILE)


def solution(mesh):
    in_specs = (
        P(("tile", "wp"), None, None),
        P(("tile", "wp"), None),
        P(("tile", "wp"), None),
        P(("tile", "wp"), None),
        P(("tile", "wp"), None),
        P(("tile", "wp")),
        P(),
    )
    out_specs = P("wp", "tile", None, None, None)
    return jax.shard_map(shards, mesh=mesh, in_specs=in_specs, out_specs=out_specs, check_vma=False)
```

```python
import functools

import jax
import jax.numpy as jnp
from jax import lax
from jax.experimental import pallas as pl
from jax.experimental.pallas import tpu as pltpu
from jax.sharding import PartitionSpec as P

TCOLS = 8
SUB = 64
KW = 8
OVER = 16
TILE = 1024
ROWS = 128
SIDE = TILE // SUB
PATCHES = SIDE * SIDE
ROW_BLOCK = 2 * (SUB + KW)
FIRST = SIDE
DUMMY = FIRST + PATCHES
UNROLL = 32

f32 = jnp.float32
bf16 = jnp.bfloat16


def lanes(shape):
    return lax.broadcasted_iota(jnp.int32, shape, len(shape) - 1)


def pack_kernel(peers, cap, routes, patch, vis, weight, cell, tap, out, *scratch):
    routes_s, patch_s, vis_v, weight_v, cell_v, tap_v, meta, meta_v, place, sems = scratch
    blocks = vis.shape[0]
    rows = 3 * cap + 1
    sources = (routes, patch, vis, weight, cell, tap)
    targets = (routes_s, patch_s, vis_v, weight_v, cell_v, tap_v)
    copies = [pltpu.make_async_copy(a, b, sems.at[i]) for i, (a, b) in enumerate(zip(sources, targets))]
    for copy in copies:
        copy.start()

    def clear(d, carry):
        meta[d, cap] = 0
        return carry

    lax.fori_loop(0, peers, clear, 0, unroll=8)
    copies[0].wait()
    copies[1].wait()

    def choose(b, carry):
        d = routes_s[b]
        k = meta[d, cap]
        meta[d, cap] = k + 1
        meta[d, k] = patch_s[b]
        place[b] = d * rows + 3 * k
        return carry

    lax.fori_loop(0, blocks, choose, 0, unroll=8)
    meta_copy = pltpu.make_async_copy(meta, meta_v, sems.at[6])
    meta_copy.start()
    for copy in copies[2:]:
        copy.wait()

    def move(step, carry):
        first = pl.multiple_of(step * 8, 8)
        block_rows = pl.ds(first, 8)
        w = weight_v[block_rows, :]
        c = cell_v[block_rows, :]
        t = tap_v[block_rows, :]
        at_u = ((t >> 4) << 3) | ((c >> 6) & 7)
        at_v = ((t & 15) << 3) | (c & 7)
        code = (((c >> 9) << 17) | (((c >> 3) & 7) << 14) | (at_u << 7) | at_v).astype(f32)
        for i in range(8):
            row = place[first + i]
            both = vis_v[first + i] * w[i : i + 1, :]
            out[row] = both[0:1, :]
            out[row + 1] = both[1:2, :]
            out[row + 2] = code[i : i + 1, :]
        return carry

    lax.fori_loop(0, blocks // 8, move, 0)
    meta_copy.wait()

    def put_meta(d, carry):
        out[d * rows + 3 * cap] = meta_v[pl.ds(d, 1), :].astype(f32)
        return carry

    lax.fori_loop(0, peers, put_meta, 0, unroll=8)


def split(x):
    hi = x.astype(bf16)
    return hi, (x - hi.astype(f32)).astype(bf16)


def twice(x):
    return jnp.concatenate([x, x], axis=0)


def look_up(table, index):
    numbers = lax.GatherDimensionNumbers(
        offset_dims=(),
        collapsed_slice_dims=(1,),
        start_index_map=(1,),
        operand_batching_dims=(0,),
        start_indices_batching_dims=(0,),
    )
    return lax.gather(
        table, index[..., None], numbers, (1, 1), mode=lax.GatherScatterMode.PROMISE_IN_BOUNDS
    )


def spread(picks, values):
    zero = jnp.zeros((16, ROWS), bf16)
    return [[jnp.where(pick, value, zero) for pick in picks] for value in values]


def patch_product(re, im, code, parity, table):
    sub = lax.broadcasted_iota(jnp.int32, (8, ROWS), 0)
    at_v = code & 127
    at_u = (code >> 7) & 127
    ku = look_up(table, at_u)
    kv = look_up(table, at_v)
    group_u = ((code >> 17) & 7) + jnp.where(sub < (at_u & 7), 1, 0)
    group_v = ((code >> 14) & 7) + jnp.where(sub < (at_v & 7), 1, 0) + 8 * parity
    step_u = twice(group_u.astype(f32)).astype(bf16)
    step_v = jnp.concatenate([group_v & 15, (group_v + 15) & 15], axis=0).astype(f32).astype(bf16)

    u_hi, u_lo = split(jnp.concatenate([re * ku, im * ku], axis=0))
    hi_rows, lo_rows = spread([step_u == float(g) for g in range(SUB // 8 + 1)], [u_hi, u_lo])
    left_hi, left_lo = jnp.concatenate(hi_rows, axis=0), jnp.concatenate(lo_rows, axis=0)
    left = jnp.concatenate([left_hi, left_lo, left_hi], axis=1)

    v_hi, v_lo = split(twice(kv))
    hi_rows, lo_rows = spread([step_v == 2.0 * g for g in range(ROWS // 16)], [v_hi, v_lo])
    right_hi, right_lo = jnp.concatenate(hi_rows, axis=0), jnp.concatenate(lo_rows, axis=0)
    right = jnp.concatenate([right_hi, right_hi, right_lo], axis=1)
    return lax.dot_general(left, right, (((1,), (1,)), ((), ())), preferred_element_type=f32)


def tap_table(kernel):
    sub = lax.broadcasted_iota(jnp.int32, (8, ROWS), 0)
    lane = lanes((8, ROWS))
    which_tap = (sub - lane) & 7
    which_level = lane >> 3
    table = jnp.zeros((8, ROWS), f32)
    for a in range(KW):
        row = jnp.zeros((8, ROWS), f32)
        for o in range(OVER):
            row = jnp.where(which_level == o, kernel[a, o], row)
        table = jnp.where(which_tap == a, row, table)
    return table


def grid_kernel(peers, cap, with_low, kernel, arrived, out, right, first, *rest):
    low, rest = (rest[0], rest[1:]) if with_low else (None, rest)
    acc, stage, meta_v, meta, slots, kernel_s, meta_sem, kernel_sem, out_sems = rest
    rows = 3 * cap + 1
    kernel_copy = pltpu.make_async_copy(kernel, kernel_s, kernel_sem)
    kernel_copy.start()
    lane_row = lanes((1, ROWS))

    def entries(s, carry):
        row = arrived[s * rows + 3 * cap].astype(jnp.int32)
        entry = (s * rows + 3 * lane_row) * 512 + (row + FIRST)
        meta_v[pl.ds(s, 1), :] = jnp.where(lane_row < cap, entry, row)
        return carry

    lax.fori_loop(0, peers, entries, 0, unroll=8)
    meta_copy = pltpu.make_async_copy(meta_v, meta, meta_sem)
    meta_copy.start()

    def clear(i, carry):
        acc[i] = jnp.zeros((ROW_BLOCK, ROWS), f32)
        return carry

    early = DUMMY // 2
    lax.fori_loop(0, early, clear, 0)
    kernel_copy.wait()
    table = tap_table(kernel_s)
    meta_copy.wait()
    share = -(-(DUMMY - early) // peers)

    def prepare(s, total):
        for k in range(cap):
            slots[total + k] = meta[s, k]
        for i in range(share):
            acc[early + s * share + i] = jnp.zeros((ROW_BLOCK, ROWS), f32)
        return total + meta[s, cap]

    total = lax.fori_loop(0, peers, prepare, 0)
    for k in range(UNROLL):
        slots[total + k] = DUMMY

    def work(step, carry):
        for i in range(UNROLL):
            entry = slots[step * UNROLL + i]
            row = entry >> 9
            where_to = entry & 511
            re = jnp.broadcast_to(arrived[row], (8, ROWS))
            im = jnp.broadcast_to(arrived[row + 1], (8, ROWS))
            code = jnp.broadcast_to(arrived[row + 2], (8, ROWS)).astype(jnp.int32)
            acc[where_to] += patch_product(re, im, code, entry & 1, table)
        return carry

    lax.fori_loop(0, (total + UNROLL - 1) // UNROLL, work, 0)

    lane = lanes((8, ROWS))

    def rows_of(c, h, band, col):
        part = acc[FIRST + band * SIDE + col, pl.ds(16 * h + 8 * c, 8), :]
        if h == 0:
            part = part + acc[band * SIDE + col, pl.ds(2 * SUB + 8 * c, 8), :]
        return part

    def copy_out(band):
        rows = pl.ds(band * SUB, SUB)
        return pltpu.make_async_copy(
            stage.at[:, rows, :], out.at[:, rows, pl.ds(ROWS, TILE - ROWS)], out_sems.at[band]
        )

    def fold(pair, carry):
        for c in range(2):
            edge = jnp.zeros((8, ROWS), f32)
            for half in range(2):
                band = pair * 2 + half
                for h in range(8):
                    before = jnp.zeros((8, ROWS), f32)
                    for t in range(TILE // ROWS):
                        even = rows_of(c, h, band, 2 * t)
                        odd = rows_of(c, h, band, 2 * t + 1)
                        rows = pl.ds(band * SUB + 8 * h, 8)
                        columns = even + jnp.where(lane < SUB, before, odd)
                        if t == 0:
                            first[c, rows, :] = columns
                        else:
                            stage[c, rows, pl.ds((t - 1) * ROWS, ROWS)] = columns
                        before = odd
                    k = half * 8 + h
                    moved = pltpu.roll(before, 8 * k, 1) if k else before
                    edge = jnp.where((lane >> 3) == k, moved, edge)
            right[c, pair] = edge
        for half in range(2):
            copy_out(pair * 2 + half).start()
        return carry

    lax.fori_loop(0, SIDE // 2, fold, 0)
    if with_low:
        for c in range(2):
            before = jnp.zeros((8, ROWS), f32)
            for t in range(TILE // ROWS):
                rows = pl.ds(2 * SUB + 8 * c, 8)
                even = acc[FIRST + (SIDE - 1) * SIDE + 2 * t, rows, :]
                odd = acc[FIRST + (SIDE - 1) * SIDE + 2 * t + 1, rows, :]
                low[c, :, pl.ds(t * ROWS, ROWS)] = even + jnp.where(lane < SUB, before, odd)
                before = odd
            low[c, :, pl.ds(TILE, ROWS)] = jnp.where(lane < KW, before, 0.0)

    def finish(band, carry):
        copy_out(band).wait()
        return carry

    lax.fori_loop(0, SIDE, finish, 0)


def edge_kernel(edge, first, grid_in, grid_out, columns, out_sems):
    lane = lanes((8, ROWS))
    pairs = SIDE // 2

    def put(pair):
        rows = pl.ds(pair * 2 * SUB, 2 * SUB)
        return pltpu.make_async_copy(
            columns.at[:, rows, :], grid_out.at[:, rows, pl.ds(0, ROWS)], out_sems.at[pair]
        )

    def add(pair, carry):
        for c in range(2):
            packed = edge[c, pair]
            for k in range(16):
                moved = pltpu.roll(packed, ROWS - 8 * k, 1) if k else packed
                rows = pl.ds(pair * 2 * SUB + 8 * k, 8)
                columns[c, rows, :] = first[c, rows, :] + jnp.where(lane < KW, moved, 0.0)
        put(pair).start()
        return carry

    lax.fori_loop(0, pairs, add, 0)
    for pair in range(pairs):
        put(pair).wait()


def in_hbm(x):
    return pltpu.with_memory_space_constraint(x, pltpu.HBM)


def shifted(block, axis, distance):
    devices = range(lax.axis_size(axis))
    route = [(i - distance, i) for i in devices if i - distance in devices]
    return lax.ppermute(block, axis, route)


def shards(visibilities, vis_weight, cell_index, tap_offsets, routes, patch_index, kernel):
    blocks = visibilities.shape[0]
    tile_count = lax.axis_size("tile")
    plane_count = lax.axis_size("wp")
    peers = tile_count * plane_count
    cap = max(2, 2 * blocks // peers)
    rows = 3 * cap + 1
    vmem = pl.BlockSpec(memory_space=pltpu.VMEM)
    hbm = pl.BlockSpec(memory_space=pltpu.HBM)

    buckets = pl.pallas_call(
        functools.partial(pack_kernel, peers, cap),
        out_shape=jax.ShapeDtypeStruct((peers * rows, 1, ROWS), f32),
        in_specs=[hbm] * 6,
        out_specs=vmem,
        scratch_shapes=[
            pltpu.SMEM((blocks,), jnp.int32),
            pltpu.SMEM((blocks,), jnp.int32),
            pltpu.VMEM((blocks, 2, ROWS), f32),
            pltpu.VMEM((blocks, ROWS), f32),
            pltpu.VMEM((blocks, ROWS), jnp.int32),
            pltpu.VMEM((blocks, ROWS), jnp.int32),
            pltpu.SMEM((peers, ROWS), jnp.int32),
            pltpu.VMEM((peers, ROWS), jnp.int32),
            pltpu.SMEM((blocks,), jnp.int32),
            pltpu.SemaphoreType.DMA((7,)),
        ],
        compiler_params=pltpu.CompilerParams(vmem_limit_bytes=8 << 20),
        name="pack",
    )(*[in_hbm(x) for x in (routes[:, 0], patch_index, visibilities, vis_weight, cell_index, tap_offsets)])

    arrived = lax.all_to_all(buckets, ("tile", "wp"), split_axis=0, concat_axis=0, tiled=True)

    with_low = tile_count > TCOLS
    out_shape = [
        jax.ShapeDtypeStruct((2, TILE, TILE), f32),
        jax.ShapeDtypeStruct((2, SIDE // 2, 8, ROWS), f32),
        jax.ShapeDtypeStruct((2, TILE, ROWS), f32),
    ]
    out_specs = [hbm, vmem, vmem]
    if with_low:
        out_shape.append(jax.ShapeDtypeStruct((2, KW, TILE + ROWS), f32))
        out_specs.append(vmem)
    results = pl.pallas_call(
        functools.partial(grid_kernel, peers, cap, with_low),
        out_shape=out_shape,
        in_specs=[hbm, vmem],
        out_specs=out_specs,
        scratch_shapes=[
            pltpu.VMEM((DUMMY // 2 + -(-(DUMMY - DUMMY // 2) // peers) * peers + 1, ROW_BLOCK, ROWS), f32),
            pltpu.VMEM((2, TILE, TILE - ROWS), f32),
            pltpu.VMEM((peers, ROWS), jnp.int32),
            pltpu.SMEM((peers, ROWS), jnp.int32),
            pltpu.SMEM((peers * cap + max(cap, UNROLL),), jnp.int32),
            pltpu.SMEM((KW, OVER), f32),
            pltpu.SemaphoreType.DMA,
            pltpu.SemaphoreType.DMA,
            pltpu.SemaphoreType.DMA((SIDE,)),
        ],
        compiler_params=pltpu.CompilerParams(vmem_limit_bytes=48 << 20),
        name="grid",
    )(in_hbm(kernel.T), arrived)
    own, right, first = results[:3]

    place = lax.axis_index("tile")
    from_left = shifted(right, "tile", 1)
    if with_low:
        from_left = jnp.where(place % TCOLS == 0, 0.0, from_left)
    own = pl.pallas_call(
        edge_kernel,
        out_shape=jax.ShapeDtypeStruct((2, TILE, TILE), f32),
        in_specs=[vmem, vmem, hbm],
        out_specs=hbm,
        scratch_shapes=[
            pltpu.VMEM((2, TILE, ROWS), f32),
            pltpu.SemaphoreType.DMA((SIDE // 2,)),
        ],
        input_output_aliases={2: 0},
        compiler_params=pltpu.CompilerParams(vmem_limit_bytes=16 << 20),
        name="edges",
    )(from_left, first, own)
    if with_low:
        low = results[3]
        from_above = shifted(low, "tile", TCOLS)
        from_corner = shifted(low[:, :, TILE:], "tile", TCOLS + 1)
        from_corner = jnp.where(place % TCOLS == 0, 0.0, from_corner)
        own = own.at[:, :KW, :].add(from_above[:, :, :TILE])
        own = own.at[:, :KW, :ROWS].add(from_corner)
    return own.reshape(1, 1, 2, TILE, TILE)


def solution(mesh):
    in_specs = (
        P(("tile", "wp"), None, None),
        P(("tile", "wp"), None),
        P(("tile", "wp"), None),
        P(("tile", "wp"), None),
        P(("tile", "wp"), None),
        P(("tile", "wp")),
        P(),
    )
    out_specs = P("wp", "tile", None, None, None)
    return jax.shard_map(shards, mesh=mesh, in_specs=in_specs, out_specs=out_specs, check_vma=False)
```

```python
import functools

import jax
import jax.numpy as jnp
from jax import lax
from jax.experimental import pallas as pl
from jax.experimental.pallas import tpu as pltpu
from jax.sharding import PartitionSpec as P

TCOLS = 8
SUB = 64
KW = 8
OVER = 16
TILE = 1024
ROWS = 128
SIDE = TILE // SUB
PATCHES = SIDE * SIDE
ROW_BLOCK = 2 * (SUB + KW)
FIRST = SIDE
DUMMY = FIRST + PATCHES
LONG, SHORT = 64, 16

f32 = jnp.float32
bf16 = jnp.bfloat16


def lanes(shape):
    return lax.broadcasted_iota(jnp.int32, shape, len(shape) - 1)


def pack_kernel(peers, cap, routes, patch, vis, weight, cell, tap, out, acc, *scratch):
    routes_s, patch_s, vis_v, weight_v, cell_v, tap_v, meta, meta_v, place, sems = scratch
    blocks = vis.shape[0]
    rows = 3 * cap + 1
    sources = (routes, patch, vis, weight, cell, tap)
    targets = (routes_s, patch_s, vis_v, weight_v, cell_v, tap_v)
    copies = [pltpu.make_async_copy(a, b, sems.at[i]) for i, (a, b) in enumerate(zip(sources, targets))]
    for copy in copies:
        copy.start()

    steps = blocks // 8
    early = acc.shape[0] - 6 * steps

    def clear_accumulators(first, number):
        for i in range(number):
            acc[first + i] = jnp.zeros((ROW_BLOCK, ROWS), f32)

    def clear(d, carry):
        meta[d, cap] = 0
        return carry

    def clear_one(i, carry):
        clear_accumulators(i, 1)
        return carry

    lax.fori_loop(0, peers, clear, 0, unroll=8)
    lax.fori_loop(0, early, clear_one, 0)
    copies[0].wait()
    copies[1].wait()

    def choose(step, carry):
        clear_accumulators(early + 4 * step, 4)
        for i in range(8):
            b = step * 8 + i
            d = routes_s[b]
            k = meta[d, cap]
            meta[d, cap] = k + 1
            meta[d, k] = patch_s[b]
            place[b] = d * rows + 3 * k
        return carry

    lax.fori_loop(0, steps, choose, 0)
    meta_copy = pltpu.make_async_copy(meta, meta_v, sems.at[6])
    meta_copy.start()
    for copy in copies[2:]:
        copy.wait()

    def move(step, carry):
        clear_accumulators(early + 4 * steps + 2 * step, 2)
        first = pl.multiple_of(step * 8, 8)
        block_rows = pl.ds(first, 8)
        w = weight_v[block_rows, :]
        c = cell_v[block_rows, :]
        t = tap_v[block_rows, :]
        at_u = ((t >> 4) << 3) | ((c >> 6) & 7)
        at_v = ((t & 15) << 3) | (c & 7)
        code = (((c >> 9) << 17) | (((c >> 3) & 7) << 14) | (at_u << 7) | at_v).astype(f32)
        for i in range(8):
            row = place[first + i]
            both = vis_v[first + i] * w[i : i + 1, :]
            out[row] = both[0:1, :]
            out[row + 1] = both[1:2, :]
            out[row + 2] = code[i : i + 1, :]
        return carry

    lax.fori_loop(0, steps, move, 0)
    meta_copy.wait()

    def put_meta(d, carry):
        out[d * rows + 3 * cap] = meta_v[pl.ds(d, 1), :].astype(f32)
        return carry

    lax.fori_loop(0, peers, put_meta, 0, unroll=8)


def split(x):
    hi = x.astype(bf16)
    return hi, (x - hi.astype(f32)).astype(bf16)


def twice(x):
    return jnp.concatenate([x, x], axis=0)


def look_up(table, index):
    numbers = lax.GatherDimensionNumbers(
        offset_dims=(),
        collapsed_slice_dims=(1,),
        start_index_map=(1,),
        operand_batching_dims=(0,),
        start_indices_batching_dims=(0,),
    )
    return lax.gather(
        table, index[..., None], numbers, (1, 1), mode=lax.GatherScatterMode.PROMISE_IN_BOUNDS
    )


def spread(picks, values):
    zero = jnp.zeros((16, ROWS), bf16)
    return [[jnp.where(pick, value, zero) for pick in picks] for value in values]


def patch_product(re, im, code, parity, table):
    sub = lax.broadcasted_iota(jnp.int32, (8, ROWS), 0)
    at_v = code & 127
    at_u = (code >> 7) & 127
    ku = look_up(table, at_u)
    kv = look_up(table, at_v)
    group_u = ((code >> 17) & 7) + jnp.where(sub < (at_u & 7), 1, 0)
    group_v = ((code >> 14) & 7) + jnp.where(sub < (at_v & 7), 1, 0) + 8 * parity
    step_u = twice(group_u.astype(f32)).astype(bf16)
    step_v = jnp.concatenate([group_v & 15, (group_v + 15) & 15], axis=0).astype(f32).astype(bf16)

    u_hi, u_lo = split(jnp.concatenate([re * ku, im * ku], axis=0))
    hi_rows, lo_rows = spread([step_u == float(g) for g in range(SUB // 8 + 1)], [u_hi, u_lo])
    left_hi, left_lo = jnp.concatenate(hi_rows, axis=0), jnp.concatenate(lo_rows, axis=0)
    left = jnp.concatenate([left_hi, left_lo, left_hi], axis=1)

    v_hi, v_lo = split(twice(kv))
    hi_rows, lo_rows = spread([step_v == 2.0 * g for g in range(ROWS // 16)], [v_hi, v_lo])
    right_hi, right_lo = jnp.concatenate(hi_rows, axis=0), jnp.concatenate(lo_rows, axis=0)
    right = jnp.concatenate([right_hi, right_hi, right_lo], axis=1)
    return lax.dot_general(left, right, (((1,), (1,)), ((), ())), preferred_element_type=f32)


def tap_table(kernel):
    sub = lax.broadcasted_iota(jnp.int32, (8, ROWS), 0)
    lane = lanes((8, ROWS))
    which_tap = (sub - lane) & 7
    which_level = lane >> 3
    table = jnp.zeros((8, ROWS), f32)
    for a in range(KW):
        row = jnp.zeros((8, ROWS), f32)
        for o in range(OVER):
            row = jnp.where(which_level == o, kernel[a, o], row)
        table = jnp.where(which_tap == a, row, table)
    return table


def add_kernel(peers, cap, kernel, arrived, acc_in, acc, right, *scratch):
    meta_v, meta, slots, kernel_s, meta_sem, kernel_sem = scratch
    rows = 3 * cap + 1
    kernel_copy = pltpu.make_async_copy(kernel, kernel_s, kernel_sem)
    kernel_copy.start()
    lane_row = lanes((1, ROWS))

    def entries(s, carry):
        row = arrived[s * rows + 3 * cap].astype(jnp.int32)
        entry = (s * rows + 3 * lane_row) * 512 + (row + FIRST)
        meta_v[pl.ds(s, 1), :] = jnp.where(lane_row < cap, entry, row)
        return carry

    lax.fori_loop(0, peers, entries, 0, unroll=8)
    meta_copy = pltpu.make_async_copy(meta_v, meta, meta_sem)
    meta_copy.start()
    kernel_copy.wait()
    table = tap_table(kernel_s)
    meta_copy.wait()

    def gather_source(s, total):
        for k in range(cap):
            slots[total + k] = meta[s, k]
        return total + meta[s, cap]

    total = lax.fori_loop(0, peers, gather_source, 0, unroll=2)
    for k in range(SHORT):
        slots[total + k] = DUMMY

    def add(first, number):
        for i in range(number):
            entry = slots[first + i]
            row = entry >> 9
            where_to = entry & 511
            re = jnp.broadcast_to(arrived[row], (8, ROWS))
            im = jnp.broadcast_to(arrived[row + 1], (8, ROWS))
            code = jnp.broadcast_to(arrived[row + 2], (8, ROWS)).astype(jnp.int32)
            acc[where_to] += patch_product(re, im, code, entry & 1, table)

    def long_step(step, carry):
        add(step * LONG, LONG)
        return carry

    long_steps = total // LONG
    lax.fori_loop(0, long_steps, long_step, 0)
    done = long_steps * LONG

    def short_step(step, carry):
        add(done + step * SHORT, SHORT)
        return carry

    lax.fori_loop(0, (total - done + SHORT - 1) // SHORT, short_step, 0)

    lane = lanes((8, ROWS))

    def pack_edge(pair, carry):
        for c in range(2):
            edge = jnp.zeros((8, ROWS), f32)
            for k in range(16):
                last = rows_of(acc, c, k % 8, pair * 2 + k // 8, SIDE - 1)
                moved = pltpu.roll(last, 8 * k, 1) if k else last
                edge = jnp.where((lane >> 3) == k, moved, edge)
            right[c, pair] = edge
        return carry

    lax.fori_loop(0, SIDE // 2, pack_edge, 0)


def rows_of(acc, c, h, band, col):
    part = acc[FIRST + band * SIDE + col, pl.ds(16 * h + 8 * c, 8), :]
    if h == 0:
        part = part + acc[band * SIDE + col, pl.ds(2 * SUB + 8 * c, 8), :]
    return part


def fold_kernel(with_low, acc, out, first, *rest):
    low, rest = (rest[0], rest[1:]) if with_low else (None, rest)
    stage, out_sems = rest
    lane = lanes((8, ROWS))

    def copy_out(band):
        rows = pl.ds(band * SUB, SUB)
        return pltpu.make_async_copy(
            stage.at[:, rows, :], out.at[:, rows, pl.ds(ROWS, TILE - ROWS)], out_sems.at[band]
        )

    def fold(band, carry):
        for c in range(2):
            for h in range(8):
                before = jnp.zeros((8, ROWS), f32)
                for t in range(TILE // ROWS):
                    even = rows_of(acc, c, h, band, 2 * t)
                    odd = rows_of(acc, c, h, band, 2 * t + 1)
                    rows = pl.ds(band * SUB + 8 * h, 8)
                    columns = even + jnp.where(lane < SUB, before, odd)
                    if t == 0:
                        first[c, rows, :] = columns
                    else:
                        stage[c, rows, pl.ds((t - 1) * ROWS, ROWS)] = columns
                    before = odd
        copy_out(band).start()
        return carry

    lax.fori_loop(0, SIDE, fold, 0)
    if with_low:
        for c in range(2):
            before = jnp.zeros((8, ROWS), f32)
            for t in range(TILE // ROWS):
                rows = pl.ds(2 * SUB + 8 * c, 8)
                even = acc[FIRST + (SIDE - 1) * SIDE + 2 * t, rows, :]
                odd = acc[FIRST + (SIDE - 1) * SIDE + 2 * t + 1, rows, :]
                low[c, :, pl.ds(t * ROWS, ROWS)] = even + jnp.where(lane < SUB, before, odd)
                before = odd
            low[c, :, pl.ds(TILE, ROWS)] = jnp.where(lane < KW, before, 0.0)

    def finish(band, carry):
        copy_out(band).wait()
        return carry

    lax.fori_loop(0, SIDE, finish, 0)


def edge_kernel(edge, first, grid_in, grid_out, columns, out_sems):
    lane = lanes((8, ROWS))
    pairs = SIDE // 2

    def put(pair):
        rows = pl.ds(pair * 2 * SUB, 2 * SUB)
        return pltpu.make_async_copy(
            columns.at[:, rows, :], grid_out.at[:, rows, pl.ds(0, ROWS)], out_sems.at[pair]
        )

    def add(pair, carry):
        for c in range(2):
            packed = edge[c, pair]
            for k in range(16):
                moved = pltpu.roll(packed, ROWS - 8 * k, 1) if k else packed
                rows = pl.ds(pair * 2 * SUB + 8 * k, 8)
                columns[c, rows, :] = first[c, rows, :] + jnp.where(lane < KW, moved, 0.0)
        put(pair).start()
        return carry

    lax.fori_loop(0, pairs, add, 0)
    for pair in range(pairs):
        put(pair).wait()


def in_hbm(x):
    return pltpu.with_memory_space_constraint(x, pltpu.HBM)


def shifted(block, axis, distance):
    devices = range(lax.axis_size(axis))
    route = [(i - distance, i) for i in devices if i - distance in devices]
    return lax.ppermute(block, axis, route)


def shards(visibilities, vis_weight, cell_index, tap_offsets, routes, patch_index, kernel):
    blocks = visibilities.shape[0]
    tile_count = lax.axis_size("tile")
    plane_count = lax.axis_size("wp")
    peers = tile_count * plane_count
    cap = max(2, 2 * blocks // peers)
    rows = 3 * cap + 1
    vmem = pl.BlockSpec(memory_space=pltpu.VMEM)
    hbm = pl.BlockSpec(memory_space=pltpu.HBM)

    acc_shape = (max(DUMMY + 1, 6 * (blocks // 8)), ROW_BLOCK, ROWS)

    buckets, acc = pl.pallas_call(
        functools.partial(pack_kernel, peers, cap),
        out_shape=[jax.ShapeDtypeStruct((peers * rows, 1, ROWS), f32), pltpu.VMEM(acc_shape, f32)],
        in_specs=[hbm] * 6,
        out_specs=[vmem, vmem],
        scratch_shapes=[
            pltpu.SMEM((blocks,), jnp.int32),
            pltpu.SMEM((blocks,), jnp.int32),
            pltpu.VMEM((blocks, 2, ROWS), f32),
            pltpu.VMEM((blocks, ROWS), f32),
            pltpu.VMEM((blocks, ROWS), jnp.int32),
            pltpu.VMEM((blocks, ROWS), jnp.int32),
            pltpu.SMEM((peers, ROWS), jnp.int32),
            pltpu.VMEM((peers, ROWS), jnp.int32),
            pltpu.SMEM((blocks,), jnp.int32),
            pltpu.SemaphoreType.DMA((7,)),
        ],
        compiler_params=pltpu.CompilerParams(vmem_limit_bytes=8 << 20),
        name="pack",
    )(*[in_hbm(x) for x in (routes[:, 0], patch_index, visibilities, vis_weight, cell_index, tap_offsets)])

    arrived = lax.all_to_all(buckets, ("tile", "wp"), split_axis=0, concat_axis=0, tiled=True)

    acc, right = pl.pallas_call(
        functools.partial(add_kernel, peers, cap),
        out_shape=[pltpu.VMEM(acc_shape, f32), jax.ShapeDtypeStruct((2, SIDE // 2, 8, ROWS), f32)],
        in_specs=[hbm, vmem, vmem],
        out_specs=[vmem, vmem],
        scratch_shapes=[
            pltpu.VMEM((peers, ROWS), jnp.int32),
            pltpu.SMEM((peers, ROWS), jnp.int32),
            pltpu.SMEM((peers * cap + max(cap, SHORT),), jnp.int32),
            pltpu.SMEM((KW, OVER), f32),
            pltpu.SemaphoreType.DMA,
            pltpu.SemaphoreType.DMA,
        ],
        input_output_aliases={2: 0},
        compiler_params=pltpu.CompilerParams(vmem_limit_bytes=4 << 20),
        name="add",
    )(in_hbm(kernel.T), arrived, acc)

    place = lax.axis_index("tile")
    from_left = shifted(right, "tile", 1)

    with_low = tile_count > TCOLS
    out_shape = [jax.ShapeDtypeStruct((2, TILE, TILE), f32), jax.ShapeDtypeStruct((2, TILE, ROWS), f32)]
    out_specs = [hbm, vmem]
    if with_low:
        out_shape.append(jax.ShapeDtypeStruct((2, KW, TILE + ROWS), f32))
        out_specs.append(vmem)
    own, first, *low = pl.pallas_call(
        functools.partial(fold_kernel, with_low),
        out_shape=out_shape,
        in_specs=[vmem],
        out_specs=out_specs,
        scratch_shapes=[pltpu.VMEM((2, TILE, TILE - ROWS), f32), pltpu.SemaphoreType.DMA((SIDE,))],
        compiler_params=pltpu.CompilerParams(vmem_limit_bytes=12 << 20),
        cost_estimate=pl.CostEstimate(flops=1 << 22, bytes_accessed=16 << 20, transcendentals=0),
        name="fold",
    )(acc)

    if with_low:
        from_left = jnp.where(place % TCOLS == 0, 0.0, from_left)
    own = pl.pallas_call(
        edge_kernel,
        out_shape=jax.ShapeDtypeStruct((2, TILE, TILE), f32),
        in_specs=[vmem, vmem, hbm],
        out_specs=hbm,
        scratch_shapes=[
            pltpu.VMEM((2, TILE, ROWS), f32),
            pltpu.SemaphoreType.DMA((SIDE // 2,)),
        ],
        input_output_aliases={2: 0},
        compiler_params=pltpu.CompilerParams(vmem_limit_bytes=4 << 20),
        name="edges",
    )(from_left, first, own)
    if with_low:
        (low,) = low
        from_above = shifted(low, "tile", TCOLS)
        from_corner = shifted(low[:, :, TILE:], "tile", TCOLS + 1)
        from_corner = jnp.where(place % TCOLS == 0, 0.0, from_corner)
        own = own.at[:, :KW, :].add(from_above[:, :, :TILE])
        own = own.at[:, :KW, :ROWS].add(from_corner)
    return own.reshape(1, 1, 2, TILE, TILE)


def solution(mesh):
    in_specs = (
        P(("tile", "wp"), None, None),
        P(("tile", "wp"), None),
        P(("tile", "wp"), None),
        P(("tile", "wp"), None),
        P(("tile", "wp"), None),
        P(("tile", "wp")),
        P(),
    )
    out_specs = P("wp", "tile", None, None, None)
    return jax.shard_map(shards, mesh=mesh, in_specs=in_specs, out_specs=out_specs, check_vma=False)
```

```python
import functools

import jax
import jax.numpy as jnp
from jax import lax
from jax.experimental import pallas as pl
from jax.experimental.pallas import tpu as pltpu
from jax.sharding import PartitionSpec as P

TCOLS = 8
SUB = 64
KW = 8
OVER = 16
TILE = 1024
ROWS = 128
SIDE = TILE // SUB
PATCHES = SIDE * SIDE
ROW_BLOCK = 2 * (SUB + KW)
FIRST = SIDE
DUMMY = FIRST + PATCHES
LONG, SHORT = 64, 16

f32 = jnp.float32
bf16 = jnp.bfloat16


def lanes(shape):
    return lax.broadcasted_iota(jnp.int32, shape, len(shape) - 1)


def pack_kernel(peers, cap, routes, patch, vis, weight, cell, tap, out, acc, *scratch):
    routes_s, patch_s, vis_v, weight_v, cell_v, tap_v, meta, meta_v, place, sems = scratch
    blocks = vis.shape[0]
    rows = 3 * cap + 1
    sources = (routes, patch, vis, weight, cell, tap)
    targets = (routes_s, patch_s, vis_v, weight_v, cell_v, tap_v)
    copies = [pltpu.make_async_copy(a, b, sems.at[i]) for i, (a, b) in enumerate(zip(sources, targets))]
    for copy in copies:
        copy.start()

    steps = blocks // 8
    me = lax.axis_index("half")

    def bucket_row(d):
        upper = jnp.where(d >= peers // 2, 1, 0)
        return ((d - upper * (peers // 2)) * 2 + (upper ^ me)) * rows

    early = acc.shape[0] - 6 * steps

    def clear_accumulators(first, number):
        for i in range(number):
            acc[first + i] = jnp.zeros((ROW_BLOCK, ROWS), f32)

    def clear(d, carry):
        meta[d, cap] = 0
        return carry

    def clear_one(i, carry):
        clear_accumulators(i, 1)
        return carry

    lax.fori_loop(0, peers, clear, 0, unroll=8)
    lax.fori_loop(0, early, clear_one, 0)
    copies[0].wait()
    copies[1].wait()

    def choose(step, carry):
        clear_accumulators(early + 4 * step, 4)
        for i in range(8):
            b = step * 8 + i
            d = routes_s[b]
            k = meta[d, cap]
            meta[d, cap] = k + 1
            meta[d, k] = patch_s[b]
            place[b] = bucket_row(d) + 3 * k
        return carry

    lax.fori_loop(0, steps, choose, 0)
    meta_copy = pltpu.make_async_copy(meta, meta_v, sems.at[6])
    meta_copy.start()
    for copy in copies[2:]:
        copy.wait()

    def move(step, carry):
        clear_accumulators(early + 4 * steps + 2 * step, 2)
        first = pl.multiple_of(step * 8, 8)
        block_rows = pl.ds(first, 8)
        w = weight_v[block_rows, :]
        c = cell_v[block_rows, :]
        t = tap_v[block_rows, :]
        at_u = ((t >> 4) << 3) | ((c >> 6) & 7)
        at_v = ((t & 15) << 3) | (c & 7)
        code = (((c >> 9) << 17) | (((c >> 3) & 7) << 14) | (at_u << 7) | at_v).astype(f32)
        for i in range(8):
            row = place[first + i]
            both = vis_v[first + i] * w[i : i + 1, :]
            out[row] = both[0:1, :]
            out[row + 1] = both[1:2, :]
            out[row + 2] = code[i : i + 1, :]
        return carry

    lax.fori_loop(0, steps, move, 0)
    meta_copy.wait()

    def put_meta(d, carry):
        out[bucket_row(d) + 3 * cap] = meta_v[pl.ds(d, 1), :].astype(f32)
        return carry

    lax.fori_loop(0, peers, put_meta, 0, unroll=8)


def split(x):
    hi = x.astype(bf16)
    return hi, (x - hi.astype(f32)).astype(bf16)


def twice(x):
    return jnp.concatenate([x, x], axis=0)


def look_up(table, index):
    numbers = lax.GatherDimensionNumbers(
        offset_dims=(),
        collapsed_slice_dims=(1,),
        start_index_map=(1,),
        operand_batching_dims=(0,),
        start_indices_batching_dims=(0,),
    )
    return lax.gather(
        table, index[..., None], numbers, (1, 1), mode=lax.GatherScatterMode.PROMISE_IN_BOUNDS
    )


def spread(picks, values):
    zero = jnp.zeros((16, ROWS), bf16)
    return [[jnp.where(pick, value, zero) for pick in picks] for value in values]


def patch_product(re, im, code, parity, table):
    sub = lax.broadcasted_iota(jnp.int32, (8, ROWS), 0)
    at_v = code & 127
    at_u = (code >> 7) & 127
    ku = look_up(table, at_u)
    kv = look_up(table, at_v)
    group_u = ((code >> 17) & 7) + jnp.where(sub < (at_u & 7), 1, 0)
    group_v = ((code >> 14) & 7) + jnp.where(sub < (at_v & 7), 1, 0) + 8 * parity
    step_u = twice(group_u.astype(f32)).astype(bf16)
    step_v = jnp.concatenate([group_v & 15, (group_v + 15) & 15], axis=0).astype(f32).astype(bf16)

    u_hi, u_lo = split(jnp.concatenate([re * ku, im * ku], axis=0))
    hi_rows, lo_rows = spread([step_u == float(g) for g in range(SUB // 8 + 1)], [u_hi, u_lo])
    left_hi, left_lo = jnp.concatenate(hi_rows, axis=0), jnp.concatenate(lo_rows, axis=0)
    left = jnp.concatenate([left_hi, left_lo, left_hi], axis=1)

    v_hi, v_lo = split(twice(kv))
    hi_rows, lo_rows = spread([step_v == 2.0 * g for g in range(ROWS // 16)], [v_hi, v_lo])
    right_hi, right_lo = jnp.concatenate(hi_rows, axis=0), jnp.concatenate(lo_rows, axis=0)
    right = jnp.concatenate([right_hi, right_hi, right_lo], axis=1)
    return lax.dot_general(left, right, (((1,), (1,)), ((), ())), preferred_element_type=f32)


def tap_table(kernel):
    sub = lax.broadcasted_iota(jnp.int32, (8, ROWS), 0)
    lane = lanes((8, ROWS))
    which_tap = (sub - lane) & 7
    which_level = lane >> 3
    table = jnp.zeros((8, ROWS), f32)
    for a in range(KW):
        row = jnp.zeros((8, ROWS), f32)
        for o in range(OVER):
            row = jnp.where(which_level == o, kernel[a, o], row)
        table = jnp.where(which_tap == a, row, table)
    return table


def add_kernel(sources, cap, stride, with_edge, kernel, arrived, acc_in, acc, *scratch):
    right, scratch = (scratch[0], scratch[1:]) if with_edge else (None, scratch)
    meta_v, meta, slots, kernel_s, meta_sem, kernel_sem = scratch
    kernel_copy = pltpu.make_async_copy(kernel, kernel_s, kernel_sem)
    kernel_copy.start()
    lane_row = lanes((1, ROWS))

    def entries(s, carry):
        row = arrived[s * stride + 3 * cap].astype(jnp.int32)
        entry = (s * stride + 3 * lane_row) * 512 + (row + FIRST)
        meta_v[pl.ds(s, 1), :] = jnp.where(lane_row < cap, entry, row)
        return carry

    lax.fori_loop(0, sources, entries, 0, unroll=8)
    meta_copy = pltpu.make_async_copy(meta_v, meta, meta_sem)
    meta_copy.start()
    kernel_copy.wait()
    table = tap_table(kernel_s)
    meta_copy.wait()

    def gather_source(s, total):
        for k in range(cap):
            slots[total + k] = meta[s, k]
        return total + meta[s, cap]

    total = lax.fori_loop(0, sources, gather_source, 0, unroll=2)
    for k in range(SHORT):
        slots[total + k] = DUMMY

    def add(first, number):
        for i in range(number):
            entry = slots[first + i]
            row = entry >> 9
            where_to = entry & 511
            re = jnp.broadcast_to(arrived[row], (8, ROWS))
            im = jnp.broadcast_to(arrived[row + 1], (8, ROWS))
            code = jnp.broadcast_to(arrived[row + 2], (8, ROWS)).astype(jnp.int32)
            acc[where_to] += patch_product(re, im, code, entry & 1, table)

    def long_step(step, carry):
        add(step * LONG, LONG)
        return carry

    long_steps = total // LONG
    lax.fori_loop(0, long_steps, long_step, 0)
    done = long_steps * LONG

    def short_step(step, carry):
        add(done + step * SHORT, SHORT)
        return carry

    lax.fori_loop(0, (total - done + SHORT - 1) // SHORT, short_step, 0)

    if not with_edge:
        return

    lane = lanes((8, ROWS))

    def pack_edge(pair, carry):
        for c in range(2):
            edge = jnp.zeros((8, ROWS), f32)
            for k in range(16):
                last = rows_of(acc, c, k % 8, pair * 2 + k // 8, SIDE - 1)
                moved = pltpu.roll(last, 8 * k, 1) if k else last
                edge = jnp.where((lane >> 3) == k, moved, edge)
            right[c, pair] = edge
        return carry

    lax.fori_loop(0, SIDE // 2, pack_edge, 0)


def rows_of(acc, c, h, band, col):
    part = acc[FIRST + band * SIDE + col, pl.ds(16 * h + 8 * c, 8), :]
    if h == 0:
        part = part + acc[band * SIDE + col, pl.ds(2 * SUB + 8 * c, 8), :]
    return part


def fold_kernel(with_low, acc, out, first, *rest):
    low, rest = (rest[0], rest[1:]) if with_low else (None, rest)
    stage, out_sems = rest
    lane = lanes((8, ROWS))

    def copy_out(band):
        rows = pl.ds(band * SUB, SUB)
        return pltpu.make_async_copy(
            stage.at[:, rows, :], out.at[:, rows, pl.ds(ROWS, TILE - ROWS)], out_sems.at[band]
        )

    def fold(band, carry):
        for c in range(2):
            for h in range(8):
                before = jnp.zeros((8, ROWS), f32)
                for t in range(TILE // ROWS):
                    even = rows_of(acc, c, h, band, 2 * t)
                    odd = rows_of(acc, c, h, band, 2 * t + 1)
                    rows = pl.ds(band * SUB + 8 * h, 8)
                    columns = even + jnp.where(lane < SUB, before, odd)
                    if t == 0:
                        first[c, rows, :] = columns
                    else:
                        stage[c, rows, pl.ds((t - 1) * ROWS, ROWS)] = columns
                    before = odd
        copy_out(band).start()
        return carry

    lax.fori_loop(0, SIDE, fold, 0)
    if with_low:
        for c in range(2):
            before = jnp.zeros((8, ROWS), f32)
            for t in range(TILE // ROWS):
                rows = pl.ds(2 * SUB + 8 * c, 8)
                even = acc[FIRST + (SIDE - 1) * SIDE + 2 * t, rows, :]
                odd = acc[FIRST + (SIDE - 1) * SIDE + 2 * t + 1, rows, :]
                low[c, :, pl.ds(t * ROWS, ROWS)] = even + jnp.where(lane < SUB, before, odd)
                before = odd
            low[c, :, pl.ds(TILE, ROWS)] = jnp.where(lane < KW, before, 0.0)

    def finish(band, carry):
        copy_out(band).wait()
        return carry

    lax.fori_loop(0, SIDE, finish, 0)


def edge_kernel(edge, first, grid_in, grid_out, columns, out_sems):
    lane = lanes((8, ROWS))
    pairs = SIDE // 2

    def put(pair):
        rows = pl.ds(pair * 2 * SUB, 2 * SUB)
        return pltpu.make_async_copy(
            columns.at[:, rows, :], grid_out.at[:, rows, pl.ds(0, ROWS)], out_sems.at[pair]
        )

    def add(pair, carry):
        for c in range(2):
            packed = edge[c, pair]
            for k in range(16):
                moved = pltpu.roll(packed, ROWS - 8 * k, 1) if k else packed
                rows = pl.ds(pair * 2 * SUB + 8 * k, 8)
                columns[c, rows, :] = first[c, rows, :] + jnp.where(lane < KW, moved, 0.0)
        put(pair).start()
        return carry

    lax.fori_loop(0, pairs, add, 0)
    for pair in range(pairs):
        put(pair).wait()


def in_hbm(x):
    return pltpu.with_memory_space_constraint(x, pltpu.HBM)


def shifted(block, distance):
    tiles = ("half", "tile")
    devices = range(lax.axis_size(tiles))
    route = [(i - distance, i) for i in devices if i - distance in devices]
    return lax.ppermute(block, tiles, route)


def shards(visibilities, vis_weight, cell_index, tap_offsets, routes, patch_index, kernel):
    blocks = visibilities.shape[0]
    tile_count = lax.axis_size(("half", "tile"))
    plane_count = lax.axis_size("wp")
    peers = tile_count * plane_count
    cap = max(2, 2 * blocks // peers)
    rows = 3 * cap + 1
    vmem = pl.BlockSpec(memory_space=pltpu.VMEM)
    hbm = pl.BlockSpec(memory_space=pltpu.HBM)

    acc_shape = (max(DUMMY + 1, 6 * (blocks // 8)), ROW_BLOCK, ROWS)

    buckets, acc = pl.pallas_call(
        functools.partial(pack_kernel, peers, cap),
        out_shape=[jax.ShapeDtypeStruct((peers * rows, 1, ROWS), f32), pltpu.VMEM(acc_shape, f32)],
        in_specs=[hbm] * 6,
        out_specs=[vmem, vmem],
        scratch_shapes=[
            pltpu.SMEM((blocks,), jnp.int32),
            pltpu.SMEM((blocks,), jnp.int32),
            pltpu.VMEM((blocks, 2, ROWS), f32),
            pltpu.VMEM((blocks, ROWS), f32),
            pltpu.VMEM((blocks, ROWS), jnp.int32),
            pltpu.VMEM((blocks, ROWS), jnp.int32),
            pltpu.SMEM((peers, ROWS), jnp.int32),
            pltpu.VMEM((peers, ROWS), jnp.int32),
            pltpu.SMEM((blocks,), jnp.int32),
            pltpu.SemaphoreType.DMA((7,)),
        ],
        compiler_params=pltpu.CompilerParams(vmem_limit_bytes=8 << 20),
        name="pack",
    )(*[in_hbm(x) for x in (routes[:, 0], patch_index, visibilities, vis_weight, cell_index, tap_offsets)])

    arrived = lax.all_to_all(buckets, ("tile", "wp"), split_axis=0, concat_axis=0, tiled=True)

    sources = peers // 2
    far = arrived.reshape(sources, 2 * rows, 1, ROWS)[:, rows:].reshape(sources * rows, 1, ROWS)
    far = lax.ppermute(far, "half", [(0, 1), (1, 0)])

    def add(part, stride, acc, with_edge):
        out_shape, out_specs = [pltpu.VMEM(acc_shape, f32)], [vmem]
        if with_edge:
            out_shape.append(jax.ShapeDtypeStruct((2, SIDE // 2, 8, ROWS), f32))
            out_specs.append(vmem)
        return pl.pallas_call(
            functools.partial(add_kernel, sources, cap, stride, with_edge),
            out_shape=out_shape,
            in_specs=[hbm, vmem, vmem],
            out_specs=out_specs,
            scratch_shapes=[
                pltpu.VMEM((sources, ROWS), jnp.int32),
                pltpu.SMEM((sources, ROWS), jnp.int32),
                pltpu.SMEM((sources * cap + max(cap, SHORT),), jnp.int32),
                pltpu.SMEM((KW, OVER), f32),
                pltpu.SemaphoreType.DMA,
                pltpu.SemaphoreType.DMA,
            ],
            input_output_aliases={2: 0},
            compiler_params=pltpu.CompilerParams(vmem_limit_bytes=4 << 20),
            cost_estimate=pl.CostEstimate(flops=1 << 33, bytes_accessed=1 << 20, transcendentals=0),
            name="add_far" if with_edge else "add_near",
        )(in_hbm(kernel.T), part, acc)

    (acc,) = add(arrived, 2 * rows, acc, False)
    acc, right = add(far, rows, acc, True)

    place = lax.axis_index(("half", "tile"))
    from_left = shifted(right, 1)

    with_low = tile_count > TCOLS
    out_shape = [jax.ShapeDtypeStruct((2, TILE, TILE), f32), jax.ShapeDtypeStruct((2, TILE, ROWS), f32)]
    out_specs = [hbm, vmem]
    if with_low:
        out_shape.append(jax.ShapeDtypeStruct((2, KW, TILE + ROWS), f32))
        out_specs.append(vmem)
    own, first, *low = pl.pallas_call(
        functools.partial(fold_kernel, with_low),
        out_shape=out_shape,
        in_specs=[vmem],
        out_specs=out_specs,
        scratch_shapes=[pltpu.VMEM((2, TILE, TILE - ROWS), f32), pltpu.SemaphoreType.DMA((SIDE,))],
        compiler_params=pltpu.CompilerParams(vmem_limit_bytes=12 << 20),
        cost_estimate=pl.CostEstimate(flops=1 << 22, bytes_accessed=16 << 20, transcendentals=0),
        name="fold",
    )(acc)

    if with_low:
        from_left = jnp.where(place % TCOLS == 0, 0.0, from_left)
    own = pl.pallas_call(
        edge_kernel,
        out_shape=jax.ShapeDtypeStruct((2, TILE, TILE), f32),
        in_specs=[vmem, vmem, hbm],
        out_specs=hbm,
        scratch_shapes=[
            pltpu.VMEM((2, TILE, ROWS), f32),
            pltpu.SemaphoreType.DMA((SIDE // 2,)),
        ],
        input_output_aliases={2: 0},
        compiler_params=pltpu.CompilerParams(vmem_limit_bytes=4 << 20),
        name="edges",
    )(from_left, first, own)
    if with_low:
        (low,) = low
        from_above = shifted(low, TCOLS)
        from_corner = shifted(low[:, :, TILE:], TCOLS + 1)
        from_corner = jnp.where(place % TCOLS == 0, 0.0, from_corner)
        own = own.at[:, :KW, :].add(from_above[:, :, :TILE])
        own = own.at[:, :KW, :ROWS].add(from_corner)
    return own.reshape(1, 1, 2, TILE, TILE)


def solution(mesh):
    tiles, planes = mesh.shape["tile"], mesh.shape["wp"]
    halves = jax.sharding.Mesh(mesh.devices.reshape(2, tiles // 2, planes), ("half", "tile", "wp"))
    every = ("half", "tile", "wp")
    in_specs = (
        P(every, None, None),
        P(every, None),
        P(every, None),
        P(every, None),
        P(every, None),
        P(every),
        P(),
    )
    out_specs = P("wp", ("half", "tile"), None, None, None)
    return jax.shard_map(shards, mesh=halves, in_specs=in_specs, out_specs=out_specs, check_vma=False)
```

```python
import functools

import jax
import jax.numpy as jnp
from jax import lax
from jax.experimental import pallas as pl
from jax.experimental.pallas import tpu as pltpu
from jax.sharding import PartitionSpec as P

TCOLS = 8
SUB = 64
KW = 8
OVER = 16
TILE = 1024
ROWS = 128
SIDE = TILE // SUB
PATCHES = SIDE * SIDE
ROW_BLOCK = 2 * (SUB + KW)
FIRST = SIDE
DUMMY = FIRST + PATCHES
LONG, SHORT = 64, 16

f32 = jnp.float32
bf16 = jnp.bfloat16


def lanes(shape):
    return lax.broadcasted_iota(jnp.int32, shape, len(shape) - 1)


def pack_kernel(peers, cap, routes, patch, vis, weight, cell, tap, out, acc, *scratch):
    routes_s, patch_s, vis_v, weight_v, cell_v, tap_v, meta, meta_v, place, bases, sems = scratch
    blocks = vis.shape[0]
    rows = 3 * cap + 1
    sources = (routes, patch, vis, weight, cell, tap)
    targets = (routes_s, patch_s, vis_v, weight_v, cell_v, tap_v)
    copies = [pltpu.make_async_copy(a, b, sems.at[i]) for i, (a, b) in enumerate(zip(sources, targets))]
    for copy in copies:
        copy.start()

    steps = blocks // 8
    me = lax.axis_index("half")

    early = acc.shape[0] - 6 * steps

    def clear_accumulators(first, number):
        for i in range(number):
            acc[first + i] = jnp.zeros((ROW_BLOCK, ROWS), f32)

    def clear(d, carry):
        meta[d, cap] = 0
        upper = jnp.where(d >= peers // 2, 1, 0)
        bases[d] = ((d - upper * (peers // 2)) * 2 + (upper ^ me)) * rows
        return carry

    def clear_one(i, carry):
        clear_accumulators(i, 1)
        return carry

    lax.fori_loop(0, peers, clear, 0, unroll=8)
    lax.fori_loop(0, early, clear_one, 0)
    copies[0].wait()
    copies[1].wait()

    def choose(step, carry):
        clear_accumulators(early + 4 * step, 4)
        for i in range(8):
            b = step * 8 + i
            d = routes_s[b]
            k = meta[d, cap]
            meta[d, cap] = k + 1
            meta[d, k] = patch_s[b]
            place[b] = bases[d] + 3 * k
        return carry

    lax.fori_loop(0, steps, choose, 0)
    meta_copy = pltpu.make_async_copy(meta, meta_v, sems.at[6])
    meta_copy.start()
    for copy in copies[2:]:
        copy.wait()

    def move(step, carry):
        clear_accumulators(early + 4 * steps + 2 * step, 2)
        first = pl.multiple_of(step * 8, 8)
        block_rows = pl.ds(first, 8)
        w = weight_v[block_rows, :]
        c = cell_v[block_rows, :]
        t = tap_v[block_rows, :]
        at_u = ((t >> 4) << 3) | ((c >> 6) & 7)
        at_v = ((t & 15) << 3) | (c & 7)
        code = (((c >> 9) << 17) | (((c >> 3) & 7) << 14) | (at_u << 7) | at_v).astype(f32)
        for i in range(8):
            row = place[first + i]
            both = vis_v[first + i] * w[i : i + 1, :]
            out[row] = both[0:1, :]
            out[row + 1] = both[1:2, :]
            out[row + 2] = code[i : i + 1, :]
        return carry

    lax.fori_loop(0, steps, move, 0)
    meta_copy.wait()

    def put_meta(d, carry):
        out[bases[d] + 3 * cap] = meta_v[pl.ds(d, 1), :].astype(f32)
        return carry

    lax.fori_loop(0, peers, put_meta, 0, unroll=8)


def split(x):
    hi = x.astype(bf16)
    return hi, (x - hi.astype(f32)).astype(bf16)


def twice(x):
    return jnp.concatenate([x, x], axis=0)


def look_up(table, index):
    numbers = lax.GatherDimensionNumbers(
        offset_dims=(),
        collapsed_slice_dims=(1,),
        start_index_map=(1,),
        operand_batching_dims=(0,),
        start_indices_batching_dims=(0,),
    )
    return lax.gather(
        table, index[..., None], numbers, (1, 1), mode=lax.GatherScatterMode.PROMISE_IN_BOUNDS
    )


def spread(picks, values):
    zero = jnp.zeros((16, ROWS), bf16)
    return [[jnp.where(pick, value, zero) for pick in picks] for value in values]


def patch_product(re, im, code, parity, table):
    sub = lax.broadcasted_iota(jnp.int32, (8, ROWS), 0)
    at_v = code & 127
    at_u = (code >> 7) & 127
    ku = look_up(table, at_u)
    kv = look_up(table, at_v)
    group_u = ((code >> 17) & 7) + jnp.where(sub < (at_u & 7), 1, 0)
    group_v = ((code >> 14) & 7) + jnp.where(sub < (at_v & 7), 1, 0) + 8 * parity
    step_u = twice(group_u.astype(f32)).astype(bf16)
    step_v = jnp.concatenate([group_v & 15, (group_v + 15) & 15], axis=0).astype(f32).astype(bf16)

    u_hi, u_lo = split(jnp.concatenate([re * ku, im * ku], axis=0))
    hi_rows, lo_rows = spread([step_u == float(g) for g in range(SUB // 8 + 1)], [u_hi, u_lo])
    left_hi, left_lo = jnp.concatenate(hi_rows, axis=0), jnp.concatenate(lo_rows, axis=0)
    left = jnp.concatenate([left_hi, left_lo, left_hi], axis=1)

    v_hi, v_lo = split(twice(kv))
    hi_rows, lo_rows = spread([step_v == 2.0 * g for g in range(ROWS // 16)], [v_hi, v_lo])
    right_hi, right_lo = jnp.concatenate(hi_rows, axis=0), jnp.concatenate(lo_rows, axis=0)
    right = jnp.concatenate([right_hi, right_hi, right_lo], axis=1)
    return lax.dot_general(left, right, (((1,), (1,)), ((), ())), preferred_element_type=f32)


def tap_table(kernel):
    sub = lax.broadcasted_iota(jnp.int32, (8, ROWS), 0)
    lane = lanes((8, ROWS))
    which_tap = (sub - lane) & 7
    which_level = lane >> 3
    table = jnp.zeros((8, ROWS), f32)
    for a in range(KW):
        row = jnp.zeros((8, ROWS), f32)
        for o in range(OVER):
            row = jnp.where(which_level == o, kernel[a, o], row)
        table = jnp.where(which_tap == a, row, table)
    return table


def add_kernel(sources, cap, stride, passed, with_edge, kernel, arrived, acc_in, acc, *scratch):
    right, scratch = (scratch[0], scratch[1:]) if with_edge else (None, scratch)
    handed, scratch = (scratch[0], scratch[1:]) if passed else (None, scratch)
    meta_v, meta, slots, kernel_s, meta_sem, kernel_sem, *handed_sem = scratch
    half = stride // 2
    handed_copies = [
        pltpu.make_async_copy(
            arrived.at[pl.ds((sources - passed + i) * stride + half, half)],
            handed.at[pl.ds(i * half, half)],
            handed_sem[0].at[i],
        )
        for i in range(passed)
    ]
    for copy in handed_copies:
        copy.start()
    kernel_copy = pltpu.make_async_copy(kernel, kernel_s, kernel_sem)
    kernel_copy.start()
    lane_row = lanes((1, ROWS))

    def entries(s, carry):
        row = arrived[s * stride + 3 * cap].astype(jnp.int32)
        entry = (s * stride + 3 * lane_row) * 512 + (row + FIRST)
        meta_v[pl.ds(s, 1), :] = jnp.where(lane_row < cap, entry, row)
        return carry

    lax.fori_loop(0, sources, entries, 0, unroll=8)
    meta_copy = pltpu.make_async_copy(meta_v, meta, meta_sem)
    meta_copy.start()
    kernel_copy.wait()
    table = tap_table(kernel_s)
    meta_copy.wait()

    def gather_source(s, total):
        for k in range(cap):
            slots[total + k] = meta[s, k]
        return total + meta[s, cap]

    total = lax.fori_loop(0, sources, gather_source, 0, unroll=2)
    for k in range(SHORT):
        slots[total + k] = DUMMY

    def add(first, number):
        for i in range(number):
            entry = slots[first + i]
            row = entry >> 9
            where_to = entry & 511
            re = jnp.broadcast_to(arrived[row], (8, ROWS))
            im = jnp.broadcast_to(arrived[row + 1], (8, ROWS))
            code = jnp.broadcast_to(arrived[row + 2], (8, ROWS)).astype(jnp.int32)
            acc[where_to] += patch_product(re, im, code, entry & 1, table)

    def long_step(step, carry):
        add(step * LONG, LONG)
        return carry

    long_steps = total // LONG
    lax.fori_loop(0, long_steps, long_step, 0)
    done = long_steps * LONG

    def short_step(step, carry):
        add(done + step * SHORT, SHORT)
        return carry

    lax.fori_loop(0, (total - done + SHORT - 1) // SHORT, short_step, 0)

    for copy in handed_copies:
        copy.wait()
    if not with_edge:
        return

    lane = lanes((8, ROWS))

    def pack_edge(pair, carry):
        for c in range(2):
            edge = jnp.zeros((8, ROWS), f32)
            for k in range(16):
                last = rows_of(acc, c, k % 8, pair * 2 + k // 8, SIDE - 1)
                moved = pltpu.roll(last, 8 * k, 1) if k else last
                edge = jnp.where((lane >> 3) == k, moved, edge)
            right[c, pair] = edge
        return carry

    lax.fori_loop(0, SIDE // 2, pack_edge, 0)


def rows_of(acc, c, h, band, col):
    part = acc[FIRST + band * SIDE + col, pl.ds(16 * h + 8 * c, 8), :]
    if h == 0:
        part = part + acc[band * SIDE + col, pl.ds(2 * SUB + 8 * c, 8), :]
    return part


def fold_kernel(with_low, acc, out, first, *rest):
    low, rest = (rest[0], rest[1:]) if with_low else (None, rest)
    stage, out_sems = rest
    lane = lanes((8, ROWS))

    def copy_out(band):
        rows = pl.ds(band * SUB, SUB)
        return pltpu.make_async_copy(
            stage.at[:, rows, :], out.at[:, rows, pl.ds(ROWS, TILE - ROWS)], out_sems.at[band]
        )

    def fold(band, carry):
        for c in range(2):
            for h in range(8):
                before = jnp.zeros((8, ROWS), f32)
                for t in range(TILE // ROWS):
                    even = rows_of(acc, c, h, band, 2 * t)
                    odd = rows_of(acc, c, h, band, 2 * t + 1)
                    rows = pl.ds(band * SUB + 8 * h, 8)
                    columns = even + jnp.where(lane < SUB, before, odd)
                    if t == 0:
                        first[c, rows, :] = columns
                    else:
                        stage[c, rows, pl.ds((t - 1) * ROWS, ROWS)] = columns
                    before = odd
        copy_out(band).start()
        return carry

    lax.fori_loop(0, SIDE, fold, 0)
    if with_low:
        for c in range(2):
            before = jnp.zeros((8, ROWS), f32)
            for t in range(TILE // ROWS):
                rows = pl.ds(2 * SUB + 8 * c, 8)
                even = acc[FIRST + (SIDE - 1) * SIDE + 2 * t, rows, :]
                odd = acc[FIRST + (SIDE - 1) * SIDE + 2 * t + 1, rows, :]
                low[c, :, pl.ds(t * ROWS, ROWS)] = even + jnp.where(lane < SUB, before, odd)
                before = odd
            low[c, :, pl.ds(TILE, ROWS)] = jnp.where(lane < KW, before, 0.0)

    def finish(band, carry):
        copy_out(band).wait()
        return carry

    lax.fori_loop(0, SIDE, finish, 0)


def edge_kernel(edge, first, grid_in, grid_out, columns, out_sems):
    lane = lanes((8, ROWS))
    pairs = SIDE // 2

    def put(pair):
        rows = pl.ds(pair * 2 * SUB, 2 * SUB)
        return pltpu.make_async_copy(
            columns.at[:, rows, :], grid_out.at[:, rows, pl.ds(0, ROWS)], out_sems.at[pair]
        )

    def add(pair, carry):
        for c in range(2):
            packed = edge[c, pair]
            for k in range(16):
                moved = pltpu.roll(packed, ROWS - 8 * k, 1) if k else packed
                rows = pl.ds(pair * 2 * SUB + 8 * k, 8)
                columns[c, rows, :] = first[c, rows, :] + jnp.where(lane < KW, moved, 0.0)
        put(pair).start()
        return carry

    lax.fori_loop(0, pairs, add, 0)
    for pair in range(pairs):
        put(pair).wait()


def in_hbm(x):
    return pltpu.with_memory_space_constraint(x, pltpu.HBM)


def shifted(block, distance):
    tiles = ("half", "tile")
    devices = range(lax.axis_size(tiles))
    route = [(i - distance, i) for i in devices if i - distance in devices]
    return lax.ppermute(block, tiles, route)


def shards(visibilities, vis_weight, cell_index, tap_offsets, routes, patch_index, kernel):
    blocks = visibilities.shape[0]
    tile_count = lax.axis_size(("half", "tile"))
    plane_count = lax.axis_size("wp")
    peers = tile_count * plane_count
    cap = max(2, 2 * blocks // peers)
    rows = 3 * cap + 1
    vmem = pl.BlockSpec(memory_space=pltpu.VMEM)
    hbm = pl.BlockSpec(memory_space=pltpu.HBM)

    acc_shape = (max(DUMMY + 1, 6 * (blocks // 8)), ROW_BLOCK, ROWS)

    buckets, acc = pl.pallas_call(
        functools.partial(pack_kernel, peers, cap),
        out_shape=[jax.ShapeDtypeStruct((peers * rows, 1, ROWS), f32), pltpu.VMEM(acc_shape, f32)],
        in_specs=[hbm] * 6,
        out_specs=[vmem, vmem],
        scratch_shapes=[
            pltpu.SMEM((blocks,), jnp.int32),
            pltpu.SMEM((blocks,), jnp.int32),
            pltpu.VMEM((blocks, 2, ROWS), f32),
            pltpu.VMEM((blocks, ROWS), f32),
            pltpu.VMEM((blocks, ROWS), jnp.int32),
            pltpu.VMEM((blocks, ROWS), jnp.int32),
            pltpu.SMEM((peers, ROWS), jnp.int32),
            pltpu.VMEM((peers, ROWS), jnp.int32),
            pltpu.SMEM((blocks,), jnp.int32),
            pltpu.SMEM((peers,), jnp.int32),
            pltpu.SemaphoreType.DMA((7,)),
        ],
        compiler_params=pltpu.CompilerParams(vmem_limit_bytes=8 << 20),
        name="pack",
    )(*[in_hbm(x) for x in (routes[:, 0], patch_index, visibilities, vis_weight, cell_index, tap_offsets)])

    arrived = lax.all_to_all(buckets, ("tile", "wp"), split_axis=0, concat_axis=0, tiled=True)

    sources = peers // 2
    later = sources // 4
    across = [(0, 1), (1, 0)]
    far = arrived.reshape(sources, 2 * rows, 1, ROWS)[: sources - later, rows:]
    far = lax.ppermute(far.reshape((sources - later) * rows, 1, ROWS), "half", across)

    def add(name, part, sources, stride, acc, passed=0, with_edge=False):
        out_shape, out_specs = [pltpu.VMEM(acc_shape, f32)], [vmem]
        if with_edge:
            out_shape.append(jax.ShapeDtypeStruct((2, SIDE // 2, 8, ROWS), f32))
            out_specs.append(vmem)
        if passed:
            out_shape.append(jax.ShapeDtypeStruct((passed * rows, 1, ROWS), f32))
            out_specs.append(vmem)
        return pl.pallas_call(
            functools.partial(add_kernel, sources, cap, stride, passed, with_edge),
            out_shape=out_shape,
            in_specs=[hbm, vmem, vmem],
            out_specs=out_specs,
            scratch_shapes=[
                pltpu.VMEM((sources, ROWS), jnp.int32),
                pltpu.SMEM((sources, ROWS), jnp.int32),
                pltpu.SMEM((sources * cap + max(cap, SHORT),), jnp.int32),
                pltpu.SMEM((KW, OVER), f32),
                pltpu.SemaphoreType.DMA,
                pltpu.SemaphoreType.DMA,
                *([pltpu.SemaphoreType.DMA((passed,))] if passed else []),
            ],
            input_output_aliases={2: 0},
            compiler_params=pltpu.CompilerParams(vmem_limit_bytes=4 << 20),
            cost_estimate=pl.CostEstimate(flops=1 << 33, bytes_accessed=1 << 20, transcendentals=0),
            name=name,
        )(in_hbm(kernel.T), part, acc)

    acc, last = add("add_near", arrived, sources, 2 * rows, acc, passed=later)
    last = lax.ppermute(last, "half", across)
    (acc,) = add("add_far", far, sources - later, rows, acc)
    acc, right = add("add_last", last, later, rows, acc, with_edge=True)

    place = lax.axis_index(("half", "tile"))
    from_left = shifted(right, 1)

    with_low = tile_count > TCOLS
    out_shape = [jax.ShapeDtypeStruct((2, TILE, TILE), f32), jax.ShapeDtypeStruct((2, TILE, ROWS), f32)]
    out_specs = [hbm, vmem]
    if with_low:
        out_shape.append(jax.ShapeDtypeStruct((2, KW, TILE + ROWS), f32))
        out_specs.append(vmem)
    own, first, *low = pl.pallas_call(
        functools.partial(fold_kernel, with_low),
        out_shape=out_shape,
        in_specs=[vmem],
        out_specs=out_specs,
        scratch_shapes=[pltpu.VMEM((2, TILE, TILE - ROWS), f32), pltpu.SemaphoreType.DMA((SIDE,))],
        compiler_params=pltpu.CompilerParams(vmem_limit_bytes=12 << 20),
        cost_estimate=pl.CostEstimate(flops=1 << 22, bytes_accessed=16 << 20, transcendentals=0),
        name="fold",
    )(acc)

    if with_low:
        from_left = jnp.where(place % TCOLS == 0, 0.0, from_left)
    own = pl.pallas_call(
        edge_kernel,
        out_shape=jax.ShapeDtypeStruct((2, TILE, TILE), f32),
        in_specs=[vmem, vmem, hbm],
        out_specs=hbm,
        scratch_shapes=[
            pltpu.VMEM((2, TILE, ROWS), f32),
            pltpu.SemaphoreType.DMA((SIDE // 2,)),
        ],
        input_output_aliases={2: 0},
        compiler_params=pltpu.CompilerParams(vmem_limit_bytes=4 << 20),
        name="edges",
    )(from_left, first, own)
    if with_low:
        (low,) = low
        from_above = shifted(low, TCOLS)
        from_corner = shifted(low[:, :, TILE:], TCOLS + 1)
        from_corner = jnp.where(place % TCOLS == 0, 0.0, from_corner)
        own = own.at[:, :KW, :].add(from_above[:, :, :TILE])
        own = own.at[:, :KW, :ROWS].add(from_corner)
    return own.reshape(1, 1, 2, TILE, TILE)


def solution(mesh):
    tiles, planes = mesh.shape["tile"], mesh.shape["wp"]
    halves = jax.sharding.Mesh(mesh.devices.reshape(2, tiles // 2, planes), ("half", "tile", "wp"))
    every = ("half", "tile", "wp")
    in_specs = (
        P(every, None, None),
        P(every, None),
        P(every, None),
        P(every, None),
        P(every, None),
        P(every),
        P(),
    )
    out_specs = P("wp", ("half", "tile"), None, None, None)
    return jax.shard_map(shards, mesh=halves, in_specs=in_specs, out_specs=out_specs, check_vma=False)
```

```python
import functools

import jax
import jax.numpy as jnp
from jax import lax
from jax.experimental import pallas as pl
from jax.experimental.pallas import tpu as pltpu
from jax.sharding import PartitionSpec as P

TCOLS = 8
SUB = 64
KW = 8
OVER = 16
TILE = 1024
ROWS = 128
SIDE = TILE // SUB
PATCHES = SIDE * SIDE
ROW_BLOCK = 2 * (SUB + KW)
FIRST = SIDE
DUMMY = FIRST + PATCHES
WIDE = 80
LONG, SHORT = 64, 16

f32 = jnp.float32
bf16 = jnp.bfloat16


def lanes(shape):
    return lax.broadcasted_iota(jnp.int32, shape, len(shape) - 1)


def pack_kernel(peers, cap, routes, patch, vis, weight, cell, tap, kernel, out, acc, table, *scratch):
    routes_s, patch_s, vis_v, weight_v, cell_v, tap_v, kernel_s, meta, meta_v, place, sems = scratch
    blocks = vis.shape[0]
    rows = 3 * cap + 1
    sources = (routes, patch, vis, weight, cell, tap, kernel)
    targets = (routes_s, patch_s, vis_v, weight_v, cell_v, tap_v, kernel_s)
    copies = [pltpu.make_async_copy(a, b, sems.at[i]) for i, (a, b) in enumerate(zip(sources, targets))]
    for copy in copies:
        copy.start()

    steps = blocks // 8
    early = acc.shape[0] - 6 * steps

    def clear_accumulators(first, number):
        for i in range(number):
            acc[first + i] = jnp.zeros((ROW_BLOCK, ROWS), f32)

    def clear(d, carry):
        meta[d, cap] = 0
        return carry

    def clear_one(i, carry):
        clear_accumulators(i, 1)
        return carry

    lax.fori_loop(0, peers, clear, 0, unroll=8)
    lax.fori_loop(0, early, clear_one, 0)
    copies[0].wait()
    copies[1].wait()

    def choose(step):
        for i in range(8):
            b = step * 8 + i
            d = routes_s[b]
            k = meta[d, cap]
            meta[d, cap] = k + 1
            meta[d, k] = patch_s[b]
            place[b] = d * rows + 3 * k

    def move(step):
        first = pl.multiple_of(step * 8, 8)
        block_rows = pl.ds(first, 8)
        w = weight_v[block_rows, :]
        c = cell_v[block_rows, :]
        t = tap_v[block_rows, :]
        at_u = ((t >> 4) << 3) | ((c >> 6) & 7)
        at_v = ((t & 15) << 3) | (c & 7)
        code = (((c >> 9) << 17) | (((c >> 3) & 7) << 14) | (at_u << 7) | at_v).astype(f32)
        for i in range(8):
            row = place[first + i]
            both = vis_v[first + i] * w[i : i + 1, :]
            out[row] = both[0:1, :]
            out[row + 1] = both[1:2, :]
            out[row + 2] = code[i : i + 1, :]

    choose(0)
    for copy in copies[2:]:
        copy.wait()

    def both_steps(step, carry):
        clear_accumulators(early + 6 * step, 6)
        choose(step + 1)
        move(step)
        return carry

    lax.fori_loop(0, steps - 1, both_steps, 0)
    meta_copy = pltpu.make_async_copy(meta, meta_v, sems.at[7])
    meta_copy.start()
    clear_accumulators(early + 6 * (steps - 1), 6)
    move(steps - 1)
    table[...] = tap_table(kernel_s)
    meta_copy.wait()

    def put_meta(d, carry):
        out[d * rows + 3 * cap] = meta_v[pl.ds(d, 1), :].astype(f32)
        return carry

    lax.fori_loop(0, peers, put_meta, 0, unroll=8)


def split(x):
    hi = x.astype(bf16)
    return hi, (x - hi.astype(f32)).astype(bf16)


def twice(x):
    return jnp.concatenate([x, x], axis=0)


def look_up(table, index):
    numbers = lax.GatherDimensionNumbers(
        offset_dims=(),
        collapsed_slice_dims=(1,),
        start_index_map=(1,),
        operand_batching_dims=(0,),
        start_indices_batching_dims=(0,),
    )
    return lax.gather(
        table, index[..., None], numbers, (1, 1), mode=lax.GatherScatterMode.PROMISE_IN_BOUNDS
    )


def spread(picks, values):
    zero = jnp.zeros((16, ROWS), bf16)
    return [[jnp.where(pick, value, zero) for pick in picks] for value in values]


def patch_product(re, im, code, table):
    sub = lax.broadcasted_iota(jnp.int32, (8, ROWS), 0)
    at_v = code & 127
    at_u = (code >> 7) & 127
    ku = look_up(table, at_u)
    kv = look_up(table, at_v)
    group_u = ((code >> 17) & 7) + jnp.where(sub < (at_u & 7), 1, 0)
    group_v = ((code >> 14) & 7) + jnp.where(sub < (at_v & 7), 1, 0)
    step_u = twice(group_u.astype(f32)).astype(bf16)
    step_v = jnp.concatenate([group_v, group_v - 1], axis=0).astype(f32).astype(bf16)

    u_hi, u_lo = split(jnp.concatenate([re * ku, im * ku], axis=0))
    hi_rows, lo_rows = spread([step_u == float(g) for g in range(SUB // 8 + 1)], [u_hi, u_lo])
    left_hi, left_lo = jnp.concatenate(hi_rows, axis=0), jnp.concatenate(lo_rows, axis=0)
    left = jnp.concatenate([left_hi, left_lo, left_hi], axis=1)

    v_hi, v_lo = split(twice(kv))
    hi_rows, lo_rows = spread([step_v == 2.0 * g for g in range(WIDE // 16)], [v_hi, v_lo])
    right_hi, right_lo = jnp.concatenate(hi_rows, axis=0), jnp.concatenate(lo_rows, axis=0)
    right = jnp.concatenate([right_hi, right_hi, right_lo], axis=1)
    return lax.dot_general(left, right, (((1,), (1,)), ((), ())), preferred_element_type=f32)


def tap_table(kernel):
    sub = lax.broadcasted_iota(jnp.int32, (8, ROWS), 0)
    lane = lanes((8, ROWS))
    which_tap = (sub - lane) & 7
    which_level = lane >> 3
    table = jnp.zeros((8, ROWS), f32)
    for a in range(KW):
        row = jnp.zeros((8, ROWS), f32)
        for o in range(OVER):
            row = jnp.where(which_level == o, kernel[a, o], row)
        table = jnp.where(which_tap == a, row, table)
    return table


def add_kernel(peers, cap, table_ref, arrived, acc_in, acc, right, *scratch):
    meta_v, meta, slots, meta_sem = scratch
    rows = 3 * cap + 1
    lane_row = lanes((1, ROWS))

    def entries(s, carry):
        row = arrived[s * rows + 3 * cap].astype(jnp.int32)
        entry = (s * rows + 3 * lane_row) * 512 + (row + FIRST)
        meta_v[pl.ds(s, 1), :] = jnp.where(lane_row < cap, entry, row)
        return carry

    lax.fori_loop(0, peers, entries, 0, unroll=8)
    meta_copy = pltpu.make_async_copy(meta_v, meta, meta_sem)
    meta_copy.start()
    table = table_ref[...]
    meta_copy.wait()

    def gather_source(s, total):
        for k in range(cap):
            slots[total + k] = meta[s, k]
        return total + meta[s, cap]

    total = lax.fori_loop(0, peers, gather_source, 0, unroll=2)
    for k in range(SHORT):
        slots[total + k] = DUMMY

    def add(first, number):
        for i in range(number):
            entry = slots[first + i]
            row = entry >> 9
            where_to = entry & 511
            re = jnp.broadcast_to(arrived[row], (8, ROWS))
            im = jnp.broadcast_to(arrived[row + 1], (8, ROWS))
            code = jnp.broadcast_to(arrived[row + 2], (8, ROWS)).astype(jnp.int32)
            acc[where_to, :, :WIDE] += patch_product(re, im, code, table)

    def long_step(step, carry):
        add(step * LONG, LONG)
        return carry

    long_steps = total // LONG
    lax.fori_loop(0, long_steps, long_step, 0)
    done = long_steps * LONG

    def short_step(step, carry):
        add(done + step * SHORT, SHORT)
        return carry

    lax.fori_loop(0, (total - done + SHORT - 1) // SHORT, short_step, 0)

    lane = lanes((8, ROWS))

    def pack_edge(pair, carry):
        for c in range(2):
            edge = jnp.zeros((8, ROWS), f32)
            for k in range(16):
                last = rows_of(acc, c, k % 8, pair * 2 + k // 8, SIDE - 1)
                moved = pltpu.roll(last, (8 * k - SUB) % ROWS, 1) if k != 8 else last
                edge = jnp.where((lane >> 3) == k, moved, edge)
            right[c, pair] = edge
        return carry

    lax.fori_loop(0, SIDE // 2, pack_edge, 0)


def rows_of(acc, c, h, band, col):
    part = acc[FIRST + band * SIDE + col, pl.ds(16 * h + 8 * c, 8), :]
    if h == 0:
        part = part + acc[band * SIDE + col, pl.ds(2 * SUB + 8 * c, 8), :]
    return part


def fold_kernel(with_low, acc, out, first, *rest):
    low, rest = (rest[0], rest[1:]) if with_low else (None, rest)
    stage, out_sems = rest
    lane = lanes((8, ROWS))

    def copy_out(band):
        rows = pl.ds(band * SUB, SUB)
        return pltpu.make_async_copy(
            stage.at[:, rows, :], out.at[:, rows, pl.ds(ROWS, TILE - ROWS)], out_sems.at[band]
        )

    def fold(band, carry):
        for c in range(2):
            for h in range(8):
                before = jnp.zeros((8, ROWS), f32)
                for t in range(TILE // ROWS):
                    even = rows_of(acc, c, h, band, 2 * t)
                    odd = pltpu.roll(rows_of(acc, c, h, band, 2 * t + 1), SUB, 1)
                    rows = pl.ds(band * SUB + 8 * h, 8)
                    columns = even + jnp.where(lane < SUB, before, odd)
                    if t == 0:
                        first[c, rows, :] = columns
                    else:
                        stage[c, rows, pl.ds((t - 1) * ROWS, ROWS)] = columns
                    before = odd
        copy_out(band).start()
        return carry

    lax.fori_loop(0, SIDE, fold, 0)
    if with_low:
        for c in range(2):
            before = jnp.zeros((8, ROWS), f32)
            for t in range(TILE // ROWS):
                rows = pl.ds(2 * SUB + 8 * c, 8)
                even = acc[FIRST + (SIDE - 1) * SIDE + 2 * t, rows, :]
                odd = pltpu.roll(acc[FIRST + (SIDE - 1) * SIDE + 2 * t + 1, rows, :], SUB, 1)
                low[c, :, pl.ds(t * ROWS, ROWS)] = even + jnp.where(lane < SUB, before, odd)
                before = odd
            low[c, :, pl.ds(TILE, ROWS)] = jnp.where(lane < KW, before, 0.0)

    def finish(band, carry):
        copy_out(band).wait()
        return carry

    lax.fori_loop(0, SIDE, finish, 0)


def edge_kernel(edge, first, grid_in, grid_out, columns, out_sems):
    lane = lanes((8, ROWS))
    pairs = SIDE // 2

    def put(pair):
        rows = pl.ds(pair * 2 * SUB, 2 * SUB)
        return pltpu.make_async_copy(
            columns.at[:, rows, :], grid_out.at[:, rows, pl.ds(0, ROWS)], out_sems.at[pair]
        )

    def add(pair, carry):
        for c in range(2):
            packed = edge[c, pair]
            for k in range(16):
                moved = pltpu.roll(packed, ROWS - 8 * k, 1) if k else packed
                rows = pl.ds(pair * 2 * SUB + 8 * k, 8)
                columns[c, rows, :] = first[c, rows, :] + jnp.where(lane < KW, moved, 0.0)
        put(pair).start()
        return carry

    lax.fori_loop(0, pairs, add, 0)
    for pair in range(pairs):
        put(pair).wait()


def in_hbm(x):
    return pltpu.with_memory_space_constraint(x, pltpu.HBM)


def shifted(block, axis, distance):
    devices = range(lax.axis_size(axis))
    route = [(i - distance, i) for i in devices if i - distance in devices]
    return lax.ppermute(block, axis, route)


def shards(visibilities, vis_weight, cell_index, tap_offsets, routes, patch_index, kernel):
    blocks = visibilities.shape[0]
    tile_count = lax.axis_size("tile")
    plane_count = lax.axis_size("wp")
    peers = tile_count * plane_count
    cap = max(2, 2 * blocks // peers)
    rows = 3 * cap + 1
    vmem = pl.BlockSpec(memory_space=pltpu.VMEM)
    hbm = pl.BlockSpec(memory_space=pltpu.HBM)

    acc_shape = (max(DUMMY + 1, 6 * (blocks // 8)), ROW_BLOCK, ROWS)

    buckets, acc, table = pl.pallas_call(
        functools.partial(pack_kernel, peers, cap),
        out_shape=[jax.ShapeDtypeStruct((peers * rows, 1, ROWS), f32), pltpu.VMEM(acc_shape, f32), pltpu.VMEM((8, ROWS), f32)],
        in_specs=[hbm] * 7,
        out_specs=[vmem] * 3,
        scratch_shapes=[
            pltpu.SMEM((blocks,), jnp.int32),
            pltpu.SMEM((blocks,), jnp.int32),
            pltpu.VMEM((blocks, 2, ROWS), f32),
            pltpu.VMEM((blocks, ROWS), f32),
            pltpu.VMEM((blocks, ROWS), jnp.int32),
            pltpu.VMEM((blocks, ROWS), jnp.int32),
            pltpu.SMEM((KW, OVER), f32),
            pltpu.SMEM((peers, ROWS), jnp.int32),
            pltpu.VMEM((peers, ROWS), jnp.int32),
            pltpu.SMEM((blocks,), jnp.int32),
            pltpu.SemaphoreType.DMA((8,)),
        ],
        compiler_params=pltpu.CompilerParams(vmem_limit_bytes=8 << 20),
        name="pack",
    )(*[in_hbm(x) for x in (routes[:, 0], patch_index, visibilities, vis_weight, cell_index, tap_offsets, kernel.T)])

    arrived = lax.all_to_all(buckets, ("tile", "wp"), split_axis=0, concat_axis=0, tiled=True)

    acc, right = pl.pallas_call(
        functools.partial(add_kernel, peers, cap),
        out_shape=[pltpu.VMEM(acc_shape, f32), jax.ShapeDtypeStruct((2, SIDE // 2, 8, ROWS), f32)],
        in_specs=[vmem, vmem, vmem],
        out_specs=[vmem, vmem],
        scratch_shapes=[
            pltpu.VMEM((peers, ROWS), jnp.int32),
            pltpu.SMEM((peers, ROWS), jnp.int32),
            pltpu.SMEM((peers * cap + max(cap, SHORT),), jnp.int32),
            pltpu.SemaphoreType.DMA,
        ],
        input_output_aliases={2: 0},
        compiler_params=pltpu.CompilerParams(vmem_limit_bytes=4 << 20),
        name="add",
    )(table, arrived, acc)

    place = lax.axis_index("tile")
    from_left = shifted(right, "tile", 1)

    with_low = tile_count > TCOLS
    out_shape = [jax.ShapeDtypeStruct((2, TILE, TILE), f32), jax.ShapeDtypeStruct((2, TILE, ROWS), f32)]
    out_specs = [hbm, vmem]
    if with_low:
        out_shape.append(jax.ShapeDtypeStruct((2, KW, TILE + ROWS), f32))
        out_specs.append(vmem)
    own, first, *low = pl.pallas_call(
        functools.partial(fold_kernel, with_low),
        out_shape=out_shape,
        in_specs=[vmem],
        out_specs=out_specs,
        scratch_shapes=[pltpu.VMEM((2, TILE, TILE - ROWS), f32), pltpu.SemaphoreType.DMA((SIDE,))],
        compiler_params=pltpu.CompilerParams(vmem_limit_bytes=12 << 20),
        cost_estimate=pl.CostEstimate(flops=1 << 22, bytes_accessed=16 << 20, transcendentals=0),
        name="fold",
    )(acc)

    if with_low:
        from_left = jnp.where(place % TCOLS == 0, 0.0, from_left)
    own = pl.pallas_call(
        edge_kernel,
        out_shape=jax.ShapeDtypeStruct((2, TILE, TILE), f32),
        in_specs=[vmem, vmem, hbm],
        out_specs=hbm,
        scratch_shapes=[
            pltpu.VMEM((2, TILE, ROWS), f32),
            pltpu.SemaphoreType.DMA((SIDE // 2,)),
        ],
        input_output_aliases={2: 0},
        compiler_params=pltpu.CompilerParams(vmem_limit_bytes=4 << 20),
        name="edges",
    )(from_left, first, own)
    if with_low:
        (low,) = low
        from_above = shifted(low, "tile", TCOLS)
        from_corner = shifted(low[:, :, TILE:], "tile", TCOLS + 1)
        from_corner = jnp.where(place % TCOLS == 0, 0.0, from_corner)
        own = own.at[:, :KW, :].add(from_above[:, :, :TILE])
        own = own.at[:, :KW, :ROWS].add(from_corner)
    return own.reshape(1, 1, 2, TILE, TILE)


def solution(mesh):
    in_specs = (
        P(("tile", "wp"), None, None),
        P(("tile", "wp"), None),
        P(("tile", "wp"), None),
        P(("tile", "wp"), None),
        P(("tile", "wp"), None),
        P(("tile", "wp")),
        P(),
    )
    out_specs = P("wp", "tile", None, None, None)
    return jax.shard_map(shards, mesh=mesh, in_specs=in_specs, out_specs=out_specs, check_vma=False)
```

```python
import functools

import jax
import jax.numpy as jnp
from jax import lax
from jax.experimental import pallas as pl
from jax.experimental.pallas import tpu as pltpu
from jax.sharding import PartitionSpec as P

TCOLS = 8
SUB = 64
KW = 8
OVER = 16
TILE = 1024
ROWS = 128
SIDE = TILE // SUB
PATCHES = SIDE * SIDE
ROW_BLOCK = SUB + KW
FIRST = SIDE
DUMMY = FIRST + PATCHES
LONG, SHORT = 64, 16

f32 = jnp.float32
bf16 = jnp.bfloat16


def lanes(shape):
    return lax.broadcasted_iota(jnp.int32, shape, len(shape) - 1)


def pack_kernel(peers, cap, routes, patch, vis, weight, cell, tap, out, acc, *scratch):
    routes_s, patch_s, vis_v, weight_v, cell_v, tap_v, meta, meta_v, place, sems = scratch
    blocks = vis.shape[0]
    rows = 3 * cap + 1
    sources = (routes, patch, vis, weight, cell, tap)
    targets = (routes_s, patch_s, vis_v, weight_v, cell_v, tap_v)
    copies = [pltpu.make_async_copy(a, b, sems.at[i]) for i, (a, b) in enumerate(zip(sources, targets))]
    for copy in copies:
        copy.start()

    steps = blocks // 8
    early = acc.shape[0] - 6 * steps

    def clear_accumulators(first, number):
        for i in range(number):
            acc[first + i] = jnp.zeros((ROW_BLOCK, 2 * ROWS), f32)

    def clear(d, carry):
        meta[d, cap] = 0
        return carry

    def clear_one(i, carry):
        clear_accumulators(i, 1)
        return carry

    lax.fori_loop(0, peers, clear, 0, unroll=8)
    lax.fori_loop(0, early, clear_one, 0)
    copies[0].wait()
    copies[1].wait()

    def choose(step, carry):
        clear_accumulators(early + 4 * step, 4)
        for i in range(8):
            b = step * 8 + i
            d = routes_s[b]
            k = meta[d, cap]
            meta[d, cap] = k + 1
            meta[d, k] = patch_s[b]
            place[b] = d * rows + 3 * k
        return carry

    lax.fori_loop(0, steps, choose, 0)
    meta_copy = pltpu.make_async_copy(meta, meta_v, sems.at[6])
    meta_copy.start()
    for copy in copies[2:]:
        copy.wait()

    def move(step, carry):
        clear_accumulators(early + 4 * steps + 2 * step, 2)
        first = pl.multiple_of(step * 8, 8)
        block_rows = pl.ds(first, 8)
        w = weight_v[block_rows, :]
        c = cell_v[block_rows, :]
        t = tap_v[block_rows, :]
        at_u = ((t >> 4) << 3) | ((c >> 6) & 7)
        at_v = ((t & 15) << 3) | (c & 7)
        code = (((c >> 9) << 17) | (((c >> 3) & 7) << 14) | (at_u << 7) | at_v).astype(f32)
        for i in range(8):
            row = place[first + i]
            both = vis_v[first + i] * w[i : i + 1, :]
            out[row] = both[0:1, :]
            out[row + 1] = both[1:2, :]
            out[row + 2] = code[i : i + 1, :]
        return carry

    lax.fori_loop(0, steps, move, 0)
    meta_copy.wait()

    def put_meta(d, carry):
        out[d * rows + 3 * cap] = meta_v[pl.ds(d, 1), :].astype(f32)
        return carry

    lax.fori_loop(0, peers, put_meta, 0, unroll=8)


def split(x):
    hi = x.astype(bf16)
    return hi, (x - hi.astype(f32)).astype(bf16)


def twice(x):
    return jnp.concatenate([x, x], axis=0)


def look_up(table, index):
    numbers = lax.GatherDimensionNumbers(
        offset_dims=(),
        collapsed_slice_dims=(1,),
        start_index_map=(1,),
        operand_batching_dims=(0,),
        start_indices_batching_dims=(0,),
    )
    return lax.gather(
        table, index[..., None], numbers, (1, 1), mode=lax.GatherScatterMode.PROMISE_IN_BOUNDS
    )


def spread(picks, values):
    zero = jnp.zeros((16, ROWS), bf16)
    return [[jnp.where(pick, value, zero) for pick in picks] for value in values]


def patch_product(re, im, code, parity, table):
    sub = lax.broadcasted_iota(jnp.int32, (8, ROWS), 0)
    at_v = code & 127
    at_u = (code >> 7) & 127
    ku = look_up(table, at_u)
    kv = look_up(table, at_v)
    group_u = ((code >> 17) & 7) + jnp.where(sub < (at_u & 7), 1, 0)
    group_v = ((code >> 14) & 7) + jnp.where(sub < (at_v & 7), 1, 0) + 8 * parity
    step_u = jnp.concatenate([group_u, group_u - 1], axis=0).astype(f32).astype(bf16)
    step_v = jnp.concatenate([group_v & 15, (group_v + 15) & 15], axis=0).astype(f32).astype(bf16)

    hi_rows, lo_rows = spread([step_u == 2.0 * g for g in range(ROW_BLOCK // 16 + 1)], split(twice(ku)))
    left_hi, left_lo = jnp.concatenate(hi_rows, axis=0), jnp.concatenate(lo_rows, axis=0)
    left = jnp.concatenate([left_hi, left_lo, left_hi], axis=1)

    picks = [step_v == 2.0 * g for g in range(ROWS // 16)]
    re_hi, re_lo = spread(picks, split(twice(re * kv)))
    im_hi, im_lo = spread(picks, split(twice(im * kv)))
    right_hi, right_lo = jnp.concatenate(re_hi + im_hi, axis=0), jnp.concatenate(re_lo + im_lo, axis=0)
    right = jnp.concatenate([right_hi, right_hi, right_lo], axis=1)
    product = lax.dot_general(left, right, (((1,), (1,)), ((), ())), preferred_element_type=f32)
    return product[:ROW_BLOCK]


def tap_table(kernel):
    sub = lax.broadcasted_iota(jnp.int32, (8, ROWS), 0)
    lane = lanes((8, ROWS))
    which_tap = (sub - lane) & 7
    which_level = lane >> 3
    table = jnp.zeros((8, ROWS), f32)
    for a in range(KW):
        row = jnp.zeros((8, ROWS), f32)
        for o in range(OVER):
            row = jnp.where(which_level == o, kernel[a, o], row)
        table = jnp.where(which_tap == a, row, table)
    return table


def add_kernel(peers, cap, kernel, arrived, acc_in, acc, right, *scratch):
    meta_v, meta, slots, kernel_s, meta_sem, kernel_sem = scratch
    rows = 3 * cap + 1
    kernel_copy = pltpu.make_async_copy(kernel, kernel_s, kernel_sem)
    kernel_copy.start()
    lane_row = lanes((1, ROWS))

    def entries(s, carry):
        row = arrived[s * rows + 3 * cap].astype(jnp.int32)
        entry = (s * rows + 3 * lane_row) * 512 + (row + FIRST)
        meta_v[pl.ds(s, 1), :] = jnp.where(lane_row < cap, entry, row)
        return carry

    lax.fori_loop(0, peers, entries, 0, unroll=8)
    meta_copy = pltpu.make_async_copy(meta_v, meta, meta_sem)
    meta_copy.start()
    kernel_copy.wait()
    table = tap_table(kernel_s)
    meta_copy.wait()

    def gather_source(s, total):
        for k in range(cap):
            slots[total + k] = meta[s, k]
        return total + meta[s, cap]

    total = lax.fori_loop(0, peers, gather_source, 0, unroll=2)
    for k in range(SHORT):
        slots[total + k] = DUMMY

    def add(first, number):
        for i in range(number):
            entry = slots[first + i]
            row = entry >> 9
            where_to = entry & 511
            re = jnp.broadcast_to(arrived[row], (8, ROWS))
            im = jnp.broadcast_to(arrived[row + 1], (8, ROWS))
            code = jnp.broadcast_to(arrived[row + 2], (8, ROWS)).astype(jnp.int32)
            acc[where_to] += patch_product(re, im, code, entry & 1, table)

    def long_step(step, carry):
        add(step * LONG, LONG)
        return carry

    long_steps = total // LONG
    lax.fori_loop(0, long_steps, long_step, 0)
    done = long_steps * LONG

    def short_step(step, carry):
        add(done + step * SHORT, SHORT)
        return carry

    lax.fori_loop(0, (total - done + SHORT - 1) // SHORT, short_step, 0)

    lane = lanes((8, ROWS))

    def pack_edge(pair, carry):
        for c in range(2):
            edge = jnp.zeros((8, ROWS), f32)
            for k in range(16):
                last = rows_of(acc, c, k % 8, pair * 2 + k // 8, SIDE - 1)
                moved = pltpu.roll(last, 8 * k, 1) if k else last
                edge = jnp.where((lane >> 3) == k, moved, edge)
            right[c, pair] = edge
        return carry

    lax.fori_loop(0, SIDE // 2, pack_edge, 0)


def rows_of(acc, c, h, band, col):
    columns = pl.ds(c * ROWS, ROWS)
    part = acc[FIRST + band * SIDE + col, pl.ds(8 * h, 8), columns]
    if h == 0:
        part = part + acc[band * SIDE + col, pl.ds(SUB, 8), columns]
    return part


def fold_kernel(with_low, acc, out, first, *rest):
    low, rest = (rest[0], rest[1:]) if with_low else (None, rest)
    stage, out_sems = rest
    lane = lanes((8, ROWS))

    def copy_out(band):
        rows = pl.ds(band * SUB, SUB)
        return pltpu.make_async_copy(
            stage.at[:, rows, :], out.at[:, rows, pl.ds(ROWS, TILE - ROWS)], out_sems.at[band]
        )

    def fold(band, carry):
        for c in range(2):
            for h in range(8):
                before = jnp.zeros((8, ROWS), f32)
                for t in range(TILE // ROWS):
                    even = rows_of(acc, c, h, band, 2 * t)
                    odd = rows_of(acc, c, h, band, 2 * t + 1)
                    rows = pl.ds(band * SUB + 8 * h, 8)
                    columns = even + jnp.where(lane < SUB, before, odd)
                    if t == 0:
                        first[c, rows, :] = columns
                    else:
                        stage[c, rows, pl.ds((t - 1) * ROWS, ROWS)] = columns
                    before = odd
        copy_out(band).start()
        return carry

    lax.fori_loop(0, SIDE, fold, 0)
    if with_low:
        for c in range(2):
            before = jnp.zeros((8, ROWS), f32)
            for t in range(TILE // ROWS):
                rows, columns = pl.ds(SUB, 8), pl.ds(c * ROWS, ROWS)
                even = acc[FIRST + (SIDE - 1) * SIDE + 2 * t, rows, columns]
                odd = acc[FIRST + (SIDE - 1) * SIDE + 2 * t + 1, rows, columns]
                low[c, :, pl.ds(t * ROWS, ROWS)] = even + jnp.where(lane < SUB, before, odd)
                before = odd
            low[c, :, pl.ds(TILE, ROWS)] = jnp.where(lane < KW, before, 0.0)

    def finish(band, carry):
        copy_out(band).wait()
        return carry

    lax.fori_loop(0, SIDE, finish, 0)


def edge_kernel(edge, first, grid_in, grid_out, columns, out_sems):
    lane = lanes((8, ROWS))
    pairs = SIDE // 2

    def put(pair):
        rows = pl.ds(pair * 2 * SUB, 2 * SUB)
        return pltpu.make_async_copy(
            columns.at[:, rows, :], grid_out.at[:, rows, pl.ds(0, ROWS)], out_sems.at[pair]
        )

    def add(pair, carry):
        for c in range(2):
            packed = edge[c, pair]
            for k in range(16):
                moved = pltpu.roll(packed, ROWS - 8 * k, 1) if k else packed
                rows = pl.ds(pair * 2 * SUB + 8 * k, 8)
                columns[c, rows, :] = first[c, rows, :] + jnp.where(lane < KW, moved, 0.0)
        put(pair).start()
        return carry

    lax.fori_loop(0, pairs, add, 0)
    for pair in range(pairs):
        put(pair).wait()


def in_hbm(x):
    return pltpu.with_memory_space_constraint(x, pltpu.HBM)


def shifted(block, axis, distance):
    devices = range(lax.axis_size(axis))
    route = [(i - distance, i) for i in devices if i - distance in devices]
    return lax.ppermute(block, axis, route)


def shards(visibilities, vis_weight, cell_index, tap_offsets, routes, patch_index, kernel):
    blocks = visibilities.shape[0]
    tile_count = lax.axis_size("tile")
    plane_count = lax.axis_size("wp")
    peers = tile_count * plane_count
    cap = max(2, 2 * blocks // peers)
    rows = 3 * cap + 1
    vmem = pl.BlockSpec(memory_space=pltpu.VMEM)
    hbm = pl.BlockSpec(memory_space=pltpu.HBM)

    acc_shape = (max(DUMMY + 1, 6 * (blocks // 8)), ROW_BLOCK, 2 * ROWS)

    buckets, acc = pl.pallas_call(
        functools.partial(pack_kernel, peers, cap),
        out_shape=[jax.ShapeDtypeStruct((peers * rows, 1, ROWS), f32), pltpu.VMEM(acc_shape, f32)],
        in_specs=[hbm] * 6,
        out_specs=[vmem, vmem],
        scratch_shapes=[
            pltpu.SMEM((blocks,), jnp.int32),
            pltpu.SMEM((blocks,), jnp.int32),
            pltpu.VMEM((blocks, 2, ROWS), f32),
            pltpu.VMEM((blocks, ROWS), f32),
            pltpu.VMEM((blocks, ROWS), jnp.int32),
            pltpu.VMEM((blocks, ROWS), jnp.int32),
            pltpu.SMEM((peers, ROWS), jnp.int32),
            pltpu.VMEM((peers, ROWS), jnp.int32),
            pltpu.SMEM((blocks,), jnp.int32),
            pltpu.SemaphoreType.DMA((7,)),
        ],
        compiler_params=pltpu.CompilerParams(vmem_limit_bytes=8 << 20),
        name="pack",
    )(*[in_hbm(x) for x in (routes[:, 0], patch_index, visibilities, vis_weight, cell_index, tap_offsets)])

    arrived = lax.all_to_all(buckets, ("tile", "wp"), split_axis=0, concat_axis=0, tiled=True)

    acc, right = pl.pallas_call(
        functools.partial(add_kernel, peers, cap),
        out_shape=[pltpu.VMEM(acc_shape, f32), jax.ShapeDtypeStruct((2, SIDE // 2, 8, ROWS), f32)],
        in_specs=[hbm, vmem, vmem],
        out_specs=[vmem, vmem],
        scratch_shapes=[
            pltpu.VMEM((peers, ROWS), jnp.int32),
            pltpu.SMEM((peers, ROWS), jnp.int32),
            pltpu.SMEM((peers * cap + max(cap, SHORT),), jnp.int32),
            pltpu.SMEM((KW, OVER), f32),
            pltpu.SemaphoreType.DMA,
            pltpu.SemaphoreType.DMA,
        ],
        input_output_aliases={2: 0},
        compiler_params=pltpu.CompilerParams(vmem_limit_bytes=4 << 20),
        name="add",
    )(in_hbm(kernel.T), arrived, acc)

    place = lax.axis_index("tile")
    from_left = shifted(right, "tile", 1)

    with_low = tile_count > TCOLS
    out_shape = [jax.ShapeDtypeStruct((2, TILE, TILE), f32), jax.ShapeDtypeStruct((2, TILE, ROWS), f32)]
    out_specs = [hbm, vmem]
    if with_low:
        out_shape.append(jax.ShapeDtypeStruct((2, KW, TILE + ROWS), f32))
        out_specs.append(vmem)
    own, first, *low = pl.pallas_call(
        functools.partial(fold_kernel, with_low),
        out_shape=out_shape,
        in_specs=[vmem],
        out_specs=out_specs,
        scratch_shapes=[pltpu.VMEM((2, TILE, TILE - ROWS), f32), pltpu.SemaphoreType.DMA((SIDE,))],
        compiler_params=pltpu.CompilerParams(vmem_limit_bytes=12 << 20),
        cost_estimate=pl.CostEstimate(flops=1 << 22, bytes_accessed=16 << 20, transcendentals=0),
        name="fold",
    )(acc)

    if with_low:
        from_left = jnp.where(place % TCOLS == 0, 0.0, from_left)
    own = pl.pallas_call(
        edge_kernel,
        out_shape=jax.ShapeDtypeStruct((2, TILE, TILE), f32),
        in_specs=[vmem, vmem, hbm],
        out_specs=hbm,
        scratch_shapes=[
            pltpu.VMEM((2, TILE, ROWS), f32),
            pltpu.SemaphoreType.DMA((SIDE // 2,)),
        ],
        input_output_aliases={2: 0},
        compiler_params=pltpu.CompilerParams(vmem_limit_bytes=4 << 20),
        name="edges",
    )(from_left, first, own)
    if with_low:
        (low,) = low
        from_above = shifted(low, "tile", TCOLS)
        from_corner = shifted(low[:, :, TILE:], "tile", TCOLS + 1)
        from_corner = jnp.where(place % TCOLS == 0, 0.0, from_corner)
        own = own.at[:, :KW, :].add(from_above[:, :, :TILE])
        own = own.at[:, :KW, :ROWS].add(from_corner)
    return own.reshape(1, 1, 2, TILE, TILE)


def solution(mesh):
    in_specs = (
        P(("tile", "wp"), None, None),
        P(("tile", "wp"), None),
        P(("tile", "wp"), None),
        P(("tile", "wp"), None),
        P(("tile", "wp"), None),
        P(("tile", "wp")),
        P(),
    )
    out_specs = P("wp", "tile", None, None, None)
    return jax.shard_map(shards, mesh=mesh, in_specs=in_specs, out_specs=out_specs, check_vma=False)
```

```python
import functools

import jax
import jax.numpy as jnp
from jax import lax
from jax.experimental import pallas as pl
from jax.experimental.pallas import tpu as pltpu
from jax.sharding import PartitionSpec as P

TCOLS = 8
SUB = 64
KW = 8
OVER = 16
TILE = 1024
ROWS = 128
SIDE = TILE // SUB
PATCHES = SIDE * SIDE
ROW_BLOCK = 2 * (SUB + KW)
FIRST = SIDE
DUMMY = FIRST + PATCHES
LONG, SHORT = 64, 16

f32 = jnp.float32
bf16 = jnp.bfloat16


def lanes(shape):
    return lax.broadcasted_iota(jnp.int32, shape, len(shape) - 1)


def pack_kernel(peers, cap, routes, patch, vis, weight, cell, tap, out, acc, *scratch):
    routes_s, patch_s, vis_v, weight_v, cell_v, tap_v, meta, meta_v, place, sems = scratch
    blocks = vis.shape[0]
    rows = 3 * cap + 1
    sources = (routes, patch, vis, weight, cell, tap)
    targets = (routes_s, patch_s, vis_v, weight_v, cell_v, tap_v)
    copies = [pltpu.make_async_copy(a, b, sems.at[i]) for i, (a, b) in enumerate(zip(sources, targets))]
    for copy in copies:
        copy.start()

    steps = blocks // 8
    early = acc.shape[0] - 6 * steps

    def clear_accumulators(first, number):
        for i in range(number):
            acc[first + i] = jnp.zeros((ROW_BLOCK, ROWS), f32)

    def clear(d, carry):
        meta[d, cap] = 0
        return carry

    def clear_one(i, carry):
        clear_accumulators(i, 1)
        return carry

    lax.fori_loop(0, peers, clear, 0, unroll=8)
    lax.fori_loop(0, early, clear_one, 0)
    copies[0].wait()
    copies[1].wait()

    def choose(step, carry):
        clear_accumulators(early + 4 * step, 4)
        for i in range(8):
            b = step * 8 + i
            d = routes_s[b]
            k = meta[d, cap]
            meta[d, cap] = k + 1
            meta[d, k] = patch_s[b]
            place[b] = d * rows + 3 * k
        return carry

    lax.fori_loop(0, steps, choose, 0)
    meta_copy = pltpu.make_async_copy(meta, meta_v, sems.at[6])
    meta_copy.start()
    for copy in copies[2:]:
        copy.wait()

    def move(step, carry):
        clear_accumulators(early + 4 * steps + 2 * step, 2)
        first = pl.multiple_of(step * 8, 8)
        block_rows = pl.ds(first, 8)
        w = weight_v[block_rows, :]
        c = cell_v[block_rows, :]
        t = tap_v[block_rows, :]
        at_u = ((t >> 4) << 3) | ((c >> 6) & 7)
        at_v = ((t & 15) << 3) | (c & 7)
        code = (((c >> 9) << 17) | (((c >> 3) & 7) << 14) | (at_u << 7) | at_v).astype(f32)
        for i in range(8):
            row = place[first + i]
            both = vis_v[first + i] * w[i : i + 1, :]
            out[row] = both[0:1, :]
            out[row + 1] = both[1:2, :]
            out[row + 2] = code[i : i + 1, :]
        return carry

    lax.fori_loop(0, steps, move, 0)
    meta_copy.wait()

    def put_meta(d, carry):
        out[d * rows + 3 * cap] = meta_v[pl.ds(d, 1), :].astype(f32)
        return carry

    lax.fori_loop(0, peers, put_meta, 0, unroll=8)


def split(x):
    hi = x.astype(bf16)
    return hi, (x - hi.astype(f32)).astype(bf16)


def twice(x):
    return jnp.concatenate([x, x], axis=0)


def look_up(table, index):
    numbers = lax.GatherDimensionNumbers(
        offset_dims=(),
        collapsed_slice_dims=(1,),
        start_index_map=(1,),
        operand_batching_dims=(0,),
        start_indices_batching_dims=(0,),
    )
    return lax.gather(
        table, index[..., None], numbers, (1, 1), mode=lax.GatherScatterMode.PROMISE_IN_BOUNDS
    )


def spread(picks, values):
    zero = jnp.zeros((16, ROWS), bf16)
    return [[jnp.where(pick, value, zero) for pick in picks] for value in values]


def patch_product(re, im, code, parity, table, wide):
    sub = lax.broadcasted_iota(jnp.int32, (8, ROWS), 0)
    at_v = code & 127
    at_u = (code >> 7) & 127
    ku = look_up(table, at_u)
    kv = look_up(table, at_v)
    group_u = ((code >> 17) & 7) + jnp.where(sub < (at_u & 7), 1, 0)
    group_v = ((code >> 14) & 7) + jnp.where(sub < (at_v & 7), 1, 0) + 8 * parity
    step_u = twice(group_u.astype(f32)).astype(bf16)
    step_v = jnp.concatenate([group_v & 15, (group_v + 15) & 15], axis=0).astype(f32).astype(bf16)

    u_hi, u_lo = split(jnp.concatenate([re * ku, im * ku], axis=0))
    hi_rows, lo_rows = spread([step_u == float(g) for g in range(SUB // 8 + 1)], [u_hi, u_lo])
    left_hi, left_lo = jnp.concatenate(hi_rows, axis=0), jnp.concatenate(lo_rows, axis=0)
    v_hi, v_lo = split(twice(kv))
    hi_rows, lo_rows = spread([step_v == 2.0 * g for g in range(ROWS // 16)], [v_hi, v_lo])
    right_hi, right_lo = jnp.concatenate(hi_rows, axis=0), jnp.concatenate(lo_rows, axis=0)

    if wide:
        left = jnp.concatenate([left_hi, left_lo], axis=1)
        right = jnp.concatenate([right_hi, right_lo], axis=0)
        right = jnp.concatenate([right, right], axis=1)
    else:
        left = jnp.concatenate([left_hi, left_lo], axis=0)
        left = jnp.concatenate([left, left], axis=1)
        right = jnp.concatenate([right_hi, right_lo], axis=1)
    product = lax.dot_general(left, right, (((1,), (1,)), ((), ())), preferred_element_type=f32)
    if wide:
        return product[:, :ROWS] + product[:, ROWS:]
    return product[:ROW_BLOCK] + product[ROW_BLOCK:]


def tap_table(kernel):
    sub = lax.broadcasted_iota(jnp.int32, (8, ROWS), 0)
    lane = lanes((8, ROWS))
    which_tap = (sub - lane) & 7
    which_level = lane >> 3
    table = jnp.zeros((8, ROWS), f32)
    for a in range(KW):
        row = jnp.zeros((8, ROWS), f32)
        for o in range(OVER):
            row = jnp.where(which_level == o, kernel[a, o], row)
        table = jnp.where(which_tap == a, row, table)
    return table


def add_kernel(peers, cap, kernel, arrived, acc_in, acc, right, *scratch):
    meta_v, meta, slots, kernel_s, meta_sem, kernel_sem = scratch
    rows = 3 * cap + 1
    kernel_copy = pltpu.make_async_copy(kernel, kernel_s, kernel_sem)
    kernel_copy.start()
    lane_row = lanes((1, ROWS))

    def entries(s, carry):
        row = arrived[s * rows + 3 * cap].astype(jnp.int32)
        entry = (s * rows + 3 * lane_row) * 512 + (row + FIRST)
        meta_v[pl.ds(s, 1), :] = jnp.where(lane_row < cap, entry, row)
        return carry

    lax.fori_loop(0, peers, entries, 0, unroll=8)
    meta_copy = pltpu.make_async_copy(meta_v, meta, meta_sem)
    meta_copy.start()
    kernel_copy.wait()
    table = tap_table(kernel_s)
    meta_copy.wait()

    def gather_source(s, total):
        for k in range(cap):
            slots[total + k] = meta[s, k]
        return total + meta[s, cap]

    total = lax.fori_loop(0, peers, gather_source, 0, unroll=2)
    for k in range(SHORT):
        slots[total + k] = DUMMY

    def add(first, number):
        for i in range(number):
            entry = slots[first + i]
            row = entry >> 9
            where_to = entry & 511
            re = jnp.broadcast_to(arrived[row], (8, ROWS))
            im = jnp.broadcast_to(arrived[row + 1], (8, ROWS))
            code = jnp.broadcast_to(arrived[row + 2], (8, ROWS)).astype(jnp.int32)
            acc[where_to] += patch_product(re, im, code, entry & 1, table, i % 4 < 2)

    def long_step(step, carry):
        add(step * LONG, LONG)
        return carry

    long_steps = total // LONG
    lax.fori_loop(0, long_steps, long_step, 0)
    done = long_steps * LONG

    def short_step(step, carry):
        add(done + step * SHORT, SHORT)
        return carry

    lax.fori_loop(0, (total - done + SHORT - 1) // SHORT, short_step, 0)

    lane = lanes((8, ROWS))

    def pack_edge(pair, carry):
        for c in range(2):
            edge = jnp.zeros((8, ROWS), f32)
            for k in range(16):
                last = rows_of(acc, c, k % 8, pair * 2 + k // 8, SIDE - 1)
                moved = pltpu.roll(last, 8 * k, 1) if k else last
                edge = jnp.where((lane >> 3) == k, moved, edge)
            right[c, pair] = edge
        return carry

    lax.fori_loop(0, SIDE // 2, pack_edge, 0)


def rows_of(acc, c, h, band, col):
    part = acc[FIRST + band * SIDE + col, pl.ds(16 * h + 8 * c, 8), :]
    if h == 0:
        part = part + acc[band * SIDE + col, pl.ds(2 * SUB + 8 * c, 8), :]
    return part


def fold_kernel(with_low, acc, out, first, *rest):
    low, rest = (rest[0], rest[1:]) if with_low else (None, rest)
    stage, out_sems = rest
    lane = lanes((8, ROWS))

    def copy_out(band):
        rows = pl.ds(band * SUB, SUB)
        return pltpu.make_async_copy(
            stage.at[:, rows, :], out.at[:, rows, pl.ds(ROWS, TILE - ROWS)], out_sems.at[band]
        )

    def fold(band, carry):
        for c in range(2):
            for h in range(8):
                before = jnp.zeros((8, ROWS), f32)
                for t in range(TILE // ROWS):
                    even = rows_of(acc, c, h, band, 2 * t)
                    odd = rows_of(acc, c, h, band, 2 * t + 1)
                    rows = pl.ds(band * SUB + 8 * h, 8)
                    columns = even + jnp.where(lane < SUB, before, odd)
                    if t == 0:
                        first[c, rows, :] = columns
                    else:
                        stage[c, rows, pl.ds((t - 1) * ROWS, ROWS)] = columns
                    before = odd
        copy_out(band).start()
        return carry

    lax.fori_loop(0, SIDE, fold, 0)
    if with_low:
        for c in range(2):
            before = jnp.zeros((8, ROWS), f32)
            for t in range(TILE // ROWS):
                rows = pl.ds(2 * SUB + 8 * c, 8)
                even = acc[FIRST + (SIDE - 1) * SIDE + 2 * t, rows, :]
                odd = acc[FIRST + (SIDE - 1) * SIDE + 2 * t + 1, rows, :]
                low[c, :, pl.ds(t * ROWS, ROWS)] = even + jnp.where(lane < SUB, before, odd)
                before = odd
            low[c, :, pl.ds(TILE, ROWS)] = jnp.where(lane < KW, before, 0.0)

    def finish(band, carry):
        copy_out(band).wait()
        return carry

    lax.fori_loop(0, SIDE, finish, 0)


def edge_kernel(edge, first, grid_in, grid_out, columns, out_sems):
    lane = lanes((8, ROWS))
    pairs = SIDE // 2

    def put(pair):
        rows = pl.ds(pair * 2 * SUB, 2 * SUB)
        return pltpu.make_async_copy(
            columns.at[:, rows, :], grid_out.at[:, rows, pl.ds(0, ROWS)], out_sems.at[pair]
        )

    def add(pair, carry):
        for c in range(2):
            packed = edge[c, pair]
            for k in range(16):
                moved = pltpu.roll(packed, ROWS - 8 * k, 1) if k else packed
                rows = pl.ds(pair * 2 * SUB + 8 * k, 8)
                columns[c, rows, :] = first[c, rows, :] + jnp.where(lane < KW, moved, 0.0)
        put(pair).start()
        return carry

    lax.fori_loop(0, pairs, add, 0)
    for pair in range(pairs):
        put(pair).wait()


def in_hbm(x):
    return pltpu.with_memory_space_constraint(x, pltpu.HBM)


def shifted(block, axis, distance):
    devices = range(lax.axis_size(axis))
    route = [(i - distance, i) for i in devices if i - distance in devices]
    return lax.ppermute(block, axis, route)


def shards(visibilities, vis_weight, cell_index, tap_offsets, routes, patch_index, kernel):
    blocks = visibilities.shape[0]
    tile_count = lax.axis_size("tile")
    plane_count = lax.axis_size("wp")
    peers = tile_count * plane_count
    cap = max(2, 2 * blocks // peers)
    rows = 3 * cap + 1
    vmem = pl.BlockSpec(memory_space=pltpu.VMEM)
    hbm = pl.BlockSpec(memory_space=pltpu.HBM)

    acc_shape = (max(DUMMY + 1, 6 * (blocks // 8)), ROW_BLOCK, ROWS)

    buckets, acc = pl.pallas_call(
        functools.partial(pack_kernel, peers, cap),
        out_shape=[jax.ShapeDtypeStruct((peers * rows, 1, ROWS), f32), pltpu.VMEM(acc_shape, f32)],
        in_specs=[hbm] * 6,
        out_specs=[vmem, vmem],
        scratch_shapes=[
            pltpu.SMEM((blocks,), jnp.int32),
            pltpu.SMEM((blocks,), jnp.int32),
            pltpu.VMEM((blocks, 2, ROWS), f32),
            pltpu.VMEM((blocks, ROWS), f32),
            pltpu.VMEM((blocks, ROWS), jnp.int32),
            pltpu.VMEM((blocks, ROWS), jnp.int32),
            pltpu.SMEM((peers, ROWS), jnp.int32),
            pltpu.VMEM((peers, ROWS), jnp.int32),
            pltpu.SMEM((blocks,), jnp.int32),
            pltpu.SemaphoreType.DMA((7,)),
        ],
        compiler_params=pltpu.CompilerParams(vmem_limit_bytes=8 << 20),
        name="pack",
    )(*[in_hbm(x) for x in (routes[:, 0], patch_index, visibilities, vis_weight, cell_index, tap_offsets)])

    arrived = lax.all_to_all(buckets, ("tile", "wp"), split_axis=0, concat_axis=0, tiled=True)

    acc, right = pl.pallas_call(
        functools.partial(add_kernel, peers, cap),
        out_shape=[pltpu.VMEM(acc_shape, f32), jax.ShapeDtypeStruct((2, SIDE // 2, 8, ROWS), f32)],
        in_specs=[hbm, vmem, vmem],
        out_specs=[vmem, vmem],
        scratch_shapes=[
            pltpu.VMEM((peers, ROWS), jnp.int32),
            pltpu.SMEM((peers, ROWS), jnp.int32),
            pltpu.SMEM((peers * cap + max(cap, SHORT),), jnp.int32),
            pltpu.SMEM((KW, OVER), f32),
            pltpu.SemaphoreType.DMA,
            pltpu.SemaphoreType.DMA,
        ],
        input_output_aliases={2: 0},
        compiler_params=pltpu.CompilerParams(vmem_limit_bytes=4 << 20),
        name="add",
    )(in_hbm(kernel.T), arrived, acc)

    place = lax.axis_index("tile")
    from_left = shifted(right, "tile", 1)

    with_low = tile_count > TCOLS
    out_shape = [jax.ShapeDtypeStruct((2, TILE, TILE), f32), jax.ShapeDtypeStruct((2, TILE, ROWS), f32)]
    out_specs = [hbm, vmem]
    if with_low:
        out_shape.append(jax.ShapeDtypeStruct((2, KW, TILE + ROWS), f32))
        out_specs.append(vmem)
    own, first, *low = pl.pallas_call(
        functools.partial(fold_kernel, with_low),
        out_shape=out_shape,
        in_specs=[vmem],
        out_specs=out_specs,
        scratch_shapes=[pltpu.VMEM((2, TILE, TILE - ROWS), f32), pltpu.SemaphoreType.DMA((SIDE,))],
        compiler_params=pltpu.CompilerParams(vmem_limit_bytes=12 << 20),
        cost_estimate=pl.CostEstimate(flops=1 << 22, bytes_accessed=16 << 20, transcendentals=0),
        name="fold",
    )(acc)

    if with_low:
        from_left = jnp.where(place % TCOLS == 0, 0.0, from_left)
    own = pl.pallas_call(
        edge_kernel,
        out_shape=jax.ShapeDtypeStruct((2, TILE, TILE), f32),
        in_specs=[vmem, vmem, hbm],
        out_specs=hbm,
        scratch_shapes=[
            pltpu.VMEM((2, TILE, ROWS), f32),
            pltpu.SemaphoreType.DMA((SIDE // 2,)),
        ],
        input_output_aliases={2: 0},
        compiler_params=pltpu.CompilerParams(vmem_limit_bytes=4 << 20),
        name="edges",
    )(from_left, first, own)
    if with_low:
        (low,) = low
        from_above = shifted(low, "tile", TCOLS)
        from_corner = shifted(low[:, :, TILE:], "tile", TCOLS + 1)
        from_corner = jnp.where(place % TCOLS == 0, 0.0, from_corner)
        own = own.at[:, :KW, :].add(from_above[:, :, :TILE])
        own = own.at[:, :KW, :ROWS].add(from_corner)
    return own.reshape(1, 1, 2, TILE, TILE)


def solution(mesh):
    in_specs = (
        P(("tile", "wp"), None, None),
        P(("tile", "wp"), None),
        P(("tile", "wp"), None),
        P(("tile", "wp"), None),
        P(("tile", "wp"), None),
        P(("tile", "wp")),
        P(),
    )
    out_specs = P("wp", "tile", None, None, None)
    return jax.shard_map(shards, mesh=mesh, in_specs=in_specs, out_specs=out_specs, check_vma=False)
```

```python
import functools

import jax
import jax.numpy as jnp
from jax import lax
from jax.experimental import pallas as pl
from jax.experimental.pallas import tpu as pltpu
from jax.sharding import PartitionSpec as P

TCOLS = 8
SUB = 64
KW = 8
OVER = 16
TILE = 1024
ROWS = 128
SIDE = TILE // SUB
PATCHES = SIDE * SIDE
ROW_BLOCK = 2 * (SUB + KW)
FIRST = SIDE
DUMMY = FIRST + PATCHES
STEPS = (128, 32, 16)

f32 = jnp.float32
bf16 = jnp.bfloat16


def lanes(shape):
    return lax.broadcasted_iota(jnp.int32, shape, len(shape) - 1)


def pack_kernel(peers, cap, routes, patch, vis, weight, cell, tap, out, acc, *scratch):
    routes_s, patch_s, vis_v, weight_v, cell_v, tap_v, count, meta, meta_v, place, sems = scratch
    blocks = vis.shape[0]
    rows = 3 * cap + 1
    sources = (routes, patch, vis, weight, cell, tap)
    targets = (routes_s, patch_s, vis_v, weight_v, cell_v, tap_v)
    copies = [pltpu.make_async_copy(a, b, sems.at[i]) for i, (a, b) in enumerate(zip(sources, targets))]
    for copy in copies:
        copy.start()

    steps = blocks // 8
    early = acc.shape[0] - 6 * steps

    def clear_accumulators(first, number):
        for i in range(number):
            acc[first + i] = jnp.zeros((ROW_BLOCK, ROWS), f32)

    def clear(d, carry):
        count[d] = 0
        return carry

    def clear_one(i, carry):
        clear_accumulators(i, 1)
        return carry

    lax.fori_loop(0, peers, clear, 0, unroll=8)
    lax.fori_loop(0, early, clear_one, 0)
    copies[0].wait()
    copies[1].wait()

    def choose(step, carry):
        clear_accumulators(early + 4 * step, 4)
        for i in range(8):
            b = step * 8 + i
            d = routes_s[b]
            k = count[d]
            count[d] = k + 1
            meta[d, k] = patch_s[b]
            place[b] = d * rows + 3 * k
        return carry

    def put_count(d, carry):
        meta[d, cap] = count[d]
        return carry

    lax.fori_loop(0, steps, choose, 0)
    lax.fori_loop(0, peers, put_count, 0, unroll=8)
    meta_copy = pltpu.make_async_copy(meta, meta_v, sems.at[6])
    meta_copy.start()
    for copy in copies[2:]:
        copy.wait()

    def move(step, carry):
        clear_accumulators(early + 4 * steps + 2 * step, 2)
        first = pl.multiple_of(step * 8, 8)
        block_rows = pl.ds(first, 8)
        w = weight_v[block_rows, :]
        c = cell_v[block_rows, :]
        t = tap_v[block_rows, :]
        at_u = ((t >> 4) << 3) | ((c >> 6) & 7)
        at_v = ((t & 15) << 3) | (c & 7)
        code = (((c >> 9) << 17) | (((c >> 3) & 7) << 14) | (at_u << 7) | at_v).astype(f32)
        for i in range(8):
            row = place[first + i]
            both = vis_v[first + i] * w[i : i + 1, :]
            out[row] = both[0:1, :]
            out[row + 1] = both[1:2, :]
            out[row + 2] = code[i : i + 1, :]
        return carry

    lax.fori_loop(0, steps, move, 0)
    meta_copy.wait()

    def put_meta(d, carry):
        out[d * rows + 3 * cap] = meta_v[pl.ds(d, 1), :].astype(f32)
        return carry

    lax.fori_loop(0, peers, put_meta, 0, unroll=8)


def split(x):
    hi = x.astype(bf16)
    return hi, (x - hi.astype(f32)).astype(bf16)


def twice(x):
    return jnp.concatenate([x, x], axis=0)


def look_up(table, index):
    numbers = lax.GatherDimensionNumbers(
        offset_dims=(),
        collapsed_slice_dims=(1,),
        start_index_map=(1,),
        operand_batching_dims=(0,),
        start_indices_batching_dims=(0,),
    )
    return lax.gather(
        table, index[..., None], numbers, (1, 1), mode=lax.GatherScatterMode.PROMISE_IN_BOUNDS
    )


def spread(picks, values):
    zero = jnp.zeros((16, ROWS), bf16)
    return [[jnp.where(pick, value, zero) for pick in picks] for value in values]


def patch_product(re, im, code, parity, table, wide):
    sub = lax.broadcasted_iota(jnp.int32, (8, ROWS), 0)
    at_v = code & 127
    at_u = (code >> 7) & 127
    ku = look_up(table, at_u)
    kv = look_up(table, at_v)
    group_u = ((code >> 17) & 7) + jnp.where(sub < (at_u & 7), 1, 0)
    group_v = ((code >> 14) & 7) + jnp.where(sub < (at_v & 7), 1, 0) + 8 * parity
    step_u = twice(group_u.astype(f32)).astype(bf16)
    step_v = jnp.concatenate([group_v & 15, (group_v + 15) & 15], axis=0).astype(f32).astype(bf16)

    u_hi, u_lo = split(jnp.concatenate([re * ku, im * ku], axis=0))
    hi_rows, lo_rows = spread([step_u == float(g) for g in range(SUB // 8 + 1)], [u_hi, u_lo])
    left_hi, left_lo = jnp.concatenate(hi_rows, axis=0), jnp.concatenate(lo_rows, axis=0)
    v_hi, v_lo = split(twice(kv))
    hi_rows, lo_rows = spread([step_v == 2.0 * g for g in range(ROWS // 16)], [v_hi, v_lo])
    right_hi, right_lo = jnp.concatenate(hi_rows, axis=0), jnp.concatenate(lo_rows, axis=0)

    if wide:
        left = jnp.concatenate([left_hi, left_lo], axis=1)
        right = jnp.concatenate([right_hi, right_lo], axis=0)
        right = jnp.concatenate([right, right], axis=1)
    else:
        left = jnp.concatenate([left_hi, left_lo], axis=0)
        left = jnp.concatenate([left, left], axis=1)
        right = jnp.concatenate([right_hi, right_lo], axis=1)
    product = lax.dot_general(left, right, (((1,), (1,)), ((), ())), preferred_element_type=f32)
    if wide:
        return product[:, :ROWS] + product[:, ROWS:]
    return product[:ROW_BLOCK] + product[ROW_BLOCK:]


def tap_table(kernel):
    sub = lax.broadcasted_iota(jnp.int32, (8, ROWS), 0)
    lane = lanes((8, ROWS))
    which_tap = (sub - lane) & 7
    which_level = lane >> 3
    table = jnp.zeros((8, ROWS), f32)
    for a in range(KW):
        row = jnp.zeros((8, ROWS), f32)
        for o in range(OVER):
            row = jnp.where(which_level == o, kernel[a, o], row)
        table = jnp.where(which_tap == a, row, table)
    return table


def add_kernel(peers, cap, kernel, arrived, acc_in, acc, right, *scratch):
    meta_v, meta, slots, kernel_s, meta_sem, kernel_sem = scratch
    rows = 3 * cap + 1
    kernel_copy = pltpu.make_async_copy(kernel, kernel_s, kernel_sem)
    kernel_copy.start()
    lane_row = lanes((1, ROWS))

    def entries(s, carry):
        row = arrived[s * rows + 3 * cap].astype(jnp.int32)
        entry = (s * rows + 3 * lane_row) * 512 + (row + FIRST)
        meta_v[pl.ds(s, 1), :] = jnp.where(lane_row < cap, entry, row)
        return carry

    lax.fori_loop(0, peers, entries, 0, unroll=8)
    meta_copy = pltpu.make_async_copy(meta_v, meta, meta_sem)
    meta_copy.start()
    kernel_copy.wait()
    table = tap_table(kernel_s)
    meta_copy.wait()

    def gather_source(s, total):
        for k in range(cap):
            slots[total + k] = meta[s, k]
        return total + meta[s, cap]

    total = lax.fori_loop(0, peers, gather_source, 0, unroll=2)
    for k in range(STEPS[-1]):
        slots[total + k] = DUMMY

    def add(first, number):
        for i in range(number):
            entry = slots[first + i]
            row = entry >> 9
            where_to = entry & 511
            re = jnp.broadcast_to(arrived[row], (8, ROWS))
            im = jnp.broadcast_to(arrived[row + 1], (8, ROWS))
            code = jnp.broadcast_to(arrived[row + 2], (8, ROWS)).astype(jnp.int32)
            acc[where_to] += patch_product(re, im, code, entry & 1, table, i % 4 < 2)

    done = 0
    for size in STEPS:
        steps = (total - done + (size - 1 if size == STEPS[-1] else 0)) // size

        def add_step(step, carry, size=size, done=done):
            add(done + step * size, size)
            return carry

        lax.fori_loop(0, steps, add_step, 0)
        done = done + steps * size

    lane = lanes((8, ROWS))

    def pack_edge(pair, carry):
        for c in range(2):
            edge = jnp.zeros((8, ROWS), f32)
            for k in range(16):
                last = rows_of(acc, c, k % 8, pair * 2 + k // 8, SIDE - 1)
                moved = pltpu.roll(last, 8 * k, 1) if k else last
                edge = jnp.where((lane >> 3) == k, moved, edge)
            right[c, pair] = edge
        return carry

    lax.fori_loop(0, SIDE // 2, pack_edge, 0)


def rows_of(acc, c, h, band, col):
    part = acc[FIRST + band * SIDE + col, pl.ds(16 * h + 8 * c, 8), :]
    if h == 0:
        part = part + acc[band * SIDE + col, pl.ds(2 * SUB + 8 * c, 8), :]
    return part


def fold_kernel(with_low, acc, out, first, *rest):
    low, rest = (rest[0], rest[1:]) if with_low else (None, rest)
    stage, out_sems = rest
    lane = lanes((8, ROWS))

    def copy_out(band):
        rows = pl.ds(band * SUB, SUB)
        return pltpu.make_async_copy(
            stage.at[:, rows, :], out.at[:, rows, pl.ds(ROWS, TILE - ROWS)], out_sems.at[band]
        )

    def fold(band, carry):
        for c in range(2):
            for h in range(8):
                before = jnp.zeros((8, ROWS), f32)
                for t in range(TILE // ROWS):
                    even = rows_of(acc, c, h, band, 2 * t)
                    odd = rows_of(acc, c, h, band, 2 * t + 1)
                    rows = pl.ds(band * SUB + 8 * h, 8)
                    columns = even + jnp.where(lane < SUB, before, odd)
                    if t == 0:
                        first[c, rows, :] = columns
                    else:
                        stage[c, rows, pl.ds((t - 1) * ROWS, ROWS)] = columns
                    before = odd
        copy_out(band).start()
        return carry

    lax.fori_loop(0, SIDE, fold, 0)
    if with_low:
        for c in range(2):
            before = jnp.zeros((8, ROWS), f32)
            for t in range(TILE // ROWS):
                rows = pl.ds(2 * SUB + 8 * c, 8)
                even = acc[FIRST + (SIDE - 1) * SIDE + 2 * t, rows, :]
                odd = acc[FIRST + (SIDE - 1) * SIDE + 2 * t + 1, rows, :]
                low[c, :, pl.ds(t * ROWS, ROWS)] = even + jnp.where(lane < SUB, before, odd)
                before = odd
            low[c, :, pl.ds(TILE, ROWS)] = jnp.where(lane < KW, before, 0.0)

    def finish(band, carry):
        copy_out(band).wait()
        return carry

    lax.fori_loop(0, SIDE, finish, 0)


def edge_kernel(edge, first, grid_in, grid_out, columns, out_sems):
    lane = lanes((8, ROWS))
    pairs = SIDE // 2

    def put(pair):
        rows = pl.ds(pair * 2 * SUB, 2 * SUB)
        return pltpu.make_async_copy(
            columns.at[:, rows, :], grid_out.at[:, rows, pl.ds(0, ROWS)], out_sems.at[pair]
        )

    def add(pair, carry):
        for c in range(2):
            packed = edge[c, pair]
            for k in range(16):
                moved = pltpu.roll(packed, ROWS - 8 * k, 1) if k else packed
                rows = pl.ds(pair * 2 * SUB + 8 * k, 8)
                columns[c, rows, :] = first[c, rows, :] + jnp.where(lane < KW, moved, 0.0)
        put(pair).start()
        return carry

    lax.fori_loop(0, pairs, add, 0)
    for pair in range(pairs):
        put(pair).wait()


def in_hbm(x):
    return pltpu.with_memory_space_constraint(x, pltpu.HBM)


def shifted(block, axis, distance):
    devices = range(lax.axis_size(axis))
    route = [(i - distance, i) for i in devices if i - distance in devices]
    return lax.ppermute(block, axis, route)


def shards(visibilities, vis_weight, cell_index, tap_offsets, routes, patch_index, kernel):
    blocks = visibilities.shape[0]
    tile_count = lax.axis_size("tile")
    plane_count = lax.axis_size("wp")
    peers = tile_count * plane_count
    cap = max(2, 2 * blocks // peers)
    rows = 3 * cap + 1
    vmem = pl.BlockSpec(memory_space=pltpu.VMEM)
    hbm = pl.BlockSpec(memory_space=pltpu.HBM)

    acc_shape = (max(DUMMY + 1, 6 * (blocks // 8)), ROW_BLOCK, ROWS)

    buckets, acc = pl.pallas_call(
        functools.partial(pack_kernel, peers, cap),
        out_shape=[jax.ShapeDtypeStruct((peers * rows, 1, ROWS), f32), pltpu.VMEM(acc_shape, f32)],
        in_specs=[hbm] * 6,
        out_specs=[vmem, vmem],
        scratch_shapes=[
            pltpu.SMEM((blocks,), jnp.int32),
            pltpu.SMEM((blocks,), jnp.int32),
            pltpu.VMEM((blocks, 2, ROWS), f32),
            pltpu.VMEM((blocks, ROWS), f32),
            pltpu.VMEM((blocks, ROWS), jnp.int32),
            pltpu.VMEM((blocks, ROWS), jnp.int32),
            pltpu.SMEM((peers,), jnp.int32),
            pltpu.SMEM((peers, ROWS), jnp.int32),
            pltpu.VMEM((peers, ROWS), jnp.int32),
            pltpu.SMEM((blocks,), jnp.int32),
            pltpu.SemaphoreType.DMA((7,)),
        ],
        compiler_params=pltpu.CompilerParams(vmem_limit_bytes=8 << 20),
        name="pack",
    )(*[in_hbm(x) for x in (routes[:, 0], patch_index, visibilities, vis_weight, cell_index, tap_offsets)])

    arrived = lax.all_to_all(buckets, ("tile", "wp"), split_axis=0, concat_axis=0, tiled=True)

    acc, right = pl.pallas_call(
        functools.partial(add_kernel, peers, cap),
        out_shape=[pltpu.VMEM(acc_shape, f32), jax.ShapeDtypeStruct((2, SIDE // 2, 8, ROWS), f32)],
        in_specs=[hbm, vmem, vmem],
        out_specs=[vmem, vmem],
        scratch_shapes=[
            pltpu.VMEM((peers, ROWS), jnp.int32),
            pltpu.SMEM((peers, ROWS), jnp.int32),
            pltpu.SMEM((peers * cap + max(cap, STEPS[-1]),), jnp.int32),
            pltpu.SMEM((KW, OVER), f32),
            pltpu.SemaphoreType.DMA,
            pltpu.SemaphoreType.DMA,
        ],
        input_output_aliases={2: 0},
        compiler_params=pltpu.CompilerParams(vmem_limit_bytes=4 << 20),
        name="add",
    )(in_hbm(kernel.T), arrived, acc)

    place = lax.axis_index("tile")
    from_left = shifted(right, "tile", 1)

    with_low = tile_count > TCOLS
    out_shape = [jax.ShapeDtypeStruct((2, TILE, TILE), f32), jax.ShapeDtypeStruct((2, TILE, ROWS), f32)]
    out_specs = [hbm, vmem]
    if with_low:
        out_shape.append(jax.ShapeDtypeStruct((2, KW, TILE + ROWS), f32))
        out_specs.append(vmem)
    own, first, *low = pl.pallas_call(
        functools.partial(fold_kernel, with_low),
        out_shape=out_shape,
        in_specs=[vmem],
        out_specs=out_specs,
        scratch_shapes=[pltpu.VMEM((2, TILE, TILE - ROWS), f32), pltpu.SemaphoreType.DMA((SIDE,))],
        compiler_params=pltpu.CompilerParams(vmem_limit_bytes=12 << 20),
        cost_estimate=pl.CostEstimate(flops=1 << 22, bytes_accessed=16 << 20, transcendentals=0),
        name="fold",
    )(acc)

    if with_low:
        from_left = jnp.where(place % TCOLS == 0, 0.0, from_left)
    own = pl.pallas_call(
        edge_kernel,
        out_shape=jax.ShapeDtypeStruct((2, TILE, TILE), f32),
        in_specs=[vmem, vmem, hbm],
        out_specs=hbm,
        scratch_shapes=[
            pltpu.VMEM((2, TILE, ROWS), f32),
            pltpu.SemaphoreType.DMA((SIDE // 2,)),
        ],
        input_output_aliases={2: 0},
        compiler_params=pltpu.CompilerParams(vmem_limit_bytes=4 << 20),
        name="edges",
    )(from_left, first, own)
    if with_low:
        (low,) = low
        from_above = shifted(low, "tile", TCOLS)
        from_corner = shifted(low[:, :, TILE:], "tile", TCOLS + 1)
        from_corner = jnp.where(place % TCOLS == 0, 0.0, from_corner)
        own = own.at[:, :KW, :].add(from_above[:, :, :TILE])
        own = own.at[:, :KW, :ROWS].add(from_corner)
    return own.reshape(1, 1, 2, TILE, TILE)


def solution(mesh):
    in_specs = (
        P(("tile", "wp"), None, None),
        P(("tile", "wp"), None),
        P(("tile", "wp"), None),
        P(("tile", "wp"), None),
        P(("tile", "wp"), None),
        P(("tile", "wp")),
        P(),
    )
    out_specs = P("wp", "tile", None, None, None)
    return jax.shard_map(shards, mesh=mesh, in_specs=in_specs, out_specs=out_specs, check_vma=False)
```

```python
import functools

import jax
import jax.numpy as jnp
from jax import lax
from jax.experimental import pallas as pl
from jax.experimental.pallas import tpu as pltpu
from jax.sharding import PartitionSpec as P

TCOLS = 8
SUB = 64
KW = 8
OVER = 16
TILE = 1024
ROWS = 128
SIDE = TILE // SUB
PATCHES = SIDE * SIDE
ROW_BLOCK = 2 * (SUB + KW)
FIRST = SIDE
DUMMY = FIRST + PATCHES
LATE = 64
WIDE = 80
STEPS = (128, 32, 16)

f32 = jnp.float32
bf16 = jnp.bfloat16


def lanes(shape):
    return lax.broadcasted_iota(jnp.int32, shape, len(shape) - 1)


def pack_kernel(peers, cap, routes, patch, vis, weight, cell, tap, out, acc, *scratch):
    routes_s, patch_s, vis_v, weight_v, cell_v, tap_v, count, meta, meta_v, place, sems = scratch
    blocks = vis.shape[0]
    rows = 3 * cap + 1
    sources = (routes, patch, vis, weight, cell, tap)
    targets = (routes_s, patch_s, vis_v, weight_v, cell_v, tap_v)
    copies = [pltpu.make_async_copy(a, b, sems.at[i]) for i, (a, b) in enumerate(zip(sources, targets))]
    for copy in copies:
        copy.start()

    steps = blocks // 8
    early = acc.shape[0] - LATE - 4 * steps

    def clear_accumulators(first, number):
        for i in range(number):
            acc[first + i] = jnp.zeros((ROW_BLOCK, ROWS), f32)

    def clear(d, carry):
        count[d] = 0
        return carry

    def clear_one(i, carry):
        clear_accumulators(i, 1)
        return carry

    lax.fori_loop(0, peers, clear, 0, unroll=8)
    lax.fori_loop(0, early, clear_one, 0)
    copies[0].wait()
    copies[1].wait()

    def choose(step, carry):
        clear_accumulators(early + 4 * step, 4)
        for i in range(8):
            b = step * 8 + i
            d = routes_s[b]
            k = count[d]
            count[d] = k + 1
            meta[d, k] = patch_s[b]
            place[b] = d * rows + 3 * k
        return carry

    def put_count(d, carry):
        meta[d, cap] = count[d]
        return carry

    lax.fori_loop(0, steps, choose, 0)
    lax.fori_loop(0, peers, put_count, 0, unroll=8)
    meta_copy = pltpu.make_async_copy(meta, meta_v, sems.at[6])
    meta_copy.start()
    for copy in copies[2:]:
        copy.wait()

    def move(step, carry):
        first = pl.multiple_of(step * 8, 8)
        block_rows = pl.ds(first, 8)
        w = weight_v[block_rows, :]
        c = cell_v[block_rows, :]
        t = tap_v[block_rows, :]
        at_u = ((t >> 4) << 3) | ((c >> 6) & 7)
        at_v = ((t & 15) << 3) | (c & 7)
        code = (((c >> 9) << 17) | (((c >> 3) & 7) << 14) | (at_u << 7) | at_v).astype(f32)
        for i in range(8):
            row = place[first + i]
            both = vis_v[first + i] * w[i : i + 1, :]
            out[row] = both[0:1, :]
            out[row + 1] = both[1:2, :]
            out[row + 2] = code[i : i + 1, :]
        return carry

    lax.fori_loop(0, steps, move, 0)
    meta_copy.wait()

    def put_meta(d, carry):
        out[d * rows + 3 * cap] = meta_v[pl.ds(d, 1), :].astype(f32)
        return carry

    lax.fori_loop(0, peers, put_meta, 0, unroll=8)


def split(x):
    hi = x.astype(bf16)
    return hi, (x - hi.astype(f32)).astype(bf16)


def twice(x):
    return jnp.concatenate([x, x], axis=0)


def look_up(table, index):
    numbers = lax.GatherDimensionNumbers(
        offset_dims=(),
        collapsed_slice_dims=(1,),
        start_index_map=(1,),
        operand_batching_dims=(0,),
        start_indices_batching_dims=(0,),
    )
    return lax.gather(
        table, index[..., None], numbers, (1, 1), mode=lax.GatherScatterMode.PROMISE_IN_BOUNDS
    )


def spread(picks, values):
    zero = jnp.zeros((16, ROWS), bf16)
    return [[jnp.where(pick, value, zero) for pick in picks] for value in values]


def patch_product(re, im, code, parity, table, wide):
    sub = lax.broadcasted_iota(jnp.int32, (8, ROWS), 0)
    at_v = code & 127
    at_u = (code >> 7) & 127
    ku = look_up(table, at_u)
    kv = look_up(table, at_v)
    group_u = ((code >> 17) & 7) + jnp.where(sub < (at_u & 7), 1, 0)
    group_v = ((code >> 14) & 7) + jnp.where(sub < (at_v & 7), 1, 0)
    step_u = twice(group_u.astype(f32)).astype(bf16)
    step_v = jnp.concatenate([group_v, group_v - 1], axis=0).astype(f32).astype(bf16)

    u_hi, u_lo = split(jnp.concatenate([re * ku, im * ku], axis=0))
    hi_rows, lo_rows = spread([step_u == float(g) for g in range(SUB // 8 + 1)], [u_hi, u_lo])
    left_hi, left_lo = jnp.concatenate(hi_rows, axis=0), jnp.concatenate(lo_rows, axis=0)
    v_hi, v_lo = split(twice(kv))
    hi_rows, lo_rows = spread([step_v == 2.0 * g for g in range(WIDE // 16)], [v_hi, v_lo])
    right_hi, right_lo = jnp.concatenate(hi_rows, axis=0), jnp.concatenate(lo_rows, axis=0)

    if wide:
        left = jnp.concatenate([left_hi, left_lo], axis=1)
        right = jnp.concatenate([right_hi, jnp.zeros((ROWS - WIDE, ROWS), bf16), right_lo], axis=0)
        right = jnp.concatenate([right, right], axis=1)
    else:
        left = jnp.concatenate([left_hi, left_lo], axis=0)
        left = jnp.concatenate([left, left], axis=1)
        right = jnp.concatenate([right_hi, right_lo], axis=1)
    product = lax.dot_general(left, right, (((1,), (1,)), ((), ())), preferred_element_type=f32)
    if wide:
        product = product[:, :WIDE] + product[:, ROWS : ROWS + WIDE]
    else:
        product = product[:ROW_BLOCK] + product[ROW_BLOCK:]
    product = jnp.concatenate([product, jnp.zeros((ROW_BLOCK, ROWS - WIDE), f32)], axis=1)
    return pltpu.roll(product, parity * SUB, 1)


def tap_table(kernel):
    sub = lax.broadcasted_iota(jnp.int32, (8, ROWS), 0)
    lane = lanes((8, ROWS))
    which_tap = (sub - lane) & 7
    which_level = lane >> 3
    table = jnp.zeros((8, ROWS), f32)
    for a in range(KW):
        row = jnp.zeros((8, ROWS), f32)
        for o in range(OVER):
            row = jnp.where(which_level == o, kernel[a, o], row)
        table = jnp.where(which_tap == a, row, table)
    return table


def add_kernel(peers, cap, kernel, arrived, acc_in, acc, right, *scratch):
    meta_v, meta, slots, kernel_s, meta_sem, kernel_sem = scratch
    rows = 3 * cap + 1
    kernel_copy = pltpu.make_async_copy(kernel, kernel_s, kernel_sem)
    kernel_copy.start()
    lane_row = lanes((1, ROWS))

    def entries(s, carry):
        row = arrived[s * rows + 3 * cap].astype(jnp.int32)
        entry = (s * rows + 3 * lane_row) * 512 + (row + FIRST)
        meta_v[pl.ds(s, 1), :] = jnp.where(lane_row < cap, entry, row)
        return carry

    lax.fori_loop(0, peers, entries, 0, unroll=8)
    meta_copy = pltpu.make_async_copy(meta_v, meta, meta_sem)
    meta_copy.start()

    def clear(i, carry):
        acc[i] = jnp.zeros((ROW_BLOCK, ROWS), f32)
        return carry

    lax.fori_loop(acc.shape[0] - LATE, acc.shape[0], clear, 0)
    kernel_copy.wait()
    table = tap_table(kernel_s)
    meta_copy.wait()

    def gather_source(s, total):
        for k in range(cap):
            slots[total + k] = meta[s, k]
        return total + meta[s, cap]

    total = lax.fori_loop(0, peers, gather_source, 0, unroll=2)
    for k in range(STEPS[-1]):
        slots[total + k] = DUMMY

    def add(first, number):
        for i in range(number):
            entry = slots[first + i]
            row = entry >> 9
            where_to = entry & 511
            re = jnp.broadcast_to(arrived[row], (8, ROWS))
            im = jnp.broadcast_to(arrived[row + 1], (8, ROWS))
            code = jnp.broadcast_to(arrived[row + 2], (8, ROWS)).astype(jnp.int32)
            acc[where_to] += patch_product(re, im, code, entry & 1, table, i % 4 < 2)

    done = 0
    for size in STEPS:
        steps = (total - done + (size - 1 if size == STEPS[-1] else 0)) // size

        def add_step(step, carry, size=size, done=done):
            add(done + step * size, size)
            return carry

        lax.fori_loop(0, steps, add_step, 0)
        done = done + steps * size

    lane = lanes((8, ROWS))

    def pack_edge(pair, carry):
        for c in range(2):
            edge = jnp.zeros((8, ROWS), f32)
            for k in range(16):
                last = rows_of(acc, c, k % 8, pair * 2 + k // 8, SIDE - 1)
                moved = pltpu.roll(last, 8 * k, 1) if k else last
                edge = jnp.where((lane >> 3) == k, moved, edge)
            right[c, pair] = edge
        return carry

    lax.fori_loop(0, SIDE // 2, pack_edge, 0)


def rows_of(acc, c, h, band, col):
    part = acc[FIRST + band * SIDE + col, pl.ds(16 * h + 8 * c, 8), :]
    if h == 0:
        part = part + acc[band * SIDE + col, pl.ds(2 * SUB + 8 * c, 8), :]
    return part


def fold_kernel(with_low, acc, out, first, *rest):
    low, rest = (rest[0], rest[1:]) if with_low else (None, rest)
    stage, out_sems = rest
    lane = lanes((8, ROWS))

    def copy_out(band):
        rows = pl.ds(band * SUB, SUB)
        return pltpu.make_async_copy(
            stage.at[:, rows, :], out.at[:, rows, pl.ds(ROWS, TILE - ROWS)], out_sems.at[band]
        )

    def fold(band, carry):
        for c in range(2):
            for h in range(8):
                before = jnp.zeros((8, ROWS), f32)
                for t in range(TILE // ROWS):
                    even = rows_of(acc, c, h, band, 2 * t)
                    odd = rows_of(acc, c, h, band, 2 * t + 1)
                    rows = pl.ds(band * SUB + 8 * h, 8)
                    columns = even + jnp.where(lane < SUB, before, odd)
                    if t == 0:
                        first[c, rows, :] = columns
                    else:
                        stage[c, rows, pl.ds((t - 1) * ROWS, ROWS)] = columns
                    before = odd
        copy_out(band).start()
        return carry

    lax.fori_loop(0, SIDE, fold, 0)
    if with_low:
        for c in range(2):
            before = jnp.zeros((8, ROWS), f32)
            for t in range(TILE // ROWS):
                rows = pl.ds(2 * SUB + 8 * c, 8)
                even = acc[FIRST + (SIDE - 1) * SIDE + 2 * t, rows, :]
                odd = acc[FIRST + (SIDE - 1) * SIDE + 2 * t + 1, rows, :]
                low[c, :, pl.ds(t * ROWS, ROWS)] = even + jnp.where(lane < SUB, before, odd)
                before = odd
            low[c, :, pl.ds(TILE, ROWS)] = jnp.where(lane < KW, before, 0.0)

    def finish(band, carry):
        copy_out(band).wait()
        return carry

    lax.fori_loop(0, SIDE, finish, 0)


def edge_kernel(edge, first, grid_in, grid_out, columns, out_sems):
    lane = lanes((8, ROWS))
    pairs = SIDE // 2

    def put(pair):
        rows = pl.ds(pair * 2 * SUB, 2 * SUB)
        return pltpu.make_async_copy(
            columns.at[:, rows, :], grid_out.at[:, rows, pl.ds(0, ROWS)], out_sems.at[pair]
        )

    def add(pair, carry):
        for c in range(2):
            packed = edge[c, pair]
            for k in range(16):
                moved = pltpu.roll(packed, ROWS - 8 * k, 1) if k else packed
                rows = pl.ds(pair * 2 * SUB + 8 * k, 8)
                columns[c, rows, :] = first[c, rows, :] + jnp.where(lane < KW, moved, 0.0)
        put(pair).start()
        return carry

    lax.fori_loop(0, pairs, add, 0)
    for pair in range(pairs):
        put(pair).wait()


def in_hbm(x):
    return pltpu.with_memory_space_constraint(x, pltpu.HBM)


def shifted(block, axis, distance):
    devices = range(lax.axis_size(axis))
    route = [(i - distance, i) for i in devices if i - distance in devices]
    return lax.ppermute(block, axis, route)


def shards(visibilities, vis_weight, cell_index, tap_offsets, routes, patch_index, kernel):
    blocks = visibilities.shape[0]
    tile_count = lax.axis_size("tile")
    plane_count = lax.axis_size("wp")
    peers = tile_count * plane_count
    cap = max(2, 2 * blocks // peers)
    rows = 3 * cap + 1
    vmem = pl.BlockSpec(memory_space=pltpu.VMEM)
    hbm = pl.BlockSpec(memory_space=pltpu.HBM)

    acc_shape = (max(DUMMY + 1, LATE + 4 * (blocks // 8)), ROW_BLOCK, ROWS)

    buckets, acc = pl.pallas_call(
        functools.partial(pack_kernel, peers, cap),
        out_shape=[jax.ShapeDtypeStruct((peers * rows, 1, ROWS), f32), pltpu.VMEM(acc_shape, f32)],
        in_specs=[hbm] * 6,
        out_specs=[vmem, vmem],
        scratch_shapes=[
            pltpu.SMEM((blocks,), jnp.int32),
            pltpu.SMEM((blocks,), jnp.int32),
            pltpu.VMEM((blocks, 2, ROWS), f32),
            pltpu.VMEM((blocks, ROWS), f32),
            pltpu.VMEM((blocks, ROWS), jnp.int32),
            pltpu.VMEM((blocks, ROWS), jnp.int32),
            pltpu.SMEM((peers,), jnp.int32),
            pltpu.SMEM((peers, ROWS), jnp.int32),
            pltpu.VMEM((peers, ROWS), jnp.int32),
            pltpu.SMEM((blocks,), jnp.int32),
            pltpu.SemaphoreType.DMA((7,)),
        ],
        compiler_params=pltpu.CompilerParams(vmem_limit_bytes=8 << 20),
        name="pack",
    )(*[in_hbm(x) for x in (routes[:, 0], patch_index, visibilities, vis_weight, cell_index, tap_offsets)])

    arrived = lax.all_to_all(buckets, ("tile", "wp"), split_axis=0, concat_axis=0, tiled=True)

    acc, right = pl.pallas_call(
        functools.partial(add_kernel, peers, cap),
        out_shape=[pltpu.VMEM(acc_shape, f32), jax.ShapeDtypeStruct((2, SIDE // 2, 8, ROWS), f32)],
        in_specs=[hbm, vmem, vmem],
        out_specs=[vmem, vmem],
        scratch_shapes=[
            pltpu.VMEM((peers, ROWS), jnp.int32),
            pltpu.SMEM((peers, ROWS), jnp.int32),
            pltpu.SMEM((peers * cap + max(cap, STEPS[-1]),), jnp.int32),
            pltpu.SMEM((KW, OVER), f32),
            pltpu.SemaphoreType.DMA,
            pltpu.SemaphoreType.DMA,
        ],
        input_output_aliases={2: 0},
        compiler_params=pltpu.CompilerParams(vmem_limit_bytes=4 << 20),
        name="add",
    )(in_hbm(kernel.T), arrived, acc)

    place = lax.axis_index("tile")
    from_left = shifted(right, "tile", 1)

    with_low = tile_count > TCOLS
    out_shape = [jax.ShapeDtypeStruct((2, TILE, TILE), f32), jax.ShapeDtypeStruct((2, TILE, ROWS), f32)]
    out_specs = [hbm, vmem]
    if with_low:
        out_shape.append(jax.ShapeDtypeStruct((2, KW, TILE + ROWS), f32))
        out_specs.append(vmem)
    own, first, *low = pl.pallas_call(
        functools.partial(fold_kernel, with_low),
        out_shape=out_shape,
        in_specs=[vmem],
        out_specs=out_specs,
        scratch_shapes=[pltpu.VMEM((2, TILE, TILE - ROWS), f32), pltpu.SemaphoreType.DMA((SIDE,))],
        compiler_params=pltpu.CompilerParams(vmem_limit_bytes=12 << 20),
        cost_estimate=pl.CostEstimate(flops=1 << 22, bytes_accessed=16 << 20, transcendentals=0),
        name="fold",
    )(acc)

    if with_low:
        from_left = jnp.where(place % TCOLS == 0, 0.0, from_left)
    own = pl.pallas_call(
        edge_kernel,
        out_shape=jax.ShapeDtypeStruct((2, TILE, TILE), f32),
        in_specs=[vmem, vmem, hbm],
        out_specs=hbm,
        scratch_shapes=[
            pltpu.VMEM((2, TILE, ROWS), f32),
            pltpu.SemaphoreType.DMA((SIDE // 2,)),
        ],
        input_output_aliases={2: 0},
        compiler_params=pltpu.CompilerParams(vmem_limit_bytes=4 << 20),
        name="edges",
    )(from_left, first, own)
    if with_low:
        (low,) = low
        from_above = shifted(low, "tile", TCOLS)
        from_corner = shifted(low[:, :, TILE:], "tile", TCOLS + 1)
        from_corner = jnp.where(place % TCOLS == 0, 0.0, from_corner)
        own = own.at[:, :KW, :].add(from_above[:, :, :TILE])
        own = own.at[:, :KW, :ROWS].add(from_corner)
    return own.reshape(1, 1, 2, TILE, TILE)


def solution(mesh):
    in_specs = (
        P(("tile", "wp"), None, None),
        P(("tile", "wp"), None),
        P(("tile", "wp"), None),
        P(("tile", "wp"), None),
        P(("tile", "wp"), None),
        P(("tile", "wp")),
        P(),
    )
    out_specs = P("wp", "tile", None, None, None)
    return jax.shard_map(shards, mesh=mesh, in_specs=in_specs, out_specs=out_specs, check_vma=False)
```

```python
import functools

import jax
import jax.numpy as jnp
from jax import lax
from jax.experimental import pallas as pl
from jax.experimental.pallas import tpu as pltpu
from jax.sharding import PartitionSpec as P

TCOLS = 8
SUB = 64
KW = 8
OVER = 16
TILE = 1024
ROWS = 128
SIDE = TILE // SUB
PATCHES = SIDE * SIDE
ROW_BLOCK = 2 * (SUB + KW)
FIRST = SIDE
DUMMY = FIRST + PATCHES
STEPS = (128, 64, 32, 16)

f32 = jnp.float32
bf16 = jnp.bfloat16


def lanes(shape):
    return lax.broadcasted_iota(jnp.int32, shape, len(shape) - 1)


def pack_kernel(peers, cap, routes, patch, vis, weight, cell, tap, out, acc, *scratch):
    routes_s, patch_s, vis_v, weight_v, cell_v, tap_v, count, meta, meta_v, place, sems = scratch
    blocks = vis.shape[0]
    rows = 3 * cap + 1
    sources = (routes, patch, vis, weight, cell, tap)
    targets = (routes_s, patch_s, vis_v, weight_v, cell_v, tap_v)
    copies = [pltpu.make_async_copy(a, b, sems.at[i]) for i, (a, b) in enumerate(zip(sources, targets))]
    for copy in copies:
        copy.start()

    steps = blocks // 8
    early = acc.shape[0] - 6 * steps

    def clear_accumulators(first, number):
        for i in range(number):
            acc[first + i] = jnp.zeros((ROW_BLOCK, ROWS), f32)

    def clear(d, carry):
        count[d] = 0
        return carry

    def clear_one(i, carry):
        clear_accumulators(i, 1)
        return carry

    lax.fori_loop(0, peers, clear, 0, unroll=8)
    lax.fori_loop(0, early, clear_one, 0)
    copies[0].wait()
    copies[1].wait()

    def choose(step, carry):
        clear_accumulators(early + 4 * step, 4)
        for i in range(8):
            b = step * 8 + i
            d = routes_s[b]
            k = count[d]
            count[d] = k + 1
            meta[d, k] = patch_s[b]
            place[b] = d * rows + 3 * k
        return carry

    def put_count(d, carry):
        meta[d, cap] = count[d]
        return carry

    lax.fori_loop(0, steps, choose, 0)
    lax.fori_loop(0, peers, put_count, 0, unroll=8)
    meta_copy = pltpu.make_async_copy(meta, meta_v, sems.at[6])
    meta_copy.start()
    for copy in copies[2:]:
        copy.wait()

    def move(step, carry):
        clear_accumulators(early + 4 * steps + 2 * step, 2)
        first = pl.multiple_of(step * 8, 8)
        block_rows = pl.ds(first, 8)
        w = weight_v[block_rows, :]
        c = cell_v[block_rows, :]
        t = tap_v[block_rows, :]
        at_u = ((t >> 4) << 3) | ((c >> 6) & 7)
        at_v = ((t & 15) << 3) | (c & 7)
        code = (((c >> 9) << 17) | (((c >> 3) & 7) << 14) | (at_u << 7) | at_v).astype(f32)
        for i in range(8):
            row = place[first + i]
            both = vis_v[first + i] * w[i : i + 1, :]
            out[row] = both[0:1, :]
            out[row + 1] = both[1:2, :]
            out[row + 2] = code[i : i + 1, :]
        return carry

    lax.fori_loop(0, steps, move, 0, unroll=4)
    meta_copy.wait()

    def put_meta(d, carry):
        out[d * rows + 3 * cap] = meta_v[pl.ds(d, 1), :].astype(f32)
        return carry

    lax.fori_loop(0, peers, put_meta, 0, unroll=8)


def split(x):
    hi = x.astype(bf16)
    return hi, (x - hi.astype(f32)).astype(bf16)


def twice(x):
    return jnp.concatenate([x, x], axis=0)


def look_up(table, index):
    numbers = lax.GatherDimensionNumbers(
        offset_dims=(),
        collapsed_slice_dims=(1,),
        start_index_map=(1,),
        operand_batching_dims=(0,),
        start_indices_batching_dims=(0,),
    )
    return lax.gather(
        table, index[..., None], numbers, (1, 1), mode=lax.GatherScatterMode.PROMISE_IN_BOUNDS
    )


def spread(picks, values):
    zero = jnp.zeros((16, ROWS), bf16)
    return [[jnp.where(pick, value, zero) for pick in picks] for value in values]


def patch_product(re, im, code, parity, table, wide):
    sub = lax.broadcasted_iota(jnp.int32, (8, ROWS), 0)
    at_v = code & 127
    at_u = (code >> 7) & 127
    ku = look_up(table, at_u)
    kv = look_up(table, at_v)
    group_u = ((code >> 17) & 7) + jnp.where(sub < (at_u & 7), 1, 0)
    group_v = ((code >> 14) & 7) + jnp.where(sub < (at_v & 7), 1, 0) + 8 * parity
    step_u = twice(group_u.astype(f32)).astype(bf16)
    step_v = jnp.concatenate([group_v & 15, (group_v + 15) & 15], axis=0).astype(f32).astype(bf16)

    u_hi, u_lo = split(jnp.concatenate([re * ku, im * ku], axis=0))
    hi_rows, lo_rows = spread([step_u == float(g) for g in range(SUB // 8 + 1)], [u_hi, u_lo])
    left_hi, left_lo = jnp.concatenate(hi_rows, axis=0), jnp.concatenate(lo_rows, axis=0)
    v_hi, v_lo = split(twice(kv))
    hi_rows, lo_rows = spread([step_v == 2.0 * g for g in range(ROWS // 16)], [v_hi, v_lo])
    right_hi, right_lo = jnp.concatenate(hi_rows, axis=0), jnp.concatenate(lo_rows, axis=0)

    if wide:
        left = jnp.concatenate([left_hi, left_lo], axis=1)
        right = jnp.concatenate([right_hi, right_lo], axis=0)
        right = jnp.concatenate([right, right], axis=1)
    else:
        left = jnp.concatenate([left_hi, left_lo], axis=0)
        left = jnp.concatenate([left, left], axis=1)
        right = jnp.concatenate([right_hi, right_lo], axis=1)
    product = lax.dot_general(left, right, (((1,), (1,)), ((), ())), preferred_element_type=f32)
    if wide:
        return product[:, :ROWS] + product[:, ROWS:]
    return product[:ROW_BLOCK] + product[ROW_BLOCK:]


def tap_table(kernel):
    sub = lax.broadcasted_iota(jnp.int32, (8, ROWS), 0)
    lane = lanes((8, ROWS))
    which_tap = (sub - lane) & 7
    which_level = lane >> 3
    table = jnp.zeros((8, ROWS), f32)
    for a in range(KW):
        row = jnp.zeros((8, ROWS), f32)
        for o in range(OVER):
            row = jnp.where(which_level == o, kernel[a, o], row)
        table = jnp.where(which_tap == a, row, table)
    return table


def add_kernel(peers, cap, kernel, arrived, acc_in, acc, right, *scratch):
    meta_v, meta, slots, kernel_s, meta_sem, kernel_sem = scratch
    rows = 3 * cap + 1
    kernel_copy = pltpu.make_async_copy(kernel, kernel_s, kernel_sem)
    kernel_copy.start()
    lane_row = lanes((1, ROWS))

    def entries(s, carry):
        row = arrived[s * rows + 3 * cap].astype(jnp.int32)
        entry = (s * rows + 3 * lane_row) * 512 + (row + FIRST)
        meta_v[pl.ds(s, 1), :] = jnp.where(lane_row < cap, entry, row)
        return carry

    lax.fori_loop(0, peers, entries, 0, unroll=8)
    meta_copy = pltpu.make_async_copy(meta_v, meta, meta_sem)
    meta_copy.start()
    kernel_copy.wait()
    table = tap_table(kernel_s)
    meta_copy.wait()

    def gather_source(s, total):
        for k in range(cap):
            slots[total + k] = meta[s, k]
        return total + meta[s, cap]

    total = lax.fori_loop(0, peers, gather_source, 0, unroll=2)
    for k in range(STEPS[-1]):
        slots[total + k] = DUMMY

    def add(first, number):
        for i in range(number):
            entry = slots[first + i]
            row = entry >> 9
            where_to = entry & 511
            re = jnp.broadcast_to(arrived[row], (8, ROWS))
            im = jnp.broadcast_to(arrived[row + 1], (8, ROWS))
            code = jnp.broadcast_to(arrived[row + 2], (8, ROWS)).astype(jnp.int32)
            acc[where_to] += patch_product(re, im, code, entry & 1, table, i % 4 < 2)

    done = 0
    for size in STEPS:
        steps = (total - done + (size - 1 if size == STEPS[-1] else 0)) // size

        def add_step(step, carry, size=size, done=done):
            add(done + step * size, size)
            return carry

        lax.fori_loop(0, steps, add_step, 0)
        done = done + steps * size

    lane = lanes((8, ROWS))

    def pack_edge(pair, carry):
        for c in range(2):
            edge = jnp.zeros((8, ROWS), f32)
            for k in range(16):
                last = rows_of(acc, c, k % 8, pair * 2 + k // 8, SIDE - 1)
                moved = pltpu.roll(last, 8 * k, 1) if k else last
                edge = jnp.where((lane >> 3) == k, moved, edge)
            right[c, pair] = edge
        return carry

    lax.fori_loop(0, SIDE // 2, pack_edge, 0)


def rows_of(acc, c, h, band, col):
    part = acc[FIRST + band * SIDE + col, pl.ds(16 * h + 8 * c, 8), :]
    if h == 0:
        part = part + acc[band * SIDE + col, pl.ds(2 * SUB + 8 * c, 8), :]
    return part


def fold_kernel(with_low, acc, out, first, *rest):
    low, rest = (rest[0], rest[1:]) if with_low else (None, rest)
    stage, out_sems = rest
    lane = lanes((8, ROWS))

    def copy_out(band):
        rows = pl.ds(band * SUB, SUB)
        return pltpu.make_async_copy(
            stage.at[:, rows, :], out.at[:, rows, pl.ds(ROWS, TILE - ROWS)], out_sems.at[band]
        )

    def fold(band, carry):
        for c in range(2):
            for h in range(8):
                before = jnp.zeros((8, ROWS), f32)
                for t in range(TILE // ROWS):
                    even = rows_of(acc, c, h, band, 2 * t)
                    odd = rows_of(acc, c, h, band, 2 * t + 1)
                    rows = pl.ds(band * SUB + 8 * h, 8)
                    columns = even + jnp.where(lane < SUB, before, odd)
                    if t == 0:
                        first[c, rows, :] = columns
                    else:
                        stage[c, rows, pl.ds((t - 1) * ROWS, ROWS)] = columns
                    before = odd
        copy_out(band).start()
        return carry

    lax.fori_loop(0, SIDE, fold, 0, unroll=2)
    if with_low:
        for c in range(2):
            before = jnp.zeros((8, ROWS), f32)
            for t in range(TILE // ROWS):
                rows = pl.ds(2 * SUB + 8 * c, 8)
                even = acc[FIRST + (SIDE - 1) * SIDE + 2 * t, rows, :]
                odd = acc[FIRST + (SIDE - 1) * SIDE + 2 * t + 1, rows, :]
                low[c, :, pl.ds(t * ROWS, ROWS)] = even + jnp.where(lane < SUB, before, odd)
                before = odd
            low[c, :, pl.ds(TILE, ROWS)] = jnp.where(lane < KW, before, 0.0)

    def finish(band, carry):
        copy_out(band).wait()
        return carry

    lax.fori_loop(0, SIDE, finish, 0)


def edge_kernel(edge, first, grid_in, grid_out, columns, out_sems):
    lane = lanes((8, ROWS))
    pairs = SIDE // 2

    def put(pair):
        rows = pl.ds(pair * 2 * SUB, 2 * SUB)
        return pltpu.make_async_copy(
            columns.at[:, rows, :], grid_out.at[:, rows, pl.ds(0, ROWS)], out_sems.at[pair]
        )

    def add(pair, carry):
        for c in range(2):
            packed = edge[c, pair]
            for k in range(16):
                moved = pltpu.roll(packed, ROWS - 8 * k, 1) if k else packed
                rows = pl.ds(pair * 2 * SUB + 8 * k, 8)
                columns[c, rows, :] = first[c, rows, :] + jnp.where(lane < KW, moved, 0.0)
        put(pair).start()
        return carry

    lax.fori_loop(0, pairs, add, 0, unroll=4)
    for pair in range(pairs):
        put(pair).wait()


def in_hbm(x):
    return pltpu.with_memory_space_constraint(x, pltpu.HBM)


def shifted(block, axis, distance):
    devices = range(lax.axis_size(axis))
    route = [(i - distance, i) for i in devices if i - distance in devices]
    return lax.ppermute(block, axis, route)


def shards(visibilities, vis_weight, cell_index, tap_offsets, routes, patch_index, kernel):
    blocks = visibilities.shape[0]
    tile_count = lax.axis_size("tile")
    plane_count = lax.axis_size("wp")
    peers = tile_count * plane_count
    cap = max(2, 2 * blocks // peers)
    rows = 3 * cap + 1
    vmem = pl.BlockSpec(memory_space=pltpu.VMEM)
    hbm = pl.BlockSpec(memory_space=pltpu.HBM)

    acc_shape = (max(DUMMY + 1, 6 * (blocks // 8)), ROW_BLOCK, ROWS)

    buckets, acc = pl.pallas_call(
        functools.partial(pack_kernel, peers, cap),
        out_shape=[jax.ShapeDtypeStruct((peers * rows, 1, ROWS), f32), pltpu.VMEM(acc_shape, f32)],
        in_specs=[hbm] * 6,
        out_specs=[vmem, vmem],
        scratch_shapes=[
            pltpu.SMEM((blocks,), jnp.int32),
            pltpu.SMEM((blocks,), jnp.int32),
            pltpu.VMEM((blocks, 2, ROWS), f32),
            pltpu.VMEM((blocks, ROWS), f32),
            pltpu.VMEM((blocks, ROWS), jnp.int32),
            pltpu.VMEM((blocks, ROWS), jnp.int32),
            pltpu.SMEM((peers,), jnp.int32),
            pltpu.SMEM((peers, ROWS), jnp.int32),
            pltpu.VMEM((peers, ROWS), jnp.int32),
            pltpu.SMEM((blocks,), jnp.int32),
            pltpu.SemaphoreType.DMA((7,)),
        ],
        compiler_params=pltpu.CompilerParams(vmem_limit_bytes=8 << 20),
        name="pack",
    )(*[in_hbm(x) for x in (routes[:, 0], patch_index, visibilities, vis_weight, cell_index, tap_offsets)])

    arrived = lax.all_to_all(buckets, ("tile", "wp"), split_axis=0, concat_axis=0, tiled=True)

    acc, right = pl.pallas_call(
        functools.partial(add_kernel, peers, cap),
        out_shape=[pltpu.VMEM(acc_shape, f32), jax.ShapeDtypeStruct((2, SIDE // 2, 8, ROWS), f32)],
        in_specs=[hbm, vmem, vmem],
        out_specs=[vmem, vmem],
        scratch_shapes=[
            pltpu.VMEM((peers, ROWS), jnp.int32),
            pltpu.SMEM((peers, ROWS), jnp.int32),
            pltpu.SMEM((peers * cap + max(cap, STEPS[-1]),), jnp.int32),
            pltpu.SMEM((KW, OVER), f32),
            pltpu.SemaphoreType.DMA,
            pltpu.SemaphoreType.DMA,
        ],
        input_output_aliases={2: 0},
        compiler_params=pltpu.CompilerParams(vmem_limit_bytes=4 << 20),
        name="add",
    )(in_hbm(kernel.T), arrived, acc)

    place = lax.axis_index("tile")
    from_left = shifted(right, "tile", 1)

    with_low = tile_count > TCOLS
    out_shape = [jax.ShapeDtypeStruct((2, TILE, TILE), f32), jax.ShapeDtypeStruct((2, TILE, ROWS), f32)]
    out_specs = [hbm, vmem]
    if with_low:
        out_shape.append(jax.ShapeDtypeStruct((2, KW, TILE + ROWS), f32))
        out_specs.append(vmem)
    own, first, *low = pl.pallas_call(
        functools.partial(fold_kernel, with_low),
        out_shape=out_shape,
        in_specs=[vmem],
        out_specs=out_specs,
        scratch_shapes=[pltpu.VMEM((2, TILE, TILE - ROWS), f32), pltpu.SemaphoreType.DMA((SIDE,))],
        compiler_params=pltpu.CompilerParams(vmem_limit_bytes=12 << 20),
        cost_estimate=pl.CostEstimate(flops=1 << 22, bytes_accessed=16 << 20, transcendentals=0),
        name="fold",
    )(acc)

    if with_low:
        from_left = jnp.where(place % TCOLS == 0, 0.0, from_left)
    own = pl.pallas_call(
        edge_kernel,
        out_shape=jax.ShapeDtypeStruct((2, TILE, TILE), f32),
        in_specs=[vmem, vmem, hbm],
        out_specs=hbm,
        scratch_shapes=[
            pltpu.VMEM((2, TILE, ROWS), f32),
            pltpu.SemaphoreType.DMA((SIDE // 2,)),
        ],
        input_output_aliases={2: 0},
        compiler_params=pltpu.CompilerParams(vmem_limit_bytes=4 << 20),
        name="edges",
    )(from_left, first, own)
    if with_low:
        (low,) = low
        from_above = shifted(low, "tile", TCOLS)
        from_corner = shifted(low[:, :, TILE:], "tile", TCOLS + 1)
        from_corner = jnp.where(place % TCOLS == 0, 0.0, from_corner)
        own = own.at[:, :KW, :].add(from_above[:, :, :TILE])
        own = own.at[:, :KW, :ROWS].add(from_corner)
    return own.reshape(1, 1, 2, TILE, TILE)


def solution(mesh):
    in_specs = (
        P(("tile", "wp"), None, None),
        P(("tile", "wp"), None),
        P(("tile", "wp"), None),
        P(("tile", "wp"), None),
        P(("tile", "wp"), None),
        P(("tile", "wp")),
        P(),
    )
    out_specs = P("wp", "tile", None, None, None)
    return jax.shard_map(shards, mesh=mesh, in_specs=in_specs, out_specs=out_specs, check_vma=False)
```

```python
import functools

import jax
import jax.numpy as jnp
from jax import lax
from jax.experimental import pallas as pl
from jax.experimental.pallas import tpu as pltpu
from jax.sharding import PartitionSpec as P

TCOLS = 8
SUB = 64
KW = 8
OVER = 16
TILE = 1024
ROWS = 128
SIDE = TILE // SUB
PATCHES = SIDE * SIDE
ROW_BLOCK = 2 * (SUB + KW)
FIRST = SIDE
DUMMY = FIRST + PATCHES
STEPS = (128, 64, 32, 16)

f32 = jnp.float32
bf16 = jnp.bfloat16


def lanes(shape):
    return lax.broadcasted_iota(jnp.int32, shape, len(shape) - 1)


def pack_kernel(peers, cap, routes, patch, vis, weight, cell, tap, out, acc, *scratch):
    routes_s, patch_s, vis_v, weight_v, cell_v, tap_v, count, meta, meta_v, place, sems = scratch
    blocks = vis.shape[0]
    rows = 3 * cap + 1
    sources = (routes, patch, vis, weight, cell, tap)
    targets = (routes_s, patch_s, vis_v, weight_v, cell_v, tap_v)
    copies = [pltpu.make_async_copy(a, b, sems.at[i]) for i, (a, b) in enumerate(zip(sources, targets))]
    for copy in copies:
        copy.start()

    steps = blocks // 8
    early = acc.shape[0] - 6 * steps

    def clear_accumulators(first, number):
        for i in range(number):
            acc[first + i] = jnp.zeros((ROW_BLOCK, ROWS), f32)

    def clear(d, carry):
        count[d] = 0
        return carry

    def clear_one(i, carry):
        clear_accumulators(i, 1)
        return carry

    lax.fori_loop(0, peers, clear, 0, unroll=8)
    lax.fori_loop(0, early, clear_one, 0)
    copies[0].wait()
    copies[1].wait()

    def choose(step, carry):
        clear_accumulators(early + 4 * step, 4)
        for i in range(8):
            b = step * 8 + i
            d = routes_s[b]
            k = count[d]
            count[d] = k + 1
            meta[d, k] = patch_s[b]
            place[b] = d * rows + 3 * k
        return carry

    def put_count(d, carry):
        meta[d, cap] = count[d]
        return carry

    lax.fori_loop(0, steps, choose, 0)
    lax.fori_loop(0, peers, put_count, 0, unroll=8)
    meta_copy = pltpu.make_async_copy(meta, meta_v, sems.at[6])
    meta_copy.start()
    for copy in copies[2:]:
        copy.wait()

    def move(step, carry):
        clear_accumulators(early + 4 * steps + 2 * step, 2)
        first = pl.multiple_of(step * 8, 8)
        block_rows = pl.ds(first, 8)
        w = weight_v[block_rows, :]
        c = cell_v[block_rows, :]
        t = tap_v[block_rows, :]
        at_u = ((t >> 4) << 3) | ((c >> 6) & 7)
        at_v = ((t & 15) << 3) | (c & 7)
        code = (((c >> 9) << 17) | (((c >> 3) & 7) << 14) | (at_u << 7) | at_v).astype(f32)
        for i in range(8):
            row = place[first + i]
            both = vis_v[first + i] * w[i : i + 1, :]
            out[row] = both[0:1, :]
            out[row + 1] = both[1:2, :]
            out[row + 2] = code[i : i + 1, :]
        return carry

    lax.fori_loop(0, steps, move, 0, unroll=4)
    meta_copy.wait()

    def put_meta(d, carry):
        out[d * rows + 3 * cap] = meta_v[pl.ds(d, 1), :].astype(f32)
        return carry

    lax.fori_loop(0, peers, put_meta, 0, unroll=8)


def split(x):
    hi = x.astype(bf16)
    return hi, (x - hi.astype(f32)).astype(bf16)


def twice(x):
    return jnp.concatenate([x, x], axis=0)


def look_up(table, index):
    numbers = lax.GatherDimensionNumbers(
        offset_dims=(),
        collapsed_slice_dims=(1,),
        start_index_map=(1,),
        operand_batching_dims=(0,),
        start_indices_batching_dims=(0,),
    )
    return lax.gather(
        table, index[..., None], numbers, (1, 1), mode=lax.GatherScatterMode.PROMISE_IN_BOUNDS
    )


def spread(picks, values):
    zero = jnp.zeros((16, ROWS), bf16)
    return [[jnp.where(pick, value, zero) for pick in picks] for value in values]


def patch_product(re, im, code, parity, table, wide):
    sub = lax.broadcasted_iota(jnp.int32, (8, ROWS), 0)
    at_v = code & 127
    at_u = (code >> 7) & 127
    ku = look_up(table, at_u)
    kv = look_up(table, at_v)
    group_u = ((code >> 17) & 7) + jnp.where(sub < (at_u & 7), 1, 0)
    group_v = ((code >> 14) & 7) + jnp.where(sub < (at_v & 7), 1, 0) + 8 * parity
    step_u = twice(group_u.astype(f32)).astype(bf16)
    step_v = jnp.concatenate([group_v & 15, (group_v + 15) & 15], axis=0).astype(f32).astype(bf16)

    u_hi, u_lo = split(jnp.concatenate([re * ku, im * ku], axis=0))
    hi_rows, lo_rows = spread([step_u == float(g) for g in range(SUB // 8 + 1)], [u_hi, u_lo])
    left_hi, left_lo = jnp.concatenate(hi_rows, axis=0), jnp.concatenate(lo_rows, axis=0)
    v_hi, v_lo = split(twice(kv))
    hi_rows, lo_rows = spread([step_v == 2.0 * g for g in range(ROWS // 16)], [v_hi, v_lo])
    right_hi, right_lo = jnp.concatenate(hi_rows, axis=0), jnp.concatenate(lo_rows, axis=0)

    if wide:
        left = jnp.concatenate([left_hi, left_lo], axis=1)
        right = jnp.concatenate([right_hi, right_lo], axis=0)
        right = jnp.concatenate([right, right], axis=1)
    else:
        left = jnp.concatenate([left_hi, left_lo], axis=0)
        left = jnp.concatenate([left, left], axis=1)
        right = jnp.concatenate([right_hi, right_lo], axis=1)
    product = lax.dot_general(left, right, (((1,), (1,)), ((), ())), preferred_element_type=f32)
    if wide:
        return product[:, :ROWS] + product[:, ROWS:]
    return product[:ROW_BLOCK] + product[ROW_BLOCK:]


def tap_table(kernel):
    sub = lax.broadcasted_iota(jnp.int32, (8, ROWS), 0)
    lane = lanes((8, ROWS))
    which_tap = (sub - lane) & 7
    which_level = lane >> 3
    table = jnp.zeros((8, ROWS), f32)
    for a in range(KW):
        row = jnp.zeros((8, ROWS), f32)
        for o in range(OVER):
            row = jnp.where(which_level == o, kernel[a, o], row)
        table = jnp.where(which_tap == a, row, table)
    return table


def add_kernel(peers, cap, kernel, arrived, acc_in, acc, right, *scratch):
    meta_v, meta, slots, kernel_s, meta_sem, kernel_sem = scratch
    rows = 3 * cap + 1
    kernel_copy = pltpu.make_async_copy(kernel, kernel_s, kernel_sem)
    kernel_copy.start()
    lane_row = lanes((1, ROWS))

    def entries(s, carry):
        row = arrived[s * rows + 3 * cap].astype(jnp.int32)
        entry = (s * rows + 3 * lane_row) * 512 + (row + FIRST)
        meta_v[pl.ds(s, 1), :] = jnp.where(lane_row < cap, entry, row)
        return carry

    lax.fori_loop(0, peers, entries, 0, unroll=8)
    meta_copy = pltpu.make_async_copy(meta_v, meta, meta_sem)
    meta_copy.start()
    kernel_copy.wait()
    table = tap_table(kernel_s)
    meta_copy.wait()

    def gather_source(s, total):
        for k in range(cap):
            slots[total + k] = meta[s, k]
        return total + meta[s, cap]

    total = lax.fori_loop(0, peers, gather_source, 0, unroll=2)
    for k in range(STEPS[-1]):
        slots[total + k] = DUMMY

    def add(first, number):
        for i in range(number):
            entry = slots[first + i]
            row = entry >> 9
            where_to = entry & 511
            re = jnp.broadcast_to(arrived[row], (8, ROWS))
            im = jnp.broadcast_to(arrived[row + 1], (8, ROWS))
            code = jnp.broadcast_to(arrived[row + 2], (8, ROWS)).astype(jnp.int32)
            acc[where_to] += patch_product(re, im, code, entry & 1, table, i % 4 < 2 and i % 16 != 13)

    done = 0
    for size in STEPS:
        steps = (total - done + (size - 1 if size == STEPS[-1] else 0)) // size

        def add_step(step, carry, size=size, done=done):
            add(done + step * size, size)
            return carry

        lax.fori_loop(0, steps, add_step, 0)
        done = done + steps * size

    lane = lanes((8, ROWS))

    def pack_edge(pair, carry):
        for c in range(2):
            edge = jnp.zeros((8, ROWS), f32)
            for k in range(16):
                last = rows_of(acc, c, k % 8, pair * 2 + k // 8, SIDE - 1)
                moved = pltpu.roll(last, 8 * k, 1) if k else last
                edge = jnp.where((lane >> 3) == k, moved, edge)
            right[c, pair] = edge
        return carry

    lax.fori_loop(0, SIDE // 2, pack_edge, 0)


def rows_of(acc, c, h, band, col):
    part = acc[FIRST + band * SIDE + col, pl.ds(16 * h + 8 * c, 8), :]
    if h == 0:
        part = part + acc[band * SIDE + col, pl.ds(2 * SUB + 8 * c, 8), :]
    return part


def fold_kernel(with_low, acc, out, first, *rest):
    low, rest = (rest[0], rest[1:]) if with_low else (None, rest)
    stage, out_sems = rest
    lane = lanes((8, ROWS))

    def copy_out(band):
        rows = pl.ds(band * SUB, SUB)
        return pltpu.make_async_copy(
            stage.at[:, rows, :], out.at[:, rows, pl.ds(ROWS, TILE - ROWS)], out_sems.at[band]
        )

    def fold(band, carry):
        for c in range(2):
            for h in range(8):
                before = jnp.zeros((8, ROWS), f32)
                for t in range(TILE // ROWS):
                    even = rows_of(acc, c, h, band, 2 * t)
                    odd = rows_of(acc, c, h, band, 2 * t + 1)
                    rows = pl.ds(band * SUB + 8 * h, 8)
                    columns = even + jnp.where(lane < SUB, before, odd)
                    if t == 0:
                        first[c, rows, :] = columns
                    else:
                        stage[c, rows, pl.ds((t - 1) * ROWS, ROWS)] = columns
                    before = odd
        copy_out(band).start()
        return carry

    lax.fori_loop(0, SIDE, fold, 0, unroll=2)
    if with_low:
        for c in range(2):
            before = jnp.zeros((8, ROWS), f32)
            for t in range(TILE // ROWS):
                rows = pl.ds(2 * SUB + 8 * c, 8)
                even = acc[FIRST + (SIDE - 1) * SIDE + 2 * t, rows, :]
                odd = acc[FIRST + (SIDE - 1) * SIDE + 2 * t + 1, rows, :]
                low[c, :, pl.ds(t * ROWS, ROWS)] = even + jnp.where(lane < SUB, before, odd)
                before = odd
            low[c, :, pl.ds(TILE, ROWS)] = jnp.where(lane < KW, before, 0.0)

    def finish(band, carry):
        copy_out(band).wait()
        return carry

    lax.fori_loop(0, SIDE, finish, 0)


def edge_kernel(edge, first, grid_in, grid_out, columns, out_sems):
    lane = lanes((8, ROWS))
    pairs = SIDE // 2

    def put(pair):
        rows = pl.ds(pair * 2 * SUB, 2 * SUB)
        return pltpu.make_async_copy(
            columns.at[:, rows, :], grid_out.at[:, rows, pl.ds(0, ROWS)], out_sems.at[pair]
        )

    def add(pair, carry):
        for c in range(2):
            packed = edge[c, pair]
            for k in range(16):
                moved = pltpu.roll(packed, ROWS - 8 * k, 1) if k else packed
                rows = pl.ds(pair * 2 * SUB + 8 * k, 8)
                columns[c, rows, :] = first[c, rows, :] + jnp.where(lane < KW, moved, 0.0)
        put(pair).start()
        return carry

    lax.fori_loop(0, pairs, add, 0, unroll=4)
    for pair in range(pairs):
        put(pair).wait()


def in_hbm(x):
    return pltpu.with_memory_space_constraint(x, pltpu.HBM)


def shifted(block, axis, distance):
    devices = range(lax.axis_size(axis))
    route = [(i - distance, i) for i in devices if i - distance in devices]
    return lax.ppermute(block, axis, route)


def shards(visibilities, vis_weight, cell_index, tap_offsets, routes, patch_index, kernel):
    blocks = visibilities.shape[0]
    tile_count = lax.axis_size("tile")
    plane_count = lax.axis_size("wp")
    peers = tile_count * plane_count
    cap = max(2, 2 * blocks // peers)
    rows = 3 * cap + 1
    vmem = pl.BlockSpec(memory_space=pltpu.VMEM)
    hbm = pl.BlockSpec(memory_space=pltpu.HBM)

    acc_shape = (max(DUMMY + 1, 6 * (blocks // 8)), ROW_BLOCK, ROWS)

    buckets, acc = pl.pallas_call(
        functools.partial(pack_kernel, peers, cap),
        out_shape=[jax.ShapeDtypeStruct((peers * rows, 1, ROWS), f32), pltpu.VMEM(acc_shape, f32)],
        in_specs=[hbm] * 6,
        out_specs=[vmem, vmem],
        scratch_shapes=[
            pltpu.SMEM((blocks,), jnp.int32),
            pltpu.SMEM((blocks,), jnp.int32),
            pltpu.VMEM((blocks, 2, ROWS), f32),
            pltpu.VMEM((blocks, ROWS), f32),
            pltpu.VMEM((blocks, ROWS), jnp.int32),
            pltpu.VMEM((blocks, ROWS), jnp.int32),
            pltpu.SMEM((peers,), jnp.int32),
            pltpu.SMEM((peers, ROWS), jnp.int32),
            pltpu.VMEM((peers, ROWS), jnp.int32),
            pltpu.SMEM((blocks,), jnp.int32),
            pltpu.SemaphoreType.DMA((7,)),
        ],
        compiler_params=pltpu.CompilerParams(vmem_limit_bytes=8 << 20),
        name="pack",
    )(*[in_hbm(x) for x in (routes[:, 0], patch_index, visibilities, vis_weight, cell_index, tap_offsets)])

    arrived = lax.all_to_all(buckets, ("tile", "wp"), split_axis=0, concat_axis=0, tiled=True)

    acc, right = pl.pallas_call(
        functools.partial(add_kernel, peers, cap),
        out_shape=[pltpu.VMEM(acc_shape, f32), jax.ShapeDtypeStruct((2, SIDE // 2, 8, ROWS), f32)],
        in_specs=[hbm, vmem, vmem],
        out_specs=[vmem, vmem],
        scratch_shapes=[
            pltpu.VMEM((peers, ROWS), jnp.int32),
            pltpu.SMEM((peers, ROWS), jnp.int32),
            pltpu.SMEM((peers * cap + max(cap, STEPS[-1]),), jnp.int32),
            pltpu.SMEM((KW, OVER), f32),
            pltpu.SemaphoreType.DMA,
            pltpu.SemaphoreType.DMA,
        ],
        input_output_aliases={2: 0},
        compiler_params=pltpu.CompilerParams(vmem_limit_bytes=4 << 20),
        name="add",
    )(in_hbm(kernel.T), arrived, acc)

    place = lax.axis_index("tile")
    from_left = shifted(right, "tile", 1)

    with_low = tile_count > TCOLS
    out_shape = [jax.ShapeDtypeStruct((2, TILE, TILE), f32), jax.ShapeDtypeStruct((2, TILE, ROWS), f32)]
    out_specs = [hbm, vmem]
    if with_low:
        out_shape.append(jax.ShapeDtypeStruct((2, KW, TILE + ROWS), f32))
        out_specs.append(vmem)
    own, first, *low = pl.pallas_call(
        functools.partial(fold_kernel, with_low),
        out_shape=out_shape,
        in_specs=[vmem],
        out_specs=out_specs,
        scratch_shapes=[pltpu.VMEM((2, TILE, TILE - ROWS), f32), pltpu.SemaphoreType.DMA((SIDE,))],
        compiler_params=pltpu.CompilerParams(vmem_limit_bytes=12 << 20),
        cost_estimate=pl.CostEstimate(flops=1 << 22, bytes_accessed=16 << 20, transcendentals=0),
        name="fold",
    )(acc)

    if with_low:
        from_left = jnp.where(place % TCOLS == 0, 0.0, from_left)
    own = pl.pallas_call(
        edge_kernel,
        out_shape=jax.ShapeDtypeStruct((2, TILE, TILE), f32),
        in_specs=[vmem, vmem, hbm],
        out_specs=hbm,
        scratch_shapes=[
            pltpu.VMEM((2, TILE, ROWS), f32),
            pltpu.SemaphoreType.DMA((SIDE // 2,)),
        ],
        input_output_aliases={2: 0},
        compiler_params=pltpu.CompilerParams(vmem_limit_bytes=4 << 20),
        name="edges",
    )(from_left, first, own)
    if with_low:
        (low,) = low
        from_above = shifted(low, "tile", TCOLS)
        from_corner = shifted(low[:, :, TILE:], "tile", TCOLS + 1)
        from_corner = jnp.where(place % TCOLS == 0, 0.0, from_corner)
        own = own.at[:, :KW, :].add(from_above[:, :, :TILE])
        own = own.at[:, :KW, :ROWS].add(from_corner)
    return own.reshape(1, 1, 2, TILE, TILE)


def solution(mesh):
    in_specs = (
        P(("tile", "wp"), None, None),
        P(("tile", "wp"), None),
        P(("tile", "wp"), None),
        P(("tile", "wp"), None),
        P(("tile", "wp"), None),
        P(("tile", "wp")),
        P(),
    )
    out_specs = P("wp", "tile", None, None, None)
    return jax.shard_map(shards, mesh=mesh, in_specs=in_specs, out_specs=out_specs, check_vma=False)
```
